512 devices in a mesh: row: 32 (over z, x), col: 16 (over y, core).
Axes of the slice: x: 4, y: 8, z: 8, core: 2. Of those that a mesh axis runs over, the one named last changes fastest.
Arguments:
- tokens: bfloat16 [512, 12288], P('row', 'col'), may hold values from -6 to 6
- weight_in: bfloat16 [12288, 24576], P('col', 'row'), may hold values from -0.0546875 to 0.0546875
- bias_in: float32 [24576], P('row'), may hold values from -3 to 3
- weight_out: bfloat16 [24576, 12288], P('row', 'col'), may hold values from -0.0390625 to 0.0390625
- out_grad: bfloat16 [512, 12288], P('row', 'col'), may hold values from -3 to 3
Outputs:
- grad_tokens: bfloat16 [512, 12288], P('row', 'col')
- grad_weight_in: bfloat16 [12288, 24576], P('col', 'row')
- grad_weight_out: bfloat16 [24576, 12288], P('row', 'col')
- grad_bias: float32 [24576], P('row')
The draws below stay inside these ranges and needn't reach their ends.
All inputs are finite; a program needn't handle non-finite values.
Results may differ from the reference program's by a relative error of at most 0.0049.
Values may be sent and summed in bfloat16 or wider, within the bound.
A program may use at most 64 MiB of HBM per device.

```python
import jax
import jax.numpy as jnp
from jax import lax

D = 12288
HID = 24576
TOKENS = 512


def shard_levels(key, dims, split, least, top_value):
    def one(dim, blocks):
        heights = jax.random.uniform(jax.random.fold_in(jax.random.fold_in(key, 6), dim), (blocks,), jnp.float32, least / len(split), top_value / len(split))
        return jnp.repeat(jnp.exp(heights), dims[dim] // blocks).reshape((-1,) + (1,) * (len(dims) - dim - 1))

    gain = one(*split[0])
    for cut in split[1:]:
        gain = gain * one(*cut)
    return gain


def noise(key, extent, scale, most, shards=(), held_as=jnp.bfloat16):
    factor_of = shard_levels(key, extent, shards, -0.22, 0.18) if shards else 1.0
    values = jax.random.normal(key, extent, jnp.float32) * scale * factor_of
    return jnp.minimum(jnp.maximum(values, -most), most).astype(held_as)


def setup_inputs(seed: int = 0) -> dict:
    seeds = jax.random.split(jax.random.key(seed), 6)
    return {
        "tokens": noise(seeds[0], (TOKENS, D), 1.0, 6.0, ((0, 32), (1, 16))),
        "weight_in": noise(seeds[1], (D, HID), D ** -0.5, 0.0546875, ((0, 16), (1, 32))),
        "bias_in": noise(seeds[2], (HID,), 0.5, 3.0, ((0, 32),), jnp.float32),
        "weight_out": noise(seeds[3], (HID, D), HID ** -0.5, 0.0390625, ((0, 32), (1, 16))),
        "out_grad": noise(seeds[4], (TOKENS, D), 0.5, 3.0, ((0, 32), (1, 16))),
    }


SQRT_HALF = 0.7071067811865476
INV_ROOT_TWO_PI = 0.3989422804014327


def gelu_value(preact):
    return preact * 0.5 * (1.0 + lax.erf(preact * SQRT_HALF))


def gelu_slope(preact):
    return 0.5 * (1.0 + lax.erf(preact * SQRT_HALF)) + preact * INV_ROOT_TWO_PI * jnp.exp(-0.5 * preact * preact)


def reference(tokens, weight_in, bias_in, weight_out, out_grad):
    preact = jnp.dot(tokens, weight_in, preferred_element_type=jnp.float32) + bias_in[None, :]
    activated = gelu_value(preact).astype(jnp.bfloat16)
    grad_act = lax.dot_general(out_grad, weight_out, (((1,), (1,)), ((), ())), preferred_element_type=jnp.float32)
    grad_preact = (grad_act * gelu_slope(preact)).astype(jnp.bfloat16)
    grad_bias = jnp.sum(grad_preact.astype(jnp.float32), axis=0)
    grad_weight_in = lax.dot_general(tokens, grad_preact, (((0,), (0,)), ((), ())), preferred_element_type=jnp.float32).astype(jnp.bfloat16)
    grad_weight_out = lax.dot_general(activated, out_grad, (((0,), (0,)), ((), ())), preferred_element_type=jnp.float32).astype(jnp.bfloat16)
    grad_tokens = lax.dot_general(grad_preact, weight_in, (((1,), (1,)), ((), ())), preferred_element_type=jnp.float32).astype(jnp.bfloat16)
    return grad_tokens, grad_weight_in, grad_weight_out, grad_bias
```

```python
import functools

import jax
import jax.numpy as jnp
from jax import lax
from jax.experimental import pallas as pl
from jax.experimental.pallas import tpu as pltpu
from jax.sharding import PartitionSpec as P

SQRT_HALF = 0.7071067811865476
INV_ROOT_TWO_PI = 0.3989422804014327
X = 4
N_SEMS = 192
BF16, F32 = jnp.bfloat16, jnp.float32
MESH = pl.DeviceIdType.MESH


def gelu_value(preact):
    return preact * 0.5 * (1.0 + lax.erf(preact * SQRT_HALF))


def gelu_slope(preact):
    return 0.5 * (1.0 + lax.erf(preact * SQRT_HALF)) + preact * INV_ROOT_TWO_PI * jnp.exp(
        -0.5 * preact * preact
    )


def around(n):
    out = [0]
    for d in range(1, n // 2):
        out += [d, -d]
    return out + [n // 2]


def copy_out(a, b, c, d, a_out, b_out, c_out, d_out, sems):
    copies = [
        pltpu.make_async_copy(src, dst, sems.at[i])
        for i, (src, dst) in enumerate(((b, b_out), (c, c_out)))
    ]
    for copy in copies:
        copy.start()
    a_out[...] = a[...]
    d_out[...] = jnp.sum(d[...], axis=0)
    for copy in copies:
        copy.wait()


def kernel(
    nz,
    ny,
    tokens,
    weight_in,
    bias_in,
    weight_out,
    out_grad,
    grad_tokens,
    grad_weight_in,
    grad_weight_out,
    grad_bias,
    tok_all,
    og_all,
    w_in,
    w_out,
    part,
    pair_out,
    pair_in,
    ring_out,
    ring_in,
    act_all,
    gp_all,
    g_full,
    g_send,
    lx_in,
    lz_sum,
    lz_out,
    lz_in,
    rz_out,
    rz_in,
    rx_sum,
    rx_in,
    gwi,
    gwo,
    send_sems,
    recv_sems,
    local_sems,
):
    nx = X
    rows, feat = tokens.shape
    hid = w_in.shape[1]
    cut = lx_in.shape[-1]
    total = nz * nx * rows
    piece = total // (2 * ny)
    hz, hy = nz // 2, ny // 2
    row, col = lax.axis_index("row"), lax.axis_index("col")
    z, x = lax.div(row, nx), lax.rem(row, nx)
    y, c = lax.div(col, 2), lax.rem(col, 2)

    def yn(d):
        return lax.rem(y + (ny + d), ny)

    def to_z(d):
        return (lax.rem(z + (nz + d), nz) * nx + x, col)

    def to_x(d):
        return (z * nx + lax.rem(x + d, nx), col)

    def to_y(d):
        return (row, yn(d) * 2 + c)

    partner = (row, y * 2 + (1 - c))
    pending = []

    def send(src, dst, device):
        i = len(pending)
        copy = pltpu.make_async_remote_copy(
            src_ref=src,
            dst_ref=dst,
            send_sem=send_sems.at[i],
            recv_sem=recv_sems.at[i],
            device_id=device,
            device_id_type=MESH,
        )
        copy.start()
        pending.append(copy)
        return copy

    def local(src, dst, i):
        copy = pltpu.make_async_copy(src, dst, local_sems.at[i])
        copy.start()
        return copy

    left, right = pl.ds(0, cut), pl.ds(cut, feat - cut)
    slot = {d: i for i, d in enumerate(around(nz))}
    slot[-hz] = slot[hz]
    near = 2 * min(hz, 3) - 1

    def direct(h, side):
        out = []
        for d in (2, 1):
            if d < h:
                out += [d, -d]
            elif d == h:
                out.append(d * side)
        return out

    def relayed(h, side):
        return [(sgn, d) for sgn in (1, -1) for d in (3, 4) if d < h or (d == h and sgn == side)]

    own_tok = local(tokens, tok_all.at[0, 0], 0)
    own_og = local(out_grad, og_all.at[0, 0], 1)
    load_in = local(weight_in, w_in, 2)
    load_out = local(weight_out, w_out, 3)

    barrier = pltpu.get_barrier_semaphore()
    friends = [to_x(j) for j in range(1, nx)] + [partner]
    for d in (1, -1, 2, -2):
        friends += [to_z(d)] * (abs(d) <= hz) + [to_y(d)] * (abs(d) <= hy)
    for device in friends:
        pl.semaphore_signal(barrier, inc=1, device_id=device, device_id_type=MESH)
    pl.semaphore_wait(barrier, len(friends))

    sources = ((tokens, tok_all), (out_grad, og_all))
    sides = (1, -1)
    rx, lz, lx, rz = ({} for _ in range(4))

    for a, (src, buf) in enumerate(sources):
        for j in range(1, nx):
            rx[a, j] = send(src.at[:, right], buf.at[0, nx - j, :, right], to_x(j))
        for d in direct(hz, sides[a]):
            lz[a, d] = send(src.at[:, left], buf.at[slot[-d], 0, :, left], to_z(d))
    own_tok.wait()
    own_og.wait()
    for a, (_, buf) in enumerate(sources):
        for j in range(1, nx):
            rx[a, j].wait_recv()
        for d in direct(hz, sides[a]):
            rz[a, d] = send(buf.at[0, :, :, right], buf.at[slot[-d], :, :, right], to_z(d))
    for a, (_, buf) in enumerate(sources):
        for sgn, d in relayed(hz, sides[a]):
            if d == 3:
                lz[a, 2 * sgn].wait_recv()
            lz[a, d * sgn] = send(
                buf.at[slot[-2 * sgn], 0, :, left], buf.at[slot[-d * sgn], 0, :, left], to_z((d - 2) * sgn)
            )
        for d in direct(hz, sides[a]):
            if not (hz > 2 and abs(d) == 2):
                lz[a, d].wait_recv()
        for j in range(1, nx):
            lx[a, 0, j] = send(buf.at[0:near, 0, :, left], buf.at[0:near, nx - j, :, left], to_x(j))
    for a, (_, buf) in enumerate(sources):
        for sgn, d in relayed(hz, sides[a]):
            if d == 3:
                rz[a, 2 * sgn].wait_recv()
            rz[a, d * sgn] = send(
                buf.at[slot[-2 * sgn], :, :, right], buf.at[slot[-d * sgn], :, :, right], to_z((d - 2) * sgn)
            )
    for a, (_, buf) in enumerate(sources):
        for sgn, d in relayed(hz, sides[a]):
            lz[a, d * sgn].wait_recv()
        if near < nz:
            for j in range(1, nx):
                lx[a, 1, j] = send(
                    buf.at[near:nz, 0, :, left], buf.at[near:nz, nx - j, :, left], to_x(j)
                )

    def gathered(a):
        for d in direct(hz, sides[a]):
            if not (hz > 2 and abs(d) == 2):
                rz[a, d].wait_recv()
        for sgn, d in relayed(hz, sides[a]):
            rz[a, d * sgn].wait_recv()
        for key, copy in lx.items():
            if key[0] == a:
                copy.wait_recv()

    def product(a, core):
        buf = sources[a][1]
        rows_of = buf[pl.ds(core * hz, hz)].reshape(total // 2, feat)
        if a == 0:
            out = jnp.dot(rows_of, w_in[...], preferred_element_type=F32)
        else:
            out = lax.dot_general(
                rows_of, w_out[...], (((1,), (1,)), ((), ())), preferred_element_type=F32
            )
        return out.reshape(ny, piece, hid)

    def order(a):
        out = [d * sgn for sgn, d in relayed(hy, sides[a])]
        one = [d for d in direct(hy, sides[a]) if abs(d) == 1]
        two = [d for d in direct(hy, sides[a]) if abs(d) == 2]
        return out + one + two + [0]

    pair, ring = {}, {}

    def to_partner(a):
        pair_out[a] = product(a, 1 - c)
        for o in order(a):
            pair[a, o] = send(pair_out.at[a, yn(o)], pair_in.at[a, yn(o)], partner)

    def keep(a):
        part[a] = product(a, c)

    def chip_sum(a, o):
        pair[a, o].wait_recv()
        return part[a, yn(o)] + pair_in[a, yn(o)]

    def ring_send(a, k, value, d):
        i = len([key for key in ring if key[0] == a])
        ring_out[a, i] = value.astype(BF16)
        ring[a, k] = (send(ring_out.at[a, i], ring_in.at[a, i], to_y(d)), i)

    def ring_got(a, k):
        copy, i = ring[a, k]
        copy.wait_recv()
        return ring_in[a, i].astype(F32)

    def ring_first(a):
        for sgn, d in relayed(hy, sides[a]):
            ring_send(a, d * sgn, chip_sum(a, d * sgn), (d - 2) * sgn)
        for d in direct(hy, sides[a]):
            if abs(d) == 1:
                ring_send(a, d, chip_sum(a, d), d)

    def ring_second(a):
        for d in direct(hy, sides[a]):
            if abs(d) == 2:
                value = chip_sum(a, d)
                for sgn, far in relayed(hy, sides[a]):
                    if sgn * d > 0:
                        value = value + ring_got(a, far * sgn)
                ring_send(a, d, value, d)

    def ring_end(a):
        value = chip_sum(a, 0)
        for d in reversed(direct(hy, sides[a])):
            value = value + ring_got(a, d)
        return value

    load_in.wait()
    gathered(0)
    to_partner(0)
    keep(0)
    gathered(1)
    load_out.wait()
    to_partner(1)
    ring_first(0)
    keep(1)
    ring_first(1)
    ring_second(0)
    ring_second(1)
    preact = ring_end(0) + bias_in[...][None, :]
    act_all[c, y] = gelu_value(preact).astype(BF16)

    spread, shared = {}, {}

    def share(buf, k, o):
        block = buf.at[c, yn(o)]
        shared[k, o] = send(block, block, partner)

    def spread_first(buf, k):
        for d in direct(hy, sides[k]):
            block = buf.at[c, y]
            spread[k, d] = send(block, block, to_y(d))
        share(buf, k, 0)

    def spread_second(buf, k):
        relays = relayed(hy, sides[k])
        for d in direct(hy, sides[k]):
            spread[k, d].wait_recv()
            block = buf.at[c, yn(-d)]
            for sgn, far in relays:
                if d == 2 * sgn:
                    spread[k, far * sgn] = send(block, block, to_y((far - 2) * sgn))
            share(buf, k, -d)

    def spread_end(buf, k):
        for sgn, far in relayed(hy, sides[k]):
            spread[k, far * sgn].wait_recv()
            share(buf, k, -far * sgn)

    def shared_all(k):
        for key, copy in shared.items():
            if key[0] == k:
                copy.wait_recv()

    spread_first(act_all, 0)
    grad_act = ring_end(1)
    gp_all[c, y] = (grad_act * gelu_slope(preact)).astype(BF16)
    spread_first(gp_all, 1)
    spread_second(gp_all, 1)
    spread_end(gp_all, 1)
    spread_second(act_all, 0)
    shared_all(1)

    grads = gp_all[...].reshape(total, hid)

    def row_terms(span):
        out = lax.dot_general(
            grads, w_in[span, :], (((1,), (1,)), ((), ())), preferred_element_type=F32
        ).reshape(nz, nx, rows, span.size)
        g_full[:, :, :, span] = out
        g_send[:, :, :, span] = out.astype(BF16)

    tx, tl, tr, tf = {}, {}, {}, {}

    def right_first():
        for sgn, d in relayed(hz, 1):
            o = d * sgn
            tr[o] = (send(g_send.at[slot[o], :, :, right], rz_in.at[len(tr)], to_z((d - 2) * sgn)), len(tr))
        for o in direct(hz, 1):
            if abs(o) == 1:
                tr[o] = (send(g_send.at[slot[o], :, :, right], rz_in.at[len(tr)], to_z(o)), len(tr))

    def right_got(o):
        copy, i = tr[o]
        copy.wait_recv()
        return rz_in[i].astype(F32)

    def right_second():
        for i, o in enumerate(d for d in direct(hz, 1) if abs(d) == 2):
            value = g_full[slot[o], :, :, right]
            for sgn, d in relayed(hz, 1):
                if sgn * o > 0:
                    value = value + right_got(d * sgn)
            rz_out[i] = value.astype(BF16)
            tr[o] = (send(rz_out.at[i], rz_in.at[len(tr)], to_z(o)), len(tr))

    def right_end():
        value = g_full[0, :, :, right]
        for o in reversed(direct(hz, 1)):
            value = value + right_got(o)
        rx_sum[...] = value
        for j in range(1, nx):
            tf[j] = send(rx_sum.at[j], rx_in.at[j - 1], to_x(j))

    def left_first():
        value = g_full[:, 0, :, left]
        for j in range(1, nx):
            tx[j].wait_recv()
            value = value + lx_in[j - 1].astype(F32)
        lz_sum[...] = value
        for sgn, d in relayed(hz, -1):
            o = d * sgn
            tl[o] = (send(lz_sum.at[slot[o]], lz_in.at[len(tl)], to_z((d - 2) * sgn)), len(tl))
        for o in direct(hz, -1):
            if abs(o) == 1:
                tl[o] = (send(lz_sum.at[slot[o]], lz_in.at[len(tl)], to_z(o)), len(tl))

    def left_got(o):
        copy, i = tl[o]
        copy.wait_recv()
        return lz_in[i]

    def left_second():
        for i, o in enumerate(d for d in direct(hz, -1) if abs(d) == 2):
            value = lz_sum[slot[o]]
            for sgn, d in relayed(hz, -1):
                if sgn * o > 0:
                    value = value + left_got(d * sgn)
            lz_out[i] = value
            tl[o] = (send(lz_out.at[i], lz_in.at[len(tl)], to_z(o)), len(tl))

    def left_end():
        value = lz_sum[0]
        for o in reversed(direct(hz, -1)):
            value = value + left_got(o)
        grad_tokens[:, left] = value.astype(BF16)

    def weight_in_grad(i, n):
        step = feat // n
        tok = tok_all[:, :, :, i * step : (i + 1) * step].reshape(total, step)
        gwi[i * step : (i + 1) * step, :] = lax.dot_general(
            tok, grads, (((0,), (0,)), ((), ())), preferred_element_type=F32
        ).astype(BF16)

    def weight_out_grad(i, n):
        step = hid // n
        act = act_all[:, :, :, i * step : (i + 1) * step].reshape(total, step)
        gwo[i * step : (i + 1) * step, :] = lax.dot_general(
            act, og_all[...].reshape(total, feat), (((0,), (0,)), ((), ())), preferred_element_type=F32
        ).astype(BF16)

    row_terms(right)
    right_first()
    row_terms(left)
    for j in range(1, nx):
        tx[j] = send(g_send.at[:, j, :, left], lx_in.at[j - 1], to_x(j))
    spread_end(act_all, 0)
    weight_in_grad(0, 3)
    right_second()
    left_first()
    weight_in_grad(1, 3)
    grad_bias[...] = jnp.sum(grads.astype(F32), axis=0, keepdims=True)
    left_second()
    right_end()
    weight_in_grad(2, 3)
    store_in = local(gwi, grad_weight_in, 2)
    shared_all(0)
    for i in range(3):
        weight_out_grad(i, 3)
    store_out = local(gwo, grad_weight_out, 3)
    left_end()
    value = rx_sum[0]
    for j in range(1, nx):
        tf[j].wait_recv()
        value = value + rx_in[j - 1]
    grad_tokens[:, right] = value.astype(BF16)
    store_in.wait()
    store_out.wait()
    for copy in pending:
        copy.wait_send()


def body(nz, ny, tokens, weight_in, bias_in, weight_out, out_grad):
    rows, feat = tokens.shape
    hid = weight_in.shape[1]
    cut = feat // 3 * 2
    rest = feat - cut
    nx = X
    total = nz * nx * rows
    piece = total // (2 * ny)
    vmem, anywhere = pl.BlockSpec(memory_space=pltpu.VMEM), pl.BlockSpec(memory_space=pl.ANY)
    out = pl.pallas_call(
        functools.partial(kernel, nz, ny),
        out_shape=(
            jax.ShapeDtypeStruct((rows, feat), BF16),
            jax.ShapeDtypeStruct((feat, hid), BF16),
            jax.ShapeDtypeStruct((hid, feat), BF16),
            jax.ShapeDtypeStruct((1, hid), F32),
        ),
        in_specs=[anywhere, anywhere, vmem, anywhere, anywhere],
        out_specs=(vmem, anywhere, anywhere, vmem),
        scratch_shapes=[
            pltpu.VMEM((nz, nx, rows, feat), BF16),
            pltpu.VMEM((nz, nx, rows, feat), BF16),
            pltpu.VMEM((feat, hid), BF16),
            pltpu.VMEM((hid, feat), BF16),
            pltpu.VMEM((2, ny, piece, hid), F32),
            pltpu.VMEM((2, ny, piece, hid), F32),
            pltpu.VMEM((2, ny, piece, hid), F32),
            pltpu.VMEM((2, ny - 1, piece, hid), BF16),
            pltpu.VMEM((2, ny - 1, piece, hid), BF16),
            pltpu.VMEM((2, ny, piece, hid), BF16),
            pltpu.VMEM((2, ny, piece, hid), BF16),
            pltpu.VMEM((nz, nx, rows, feat), F32),
            pltpu.VMEM((nz, nx, rows, feat), BF16),
            pltpu.VMEM((nx - 1, nz, rows, cut), BF16),
            pltpu.VMEM((nz, rows, cut), F32),
            pltpu.VMEM((2, rows, cut), F32),
            pltpu.VMEM((nz - 1, rows, cut), F32),
            pltpu.VMEM((2, nx, rows, rest), BF16),
            pltpu.VMEM((nz - 1, nx, rows, rest), BF16),
            pltpu.VMEM((nx, rows, rest), F32),
            pltpu.VMEM((nx - 1, rows, rest), F32),
            pltpu.VMEM((feat, hid), BF16),
            pltpu.VMEM((hid, feat), BF16),
            pltpu.SemaphoreType.DMA((N_SEMS,)),
            pltpu.SemaphoreType.DMA((N_SEMS,)),
            pltpu.SemaphoreType.DMA((4,)),
        ],
        compiler_params=pltpu.CompilerParams(
            collective_id=0, has_side_effects=True, vmem_limit_bytes=56 * 1024 * 1024
        ),
    )(tokens, weight_in, bias_in, weight_out, out_grad)
    return pl.pallas_call(
        copy_out,
        out_shape=(
            jax.ShapeDtypeStruct((rows, feat), BF16),
            jax.ShapeDtypeStruct((feat, hid), BF16),
            jax.ShapeDtypeStruct((hid, feat), BF16),
            jax.ShapeDtypeStruct((hid,), F32),
        ),
        in_specs=[vmem, anywhere, anywhere, vmem],
        out_specs=(vmem, anywhere, anywhere, vmem),
        scratch_shapes=[pltpu.SemaphoreType.DMA((2,))],
        compiler_params=pltpu.CompilerParams(vmem_limit_bytes=56 * 1024 * 1024),
    )(*out)


def solution(mesh):
    nz, ny = mesh.shape["row"] // X, mesh.shape["col"] // 2
    in_specs = (P("row", "col"), P("col", "row"), P("row"), P("row", "col"), P("row", "col"))
    out_specs = (P("row", "col"), P("col", "row"), P("row", "col"), P("row"))
    return jax.shard_map(
        functools.partial(body, nz, ny),
        mesh=mesh,
        in_specs=in_specs,
        out_specs=out_specs,
        check_vma=False,
    )
```

```python
import functools

import jax
import jax.numpy as jnp
from jax import lax
from jax.experimental import pallas as pl
from jax.experimental.pallas import tpu as pltpu
from jax.sharding import PartitionSpec as P

SQRT_HALF = 0.7071067811865476
INV_ROOT_TWO_PI = 0.3989422804014327
X = 4
N_SEMS = 192
BF16, F32 = jnp.bfloat16, jnp.float32
MESH = pl.DeviceIdType.MESH


def gelu_value(preact):
    return preact * 0.5 * (1.0 + lax.erf(preact * SQRT_HALF))


def gelu_slope(preact):
    return 0.5 * (1.0 + lax.erf(preact * SQRT_HALF)) + preact * INV_ROOT_TWO_PI * jnp.exp(
        -0.5 * preact * preact
    )


def around(n):
    out = [0]
    for d in range(1, n // 2):
        out += [d, -d]
    return out + [n // 2]


def copy_out(a, b, c, d, a_out, b_out, c_out, d_out, b_vmem, c_vmem, sems):
    n = 3
    step = b.shape[0] // n
    jobs = [(b, b_vmem, b_out), (c, c_vmem, c_out)]
    spans = [pl.ds(i * step, step) for i in range(n)]
    loads = [
        pltpu.make_async_copy(src.at[span], held.at[span], sems.at[0, i, k])
        for i, span in enumerate(spans)
        for k, (src, held, _) in enumerate(jobs)
    ]
    stores = [
        pltpu.make_async_copy(held.at[span], dst.at[span], sems.at[1, i, k])
        for i, span in enumerate(spans)
        for k, (_, held, dst) in enumerate(jobs)
    ]
    for load in loads:
        load.start()
    a_out[...] = a[...]
    d_out[...] = jnp.sum(d[...], axis=0)
    for load, store in zip(loads, stores):
        load.wait()
        store.start()
    for store in stores:
        store.wait()


def kernel(
    nz,
    ny,
    tokens,
    weight_in,
    bias_in,
    weight_out,
    out_grad,
    grad_tokens,
    grad_weight_in,
    grad_weight_out,
    grad_bias,
    tok_all,
    og_all,
    w_in,
    w_out,
    part,
    pair_out,
    pair_in,
    ring_out,
    ring_in,
    act_all,
    gp_all,
    g_full,
    g_send,
    lx_in,
    lz_sum,
    lz_out,
    lz_in,
    rz_out,
    rz_in,
    rx_sum,
    rx_in,
    gwi,
    gwo,
    send_sems,
    recv_sems,
    local_sems,
):
    nx = X
    rows, feat = tokens.shape
    hid = w_in.shape[1]
    cut = lx_in.shape[-1]
    total = nz * nx * rows
    piece = total // (2 * ny)
    hz, hy = nz // 2, ny // 2
    row, col = lax.axis_index("row"), lax.axis_index("col")
    z, x = lax.div(row, nx), lax.rem(row, nx)
    y, c = lax.div(col, 2), lax.rem(col, 2)

    def yn(d):
        return lax.rem(y + (ny + d), ny)

    def to_z(d):
        return (lax.rem(z + (nz + d), nz) * nx + x, col)

    def to_x(d):
        return (z * nx + lax.rem(x + d, nx), col)

    def to_y(d):
        return (row, yn(d) * 2 + c)

    partner = (row, y * 2 + (1 - c))
    pending = []

    def send(src, dst, device):
        i = len(pending)
        copy = pltpu.make_async_remote_copy(
            src_ref=src,
            dst_ref=dst,
            send_sem=send_sems.at[i],
            recv_sem=recv_sems.at[i],
            device_id=device,
            device_id_type=MESH,
        )
        copy.start()
        pending.append(copy)
        return copy

    def local(src, dst, i):
        copy = pltpu.make_async_copy(src, dst, local_sems.at[i])
        copy.start()
        return copy

    left, right = pl.ds(0, cut), pl.ds(cut, feat - cut)
    slot = {d: i for i, d in enumerate(around(nz))}
    slot[-hz] = slot[hz]
    near = 2 * min(hz, 3) - 1

    def direct(h, side):
        out = []
        for d in (2, 1):
            if d < h:
                out += [d, -d]
            elif d == h:
                out.append(d * side)
        return out

    def relayed(h, side):
        return [(sgn, d) for sgn in (1, -1) for d in (3, 4) if d < h or (d == h and sgn == side)]

    own_tok = local(tokens, tok_all.at[0, 0], 0)
    own_og = local(out_grad, og_all.at[0, 0], 1)
    load_in = local(weight_in, w_in, 2)
    load_out = local(weight_out, w_out, 3)

    barrier = pltpu.get_barrier_semaphore()
    friends = [to_x(j) for j in range(1, nx)] + [partner]
    for d in (1, -1, 2, -2):
        friends += [to_z(d)] * (abs(d) <= hz) + [to_y(d)] * (abs(d) <= hy)
    for device in friends:
        pl.semaphore_signal(barrier, inc=1, device_id=device, device_id_type=MESH)
    pl.semaphore_wait(barrier, len(friends))

    sources = ((tokens, tok_all), (out_grad, og_all))
    sides = (1, -1)
    rx, lz, lx, rz = ({} for _ in range(4))

    own_tok.wait()
    own_og.wait()
    for a, (_, buf) in enumerate(sources):
        for j in range(1, nx):
            rx[a, j] = send(buf.at[0, 0, :, right], buf.at[0, nx - j, :, right], to_x(j))
        for d in direct(hz, sides[a]):
            lz[a, d] = send(buf.at[0, 0, :, left], buf.at[slot[-d], 0, :, left], to_z(d))
    for a, (_, buf) in enumerate(sources):
        for j in range(1, nx):
            rx[a, j].wait_recv()
        for d in direct(hz, sides[a]):
            rz[a, d] = send(buf.at[0, :, :, right], buf.at[slot[-d], :, :, right], to_z(d))
    for a, (_, buf) in enumerate(sources):
        for sgn, d in relayed(hz, sides[a]):
            if d == 3:
                lz[a, 2 * sgn].wait_recv()
            lz[a, d * sgn] = send(
                buf.at[slot[-2 * sgn], 0, :, left], buf.at[slot[-d * sgn], 0, :, left], to_z((d - 2) * sgn)
            )
        for d in direct(hz, sides[a]):
            if not (hz > 2 and abs(d) == 2):
                lz[a, d].wait_recv()
        for j in range(1, nx):
            lx[a, 0, j] = send(buf.at[0:near, 0, :, left], buf.at[0:near, nx - j, :, left], to_x(j))
    for a, (_, buf) in enumerate(sources):
        for sgn, d in relayed(hz, sides[a]):
            if d == 3:
                rz[a, 2 * sgn].wait_recv()
            rz[a, d * sgn] = send(
                buf.at[slot[-2 * sgn], :, :, right], buf.at[slot[-d * sgn], :, :, right], to_z((d - 2) * sgn)
            )
    for a, (_, buf) in enumerate(sources):
        for sgn, d in relayed(hz, sides[a]):
            lz[a, d * sgn].wait_recv()
        if near < nz:
            for j in range(1, nx):
                lx[a, 1, j] = send(
                    buf.at[near:nz, 0, :, left], buf.at[near:nz, nx - j, :, left], to_x(j)
                )

    def gathered(a):
        for d in direct(hz, sides[a]):
            if not (hz > 2 and abs(d) == 2):
                rz[a, d].wait_recv()
        for sgn, d in relayed(hz, sides[a]):
            rz[a, d * sgn].wait_recv()
        for key, copy in lx.items():
            if key[0] == a:
                copy.wait_recv()

    def product(a, core):
        buf = sources[a][1]
        rows_of = buf[pl.ds(core * hz, hz)].reshape(total // 2, feat)
        if a == 0:
            out = jnp.dot(rows_of, w_in[...], preferred_element_type=F32)
        else:
            out = lax.dot_general(
                rows_of, w_out[...], (((1,), (1,)), ((), ())), preferred_element_type=F32
            )
        return out.reshape(ny, piece, hid)

    pair, ring, waited, group = {}, {}, {}, {}

    def to_partner(a):
        out = product(a, 1 - c)
        for i in range(ny):
            pair_out[a, lax.rem(i + ny - y, ny)] = out[i]
        lo, hi = (hy - 1, hy + 2) if ny > 4 else (0, ny)
        for first, last in ((lo, hi), (0, lo), (hi, ny)):
            if first < last:
                span = pl.ds(first, last - first)
                copy = send(pair_out.at[a, span], pair_in.at[a, span], partner)
                for i in range(first, last):
                    pair[a, i] = copy
                    waited[a, first] = False
                    group[a, i] = first

    def keep(a):
        part[a] = product(a, c)

    def chip_sum(a, o):
        i = o % ny
        if not waited[a, group[a, i]]:
            pair[a, i].wait_recv()
            waited[a, group[a, i]] = True
        return part[a, yn(o)] + pair_in[a, i]

    def ring_send(a, k, value, d):
        i = len([key for key in ring if key[0] == a])
        ring_out[a, i] = value.astype(BF16)
        ring[a, k] = (send(ring_out.at[a, i], ring_in.at[a, i], to_y(d)), i)

    def ring_got(a, k):
        copy, i = ring[a, k]
        copy.wait_recv()
        return ring_in[a, i].astype(F32)

    def ring_first(a):
        for sgn, d in relayed(hy, sides[a]):
            ring_send(a, d * sgn, chip_sum(a, d * sgn), (d - 2) * sgn)
        for d in direct(hy, sides[a]):
            if abs(d) == 1:
                ring_send(a, d, chip_sum(a, d), d)

    def ring_second(a):
        for d in direct(hy, sides[a]):
            if abs(d) == 2:
                value = chip_sum(a, d)
                for sgn, far in relayed(hy, sides[a]):
                    if sgn * d > 0:
                        value = value + ring_got(a, far * sgn)
                ring_send(a, d, value, d)

    def ring_end(a):
        value = chip_sum(a, 0)
        for d in reversed(direct(hy, sides[a])):
            value = value + ring_got(a, d)
        return value

    load_in.wait()
    gathered(0)
    to_partner(0)
    keep(0)
    gathered(1)
    load_out.wait()
    to_partner(1)
    ring_first(0)
    keep(1)
    ring_first(1)
    ring_second(0)
    ring_second(1)
    preact = ring_end(0) + bias_in[...][None, :]
    act_all[c, y] = gelu_value(preact).astype(BF16)

    spread, shared = {}, {}

    def share(buf, k, o):
        if k == 0:
            return
        block = buf.at[c, yn(o)]
        shared[k, o] = send(block, block, partner)

    def spread_first(buf, k):
        for d in direct(hy, sides[k]):
            block = buf.at[c, y]
            spread[k, d] = send(block, block, to_y(d))
        share(buf, k, 0)

    def spread_second(buf, k):
        relays = relayed(hy, sides[k])
        for d in direct(hy, sides[k]):
            spread[k, d].wait_recv()
            block = buf.at[c, yn(-d)]
            for sgn, far in relays:
                if d == 2 * sgn:
                    spread[k, far * sgn] = send(block, block, to_y((far - 2) * sgn))
            share(buf, k, -d)

    def spread_end(buf, k):
        for sgn, far in relayed(hy, sides[k]):
            spread[k, far * sgn].wait_recv()
            share(buf, k, -far * sgn)
        if k == 0:
            shared[0, 0] = send(buf.at[c], buf.at[c], partner)

    def shared_all(k):
        for key, copy in shared.items():
            if key[0] == k:
                copy.wait_recv()

    spread_first(act_all, 0)
    grad_act = ring_end(1)
    gp_all[c, y] = (grad_act * gelu_slope(preact)).astype(BF16)
    spread_first(gp_all, 1)
    spread_second(gp_all, 1)
    spread_end(gp_all, 1)
    spread_second(act_all, 0)
    shared_all(1)

    grads = gp_all[...].reshape(total, hid)

    def row_terms(span):
        out = lax.dot_general(
            grads, w_in[span, :], (((1,), (1,)), ((), ())), preferred_element_type=F32
        ).reshape(nz, nx, rows, span.size)
        g_full[:, :, :, span] = out
        g_send[:, :, :, span] = out.astype(BF16)

    tx, tl, tr, tf = {}, {}, {}, {}

    def right_first():
        for sgn, d in relayed(hz, 1):
            o = d * sgn
            tr[o] = (send(g_send.at[slot[o], :, :, right], rz_in.at[len(tr)], to_z((d - 2) * sgn)), len(tr))
        for o in direct(hz, 1):
            if abs(o) == 1:
                tr[o] = (send(g_send.at[slot[o], :, :, right], rz_in.at[len(tr)], to_z(o)), len(tr))

    def right_got(o):
        copy, i = tr[o]
        copy.wait_recv()
        return rz_in[i].astype(F32)

    def right_second():
        for i, o in enumerate(d for d in direct(hz, 1) if abs(d) == 2):
            value = g_full[slot[o], :, :, right]
            for sgn, d in relayed(hz, 1):
                if sgn * o > 0:
                    value = value + right_got(d * sgn)
            rz_out[i] = value.astype(BF16)
            tr[o] = (send(rz_out.at[i], rz_in.at[len(tr)], to_z(o)), len(tr))

    def right_end():
        value = g_full[0, :, :, right]
        for o in reversed(direct(hz, 1)):
            value = value + right_got(o)
        rx_sum[...] = value
        for j in range(1, nx):
            tf[j] = send(rx_sum.at[j], rx_in.at[j - 1], to_x(j))

    def left_first():
        value = g_full[:, 0, :, left]
        for j in range(1, nx):
            tx[j].wait_recv()
            value = value + lx_in[j - 1].astype(F32)
        lz_sum[...] = value
        for sgn, d in relayed(hz, -1):
            o = d * sgn
            tl[o] = (send(lz_sum.at[slot[o]], lz_in.at[len(tl)], to_z((d - 2) * sgn)), len(tl))
        for o in direct(hz, -1):
            if abs(o) == 1:
                tl[o] = (send(lz_sum.at[slot[o]], lz_in.at[len(tl)], to_z(o)), len(tl))

    def left_got(o):
        copy, i = tl[o]
        copy.wait_recv()
        return lz_in[i]

    def left_second():
        for i, o in enumerate(d for d in direct(hz, -1) if abs(d) == 2):
            value = lz_sum[slot[o]]
            for sgn, d in relayed(hz, -1):
                if sgn * o > 0:
                    value = value + left_got(d * sgn)
            lz_out[i] = value
            tl[o] = (send(lz_out.at[i], lz_in.at[len(tl)], to_z(o)), len(tl))

    def left_end():
        value = lz_sum[0]
        for o in reversed(direct(hz, -1)):
            value = value + left_got(o)
        grad_tokens[:, left] = value.astype(BF16)

    def weight_in_grad(i, n):
        step = feat // n
        tok = tok_all[:, :, :, i * step : (i + 1) * step].reshape(total, step)
        gwi[i * step : (i + 1) * step, :] = lax.dot_general(
            tok, grads, (((0,), (0,)), ((), ())), preferred_element_type=F32
        ).astype(BF16)

    def weight_out_grad(i, n):
        step = hid // n
        act = act_all[:, :, :, i * step : (i + 1) * step].reshape(total, step)
        gwo[i * step : (i + 1) * step, :] = lax.dot_general(
            act, og_all[...].reshape(total, feat), (((0,), (0,)), ((), ())), preferred_element_type=F32
        ).astype(BF16)

    row_terms(right)
    right_first()
    row_terms(left)
    for j in range(1, nx):
        tx[j] = send(g_send.at[:, j, :, left], lx_in.at[j - 1], to_x(j))
    spread_end(act_all, 0)
    weight_in_grad(0, 3)
    right_second()
    left_first()
    weight_in_grad(1, 3)
    grad_bias[...] = jnp.sum(grads.astype(F32), axis=0, keepdims=True)
    left_second()
    right_end()
    weight_in_grad(2, 3)
    store_in = local(gwi, grad_weight_in, 2)
    shared_all(0)
    for i in range(3):
        weight_out_grad(i, 3)
    store_out = local(gwo, grad_weight_out, 3)
    left_end()
    value = rx_sum[0]
    for j in range(1, nx):
        tf[j].wait_recv()
        value = value + rx_in[j - 1]
    grad_tokens[:, right] = value.astype(BF16)
    store_in.wait()
    store_out.wait()
    for copy in pending:
        copy.wait_send()


def body(nz, ny, tokens, weight_in, bias_in, weight_out, out_grad):
    rows, feat = tokens.shape
    hid = weight_in.shape[1]
    cut = feat // 3 * 2
    rest = feat - cut
    nx = X
    total = nz * nx * rows
    piece = total // (2 * ny)
    vmem, anywhere = pl.BlockSpec(memory_space=pltpu.VMEM), pl.BlockSpec(memory_space=pl.ANY)
    out = pl.pallas_call(
        functools.partial(kernel, nz, ny),
        out_shape=(
            jax.ShapeDtypeStruct((rows, feat), BF16),
            jax.ShapeDtypeStruct((feat, hid), BF16),
            jax.ShapeDtypeStruct((hid, feat), BF16),
            jax.ShapeDtypeStruct((1, hid), F32),
        ),
        in_specs=[anywhere, anywhere, vmem, anywhere, anywhere],
        out_specs=(vmem, anywhere, anywhere, vmem),
        scratch_shapes=[
            pltpu.VMEM((nz, nx, rows, feat), BF16),
            pltpu.VMEM((nz, nx, rows, feat), BF16),
            pltpu.VMEM((feat, hid), BF16),
            pltpu.VMEM((hid, feat), BF16),
            pltpu.VMEM((2, ny, piece, hid), F32),
            pltpu.VMEM((2, ny, piece, hid), F32),
            pltpu.VMEM((2, ny, piece, hid), F32),
            pltpu.VMEM((2, ny - 1, piece, hid), BF16),
            pltpu.VMEM((2, ny - 1, piece, hid), BF16),
            pltpu.VMEM((2, ny, piece, hid), BF16),
            pltpu.VMEM((2, ny, piece, hid), BF16),
            pltpu.VMEM((nz, nx, rows, feat), F32),
            pltpu.VMEM((nz, nx, rows, feat), BF16),
            pltpu.VMEM((nx - 1, nz, rows, cut), BF16),
            pltpu.VMEM((nz, rows, cut), F32),
            pltpu.VMEM((2, rows, cut), F32),
            pltpu.VMEM((nz - 1, rows, cut), F32),
            pltpu.VMEM((2, nx, rows, rest), BF16),
            pltpu.VMEM((nz - 1, nx, rows, rest), BF16),
            pltpu.VMEM((nx, rows, rest), F32),
            pltpu.VMEM((nx - 1, rows, rest), F32),
            pltpu.VMEM((feat, hid), BF16),
            pltpu.VMEM((hid, feat), BF16),
            pltpu.SemaphoreType.DMA((N_SEMS,)),
            pltpu.SemaphoreType.DMA((N_SEMS,)),
            pltpu.SemaphoreType.DMA((4,)),
        ],
        compiler_params=pltpu.CompilerParams(
            collective_id=0, has_side_effects=True, vmem_limit_bytes=56 * 1024 * 1024
        ),
    )(tokens, weight_in, bias_in, weight_out, out_grad)
    return pl.pallas_call(
        copy_out,
        out_shape=(
            jax.ShapeDtypeStruct((rows, feat), BF16),
            jax.ShapeDtypeStruct((feat, hid), BF16),
            jax.ShapeDtypeStruct((hid, feat), BF16),
            jax.ShapeDtypeStruct((hid,), F32),
        ),
        in_specs=[vmem, anywhere, anywhere, vmem],
        out_specs=(vmem, anywhere, anywhere, vmem),
        scratch_shapes=[
            pltpu.VMEM((feat, hid), BF16),
            pltpu.VMEM((hid, feat), BF16),
            pltpu.SemaphoreType.DMA((2, 3, 2)),
        ],
        compiler_params=pltpu.CompilerParams(vmem_limit_bytes=56 * 1024 * 1024),
    )(*out)


def solution(mesh):
    nz, ny = mesh.shape["row"] // X, mesh.shape["col"] // 2
    in_specs = (P("row", "col"), P("col", "row"), P("row"), P("row", "col"), P("row", "col"))
    out_specs = (P("row", "col"), P("col", "row"), P("row", "col"), P("row"))
    return jax.shard_map(
        functools.partial(body, nz, ny),
        mesh=mesh,
        in_specs=in_specs,
        out_specs=out_specs,
        check_vma=False,
    )
```

```python
import functools

import jax
import jax.numpy as jnp
from jax import lax
from jax.experimental import pallas as pl
from jax.experimental.pallas import tpu as pltpu
from jax.sharding import PartitionSpec as P

SQRT_HALF = 0.7071067811865476
INV_ROOT_TWO_PI = 0.3989422804014327
X = 4
N_SEMS = 192
CHUNKS = 2
BF16, F32 = jnp.bfloat16, jnp.float32
MESH = pl.DeviceIdType.MESH


def gelu_value(preact):
    return preact * 0.5 * (1.0 + lax.erf(preact * SQRT_HALF))


def gelu_slope(preact):
    return 0.5 * (1.0 + lax.erf(preact * SQRT_HALF)) + preact * INV_ROOT_TWO_PI * jnp.exp(
        -0.5 * preact * preact
    )


def around(n):
    out = [0]
    for d in range(1, n // 2):
        out += [d, -d]
    return out + [n // 2]


def copy_out(a, b, c, d, a_out, b_out, c_out, d_out, b_vmem, c_vmem, sems):
    n = 3
    step = b.shape[0] // n
    jobs = [(b, b_vmem, b_out), (c, c_vmem, c_out)]
    spans = [pl.ds(i * step, step) for i in range(n)]
    loads = [
        pltpu.make_async_copy(src.at[span], held.at[span], sems.at[0, i, k])
        for i, span in enumerate(spans)
        for k, (src, held, _) in enumerate(jobs)
    ]
    stores = [
        pltpu.make_async_copy(held.at[span], dst.at[span], sems.at[1, i, k])
        for i, span in enumerate(spans)
        for k, (_, held, dst) in enumerate(jobs)
    ]
    for load in loads:
        load.start()
    a_out[...] = a[...]
    d_out[...] = jnp.sum(d[...], axis=0)
    for load, store in zip(loads, stores):
        load.wait()
        store.start()
    for store in stores:
        store.wait()


def kernel(
    nz,
    ny,
    chunks,
    tokens,
    weight_in,
    bias_in,
    weight_out,
    out_grad,
    grad_tokens,
    grad_weight_in,
    grad_weight_out,
    grad_bias,
    tok_half,
    og_half,
    tok_other,
    og_other,
    stage,
    own_right,
    w_in,
    w_out,
    part,
    ring_out,
    ring_in,
    act_all,
    gp_all,
    g_full,
    g_send,
    lx_in,
    lz_sum,
    lz_out,
    lz_in,
    rz_out,
    rz_in,
    rx_sum,
    rx_in,
    gwi,
    gwo,
    send_sems,
    recv_sems,
    slot_sems,
    local_sems,
):
    nx = X
    nxs = nx // 2
    rows, feat = tokens.shape
    hid = w_in.shape[-1]
    cut = stage.shape[-1]
    rest = feat - cut
    pr = nz * rows // ny
    hz, hy = nz // 2, ny // 2
    per = nxs // chunks
    spans = [pl.ds(k * per, per) for k in range(chunks)]
    row, col = lax.axis_index("row"), lax.axis_index("col")
    z, x = lax.div(row, nx), lax.rem(row, nx)
    y, c = lax.div(col, 2), lax.rem(col, 2)
    first_core, second_core = c == 0, c == 1

    def yn(d):
        return lax.rem(y + (ny + d), ny)

    def to_z(d):
        return (lax.rem(z + (nz + d), nz) * nx + x, col)

    def to_x(j, core):
        return (z * nx + lax.rem(x + j, nx), y * 2 + core)

    def to_y(d):
        return (row, yn(d) * 2 + c)

    partner = (row, y * 2 + (1 - c))
    pending = []
    slot_ids = {}

    def slot_id(key, count):
        if key not in slot_ids:
            slot_ids[key] = sum(n for _, n in slot_ids.values()), count
        return slot_ids[key][0]

    def send(src, dst, device, recv_sem=None, only=None):
        i = len(pending)
        copy = pltpu.make_async_remote_copy(
            src_ref=src,
            dst_ref=dst,
            send_sem=send_sems.at[i],
            recv_sem=recv_sems.at[i] if recv_sem is None else recv_sem,
            device_id=device,
            device_id_type=MESH,
        )
        if only is None:
            copy.start()
        else:
            pl.when(only)(copy.start)
        pending.append((copy, only))
        return copy

    def landed(dst, sem, only=None):
        copy = pltpu.make_async_remote_copy(
            src_ref=dst,
            dst_ref=dst,
            send_sem=send_sems.at[0],
            recv_sem=sem,
            device_id=partner,
            device_id_type=MESH,
        )
        if only is None:
            copy.wait_recv()
        else:
            pl.when(only)(copy.wait_recv)

    def local(src, dst, i):
        copy = pltpu.make_async_copy(src, dst, local_sems.at[i])
        copy.start()
        return copy

    left, right = pl.ds(0, cut), pl.ds(cut, rest)
    slot = {d: i for i, d in enumerate(around(nz))}
    slot[-hz] = slot[hz]
    near = 2 * min(hz, 3) - 1
    batches = [pl.ds(0, near)] + [pl.ds(near, nz - near)] * (near < nz)

    def direct(h, side):
        out = []
        for d in (2, 1):
            if d < h:
                out += [d, -d]
            elif d == h:
                out.append(d * side)
        return out

    def relayed(h, side):
        return [(sgn, d) for sgn in (1, -1) for d in (3, 4) if d < h or (d == h and sgn == side)]

    sources = ((tokens, tok_half), (out_grad, og_half))
    sides = (1, -1)
    own = []
    for a, (src, _) in enumerate(sources):
        own.append(local(src.at[:, left], stage.at[a, 0], 2 * a))
        own.append(local(src.at[:, right], own_right.at[a], 2 * a + 1))
    load_in = local(weight_in, w_in.at[c], 4)
    load_out = local(weight_out, w_out.at[c], 5)

    barrier = pltpu.get_barrier_semaphore()
    friends = [to_x(j, core) for j in range(1, nx) for core in (0, 1)] + [partner]
    for d in (1, -1, 2, -2):
        friends += [to_z(d)] * (abs(d) <= hz) + [to_y(d)] * (abs(d) <= hy)
    for device in friends:
        pl.semaphore_signal(barrier, inc=1, device_id=device, device_id_type=MESH)
    pl.semaphore_wait(barrier, len(friends))
    for copy in own:
        copy.wait()

    lz, rz = {}, {}
    hops = sorted(range(1, nx), key=lambda j: (nx - j) % nxs)

    def x_sem(a, kind, xs, block):
        return slot_sems.at[slot_id((a, kind, xs), 2) + block]

    def over_x(a, kind, src, dst):
        for j in [0] + hops:
            core, xs = divmod((nx - j) % nx, nxs)
            if j == 0:
                send(src, dst(0, 1), partner, x_sem(a, kind, 0, 1), second_core)
            else:
                send(src, dst(xs, c), to_x(j, core), x_sem(a, kind, xs, c))

    def from_x(a, kind, xs, dst):
        for block in (0, 1):
            only = second_core if (xs, block) == (0, 0) else None
            landed(dst(xs, block), x_sem(a, kind, xs, block), only)

    def right_at(a):
        buf = sources[a][1]
        return lambda xs, block: buf.at[xs, block, 0, :, right]

    def left_at(a, zs):
        buf = sources[a][1]
        return lambda xs, block: buf.at[xs, block, zs, :, left]

    def right_block(a, k, s):
        return sources[a][1].at[spans[k], :, s, :, right]

    for a in (0, 1):
        over_x(a, "r", own_right.at[a], right_at(a))
        for d in direct(hz, sides[a]):
            lz[a, d] = send(stage.at[a, 0], stage.at[a, slot[-d]], to_z(d))

    @pl.when(first_core)
    def _():
        for a, (_, buf) in enumerate(sources):
            buf[0, 0, 0, :, right] = own_right[a]

    load_in.wait()
    send_in = send(w_in.at[c], w_in.at[c], partner)
    load_out.wait()
    send_out = send(w_out.at[c], w_out.at[c], partner)

    for k in range(chunks):
        for a in (0, 1):
            for xs in range(k * per, (k + 1) * per):
                from_x(a, "r", xs, right_at(a))
            for d in direct(hz, sides[a]):
                rz[a, k, d] = send(right_block(a, k, 0), right_block(a, k, slot[-d]), to_z(d))
    for a in (0, 1):
        for sgn, d in relayed(hz, sides[a]):
            if d == 3:
                lz[a, 2 * sgn].wait_recv()
            lz[a, d * sgn] = send(
                stage.at[a, slot[-2 * sgn]], stage.at[a, slot[-d * sgn]], to_z((d - 2) * sgn)
            )
        for d in direct(hz, sides[a]):
            if not (hz > 2 and abs(d) == 2):
                lz[a, d].wait_recv()
        over_x(a, 0, stage.at[a, batches[0]], left_at(a, batches[0]))
    for k in range(chunks):
        for a in (0, 1):
            for sgn, d in relayed(hz, sides[a]):
                if d == 3:
                    rz[a, k, 2 * sgn].wait_recv()
                rz[a, k, d * sgn] = send(
                    right_block(a, k, slot[-2 * sgn]),
                    right_block(a, k, slot[-d * sgn]),
                    to_z((d - 2) * sgn),
                )
    for a in (0, 1):
        for sgn, d in relayed(hz, sides[a]):
            lz[a, d * sgn].wait_recv()
        if near < nz:
            over_x(a, 1, stage.at[a, batches[1]], left_at(a, batches[1]))

    @pl.when(first_core)
    def _():
        for a, (_, buf) in enumerate(sources):
            buf[0, 0, :, :, left] = stage[a]

    def gathered(a, k):
        for d in direct(hz, sides[a]):
            if not (hz > 2 and abs(d) == 2):
                rz[a, k, d].wait_recv()
        for sgn, d in relayed(hz, sides[a]):
            rz[a, k, d * sgn].wait_recv()
        for xs in range(k * per, (k + 1) * per):
            for i, zs in enumerate(batches):
                from_x(a, i, xs, left_at(a, zs))

    def product(a, k):
        total = 0
        for block in (0, 1):
            lhs = sources[a][1][spans[k], block].reshape(per * nz * rows, feat)
            if a == 0:
                out = jnp.dot(lhs, w_in[block], preferred_element_type=F32)
            else:
                out = lax.dot_general(
                    lhs, w_out[block], (((1,), (1,)), ((), ())), preferred_element_type=F32
                )
            total = out if block == 0 else total + out
        part[a, spans[k]] = total.reshape(per, ny, pr, hid)

    ring = {}

    def ring_send(a, k, o, value, d):
        i = len([key for key in ring if key[:2] == (a, k)])
        ring_out[a, k, i] = value.astype(BF16)
        ring[a, k, o] = (send(ring_out.at[a, k, i], ring_in.at[a, k, i], to_y(d)), i)

    def ring_got(a, k, o):
        copy, i = ring[a, k, o]
        copy.wait_recv()
        return ring_in[a, k, i].astype(F32)

    def ring_first(a, k):
        for sgn, d in relayed(hy, sides[a]):
            ring_send(a, k, d * sgn, part[a, spans[k], yn(d * sgn)], (d - 2) * sgn)
        for d in direct(hy, sides[a]):
            if abs(d) == 1:
                ring_send(a, k, d, part[a, spans[k], yn(d)], d)

    def ring_second(a, k):
        for d in direct(hy, sides[a]):
            if abs(d) == 2:
                value = part[a, spans[k], yn(d)]
                for sgn, far in relayed(hy, sides[a]):
                    if sgn * d > 0:
                        value = value + ring_got(a, k, far * sgn)
                ring_send(a, k, d, value, d)

    def ring_end(a, k):
        value = part[a, spans[k], y]
        for d in reversed(direct(hy, sides[a])):
            value = value + ring_got(a, k, d)
        return value

    for k in range(chunks):
        for a in (0, 1):
            gathered(a, k)
            if k == 0:
                (send_in, send_out)[a].wait_recv()
            product(a, k)
            ring_first(a, k)
    shared = []
    for a, other in enumerate((tok_other, og_other)):
        shared.append(send(sources[a][1].at[:, 1 - c], other, partner))
    for k in range(chunks):
        ring_second(0, k)
        ring_second(1, k)

    spread = {}

    def spread_first(buf, a, k):
        for d in direct(hy, sides[a]):
            block = buf.at[c, spans[k], y]
            spread[a, k, d] = send(block, block, to_y(d))

    def spread_second(buf, a, k):
        for d in direct(hy, sides[a]):
            spread[a, k, d].wait_recv()
            block = buf.at[c, spans[k], yn(-d)]
            for sgn, far in relayed(hy, sides[a]):
                if d == 2 * sgn:
                    spread[a, k, far * sgn] = send(block, block, to_y((far - 2) * sgn))

    def spread_end(a, k):
        for sgn, far in relayed(hy, sides[a]):
            spread[a, k, far * sgn].wait_recv()

    for k in range(chunks):
        preact = ring_end(0, k) + bias_in[...][None, None, :]
        act_all[c, spans[k], y] = gelu_value(preact).astype(BF16)
        slope = gelu_slope(preact)
        gp_all[c, spans[k], y] = (ring_end(1, k) * slope).astype(BF16)
        spread_first(gp_all, 1, k)
    for k in range(chunks):
        spread_second(gp_all, 1, k)
    for k in range(chunks):
        spread_first(act_all, 0, k)

    def row_terms(k, span):
        grads = gp_all[c, spans[k]].reshape(per * nz * rows, hid)
        for block in (0, 1):
            out = lax.dot_general(
                grads, w_in[block, span, :], (((1,), (1,)), ((), ())), preferred_element_type=F32
            ).reshape(per, nz, rows, span.size)
            g_full[spans[k], block, :, :, span] = out
            g_send[spans[k], block, :, :, span] = out.astype(BF16)

    tl, tr = {}, {}

    def home(kind, k, src, dst):
        for xs in range(k * per, (k + 1) * per):
            s = c * nxs + xs
            for block in (0, 1):
                sem = slot_sems.at[slot_id(kind, nx) + s]
                only = second_core if (xs, block) == (0, 0) else None
                send(src(xs, block), dst.at[s], to_x(s, block), sem, only)

    def at_home(kind, dst):
        for s in range(nx):
            sem = slot_sems.at[slot_id(kind, nx) + s]
            landed(dst.at[s], sem, second_core if s == 0 else None)

    def right_put(k, o, src, d):
        i = len([key for key in tr if key[0] == k])
        tr[k, o] = (send(src, rz_in.at[k, i], to_z(d)), i)

    def right_got(k, o):
        copy, i = tr[k, o]
        copy.wait_recv()
        return rz_in[k, i].astype(F32)

    def right_first(k):
        for sgn, d in relayed(hz, 1):
            o = d * sgn
            right_put(k, o, g_send.at[spans[k], :, slot[o], :, right], (d - 2) * sgn)
        for o in direct(hz, 1):
            if abs(o) == 1:
                right_put(k, o, g_send.at[spans[k], :, slot[o], :, right], o)

    def right_second(k):
        for i, o in enumerate(d for d in direct(hz, 1) if abs(d) == 2):
            value = g_full[spans[k], :, slot[o], :, right]
            for sgn, d in relayed(hz, 1):
                if sgn * o > 0:
                    value = value + right_got(k, d * sgn)
            rz_out[k, i] = value.astype(BF16)
            right_put(k, o, rz_out.at[k, i], o)

    def right_end(k):
        value = g_full[spans[k], :, 0, :, right]
        for o in reversed(direct(hz, 1)):
            value = value + right_got(k, o)
        rx_sum[spans[k]] = value
        home("right", k, lambda xs, block: rx_sum.at[xs, block], rx_in)

    def left_put(o, src, d):
        tl[o] = (send(src, lz_in.at[len(tl)], to_z(d)), len(tl))

    def left_got(o):
        copy, i = tl[o]
        copy.wait_recv()
        return lz_in[i]

    def left_first():
        at_home("left", lx_in)

        @pl.when(first_core)
        def _():
            lx_in[0] = g_send[0, 0, :, :, left]

        value = lx_in[0].astype(F32)
        for s in range(1, nx):
            value = value + lx_in[s].astype(F32)
        lz_sum[...] = value
        for sgn, d in relayed(hz, -1):
            left_put(d * sgn, lz_sum.at[slot[d * sgn]], (d - 2) * sgn)
        for o in direct(hz, -1):
            if abs(o) == 1:
                left_put(o, lz_sum.at[slot[o]], o)

    def left_second():
        for i, o in enumerate(d for d in direct(hz, -1) if abs(d) == 2):
            value = lz_sum[slot[o]]
            for sgn, d in relayed(hz, -1):
                if sgn * o > 0:
                    value = value + left_got(d * sgn)
            lz_out[i] = value
            left_put(o, lz_out.at[i], o)

    def left_end():
        value = lz_sum[0]
        for o in reversed(direct(hz, -1)):
            value = value + left_got(o)
        grad_tokens[:, left] = value.astype(BF16)

    half = nxs * nz * rows

    def weight_in_grad(i, n):
        step = feat // n
        span = pl.ds(i * step, step)
        out = lax.dot_general(
            tok_half[:, c, :, :, span].reshape(half, step),
            gp_all[c].reshape(half, hid),
            (((0,), (0,)), ((), ())),
            preferred_element_type=F32,
        ) + lax.dot_general(
            tok_other[:, :, :, span].reshape(half, step),
            gp_all[1 - c].reshape(half, hid),
            (((0,), (0,)), ((), ())),
            preferred_element_type=F32,
        )
        gwi[span, :] = out.astype(BF16)

    def weight_out_grad(i, n):
        step = hid // n
        span = pl.ds(i * step, step)
        out = lax.dot_general(
            act_all[c, :, :, :, span].reshape(half, step),
            og_half[:, c].reshape(half, feat),
            (((0,), (0,)), ((), ())),
            preferred_element_type=F32,
        ) + lax.dot_general(
            act_all[1 - c, :, :, :, span].reshape(half, step),
            og_other[...].reshape(half, feat),
            (((0,), (0,)), ((), ())),
            preferred_element_type=F32,
        )
        gwo[span, :] = out.astype(BF16)

    for k in range(chunks):
        spread_end(1, k)
        row_terms(k, right)
        right_first(k)
        row_terms(k, left)
        home("left", k, lambda xs, block: g_send.at[xs, block, :, :, left], lx_in)
    shared.append(send(gp_all.at[c], gp_all.at[c], partner))
    for k in range(chunks):
        spread_second(act_all, 0, k)
    for k in range(chunks):
        right_second(k)
    left_first()
    for copy in shared:
        copy.wait_recv()
    weight_in_grad(0, 3)
    for k in range(chunks):
        spread_end(0, k)
    share_act = send(act_all.at[c], act_all.at[c], partner)
    for k in range(chunks):
        right_end(k)
    left_second()
    for i in (1, 2):
        weight_in_grad(i, 3)
    store_in = local(gwi, grad_weight_in, 4)
    grad_bias[...] = jnp.sum(gp_all[...].astype(F32).reshape(2 * half, hid), axis=0, keepdims=True)
    share_act.wait_recv()
    for i in range(3):
        weight_out_grad(i, 3)
    store_out = local(gwo, grad_weight_out, 5)
    left_end()
    at_home("right", rx_in)

    @pl.when(first_core)
    def _():
        rx_in[0] = rx_sum[0, 0]

    value = rx_in[0]
    for s in range(1, nx):
        value = value + rx_in[s]
    grad_tokens[:, right] = value.astype(BF16)
    store_in.wait()
    store_out.wait()
    for copy, only in pending:
        if only is None:
            copy.wait_send()
        else:
            pl.when(only)(copy.wait_send)


def body(nz, ny, tokens, weight_in, bias_in, weight_out, out_grad):
    rows, feat = tokens.shape
    hid = weight_in.shape[1]
    cut = feat // 3 * 2
    rest = feat - cut
    nx = X
    nxs = nx // 2
    chunks = min(CHUNKS, nxs)
    per = nxs // chunks
    pr = nz * rows // ny
    vmem, anywhere = pl.BlockSpec(memory_space=pltpu.VMEM), pl.BlockSpec(memory_space=pl.ANY)
    out = pl.pallas_call(
        functools.partial(kernel, nz, ny, chunks),
        out_shape=(
            jax.ShapeDtypeStruct((rows, feat), BF16),
            jax.ShapeDtypeStruct((feat, hid), BF16),
            jax.ShapeDtypeStruct((hid, feat), BF16),
            jax.ShapeDtypeStruct((1, hid), F32),
        ),
        in_specs=[anywhere, anywhere, vmem, anywhere, anywhere],
        out_specs=(vmem, anywhere, anywhere, vmem),
        scratch_shapes=[
            pltpu.VMEM((nxs, 2, nz, rows, feat), BF16),
            pltpu.VMEM((nxs, 2, nz, rows, feat), BF16),
            pltpu.VMEM((nxs, nz, rows, feat), BF16),
            pltpu.VMEM((nxs, nz, rows, feat), BF16),
            pltpu.VMEM((2, nz, rows, cut), BF16),
            pltpu.VMEM((2, rows, rest), BF16),
            pltpu.VMEM((2, feat, hid), BF16),
            pltpu.VMEM((2, hid, feat), BF16),
            pltpu.VMEM((2, nxs, ny, pr, hid), F32),
            pltpu.VMEM((2, chunks, ny - 1, per, pr, hid), BF16),
            pltpu.VMEM((2, chunks, ny - 1, per, pr, hid), BF16),
            pltpu.VMEM((2, nxs, ny, pr, hid), BF16),
            pltpu.VMEM((2, nxs, ny, pr, hid), BF16),
            pltpu.VMEM((nxs, 2, nz, rows, feat), F32),
            pltpu.VMEM((nxs, 2, nz, rows, feat), BF16),
            pltpu.VMEM((nx, nz, rows, cut), BF16),
            pltpu.VMEM((nz, rows, cut), F32),
            pltpu.VMEM((2, rows, cut), F32),
            pltpu.VMEM((nz - 1, rows, cut), F32),
            pltpu.VMEM((chunks, 2, per, 2, rows, rest), BF16),
            pltpu.VMEM((chunks, nz - 1, per, 2, rows, rest), BF16),
            pltpu.VMEM((nxs, 2, rows, rest), F32),
            pltpu.VMEM((nx, rows, rest), F32),
            pltpu.VMEM((feat, hid), BF16),
            pltpu.VMEM((hid, feat), BF16),
            pltpu.SemaphoreType.DMA((N_SEMS,)),
            pltpu.SemaphoreType.DMA((N_SEMS,)),
            pltpu.SemaphoreType.DMA((64,)),
            pltpu.SemaphoreType.DMA((6,)),
        ],
        compiler_params=pltpu.CompilerParams(
            collective_id=0, has_side_effects=True, vmem_limit_bytes=56 * 1024 * 1024
        ),
    )(tokens, weight_in, bias_in, weight_out, out_grad)
    return pl.pallas_call(
        copy_out,
        out_shape=(
            jax.ShapeDtypeStruct((rows, feat), BF16),
            jax.ShapeDtypeStruct((feat, hid), BF16),
            jax.ShapeDtypeStruct((hid, feat), BF16),
            jax.ShapeDtypeStruct((hid,), F32),
        ),
        in_specs=[vmem, anywhere, anywhere, vmem],
        out_specs=(vmem, anywhere, anywhere, vmem),
        scratch_shapes=[
            pltpu.VMEM((feat, hid), BF16),
            pltpu.VMEM((hid, feat), BF16),
            pltpu.SemaphoreType.DMA((2, 3, 2)),
        ],
        compiler_params=pltpu.CompilerParams(vmem_limit_bytes=56 * 1024 * 1024),
    )(*out)


def solution(mesh):
    nz, ny = mesh.shape["row"] // X, mesh.shape["col"] // 2
    in_specs = (P("row", "col"), P("col", "row"), P("row"), P("row", "col"), P("row", "col"))
    out_specs = (P("row", "col"), P("col", "row"), P("row", "col"), P("row"))
    return jax.shard_map(
        functools.partial(body, nz, ny),
        mesh=mesh,
        in_specs=in_specs,
        out_specs=out_specs,
        check_vma=False,
    )
```

```python
import functools

import jax
import jax.numpy as jnp
from jax import lax
from jax.experimental import pallas as pl
from jax.experimental.pallas import tpu as pltpu
from jax.sharding import PartitionSpec as P

SQRT_HALF = 0.7071067811865476
INV_ROOT_TWO_PI = 0.3989422804014327
X = 4
N_SEMS = 192
CHUNKS = 2
LIMIT = 56 * 1024 * 1024
BF16, F32 = jnp.bfloat16, jnp.float32
MESH = pl.DeviceIdType.MESH


def gelu_value(preact):
    return preact * 0.5 * (1.0 + lax.erf(preact * SQRT_HALF))


def gelu_slope(preact):
    return 0.5 * (1.0 + lax.erf(preact * SQRT_HALF)) + preact * INV_ROOT_TWO_PI * jnp.exp(
        -0.5 * preact * preact
    )


def around(n):
    out = [0]
    for d in range(1, n // 2):
        out += [d, -d]
    return out + [n // 2]


def copy_out(*refs):
    copies = [pltpu.make_async_copy(refs[i], refs[4 + i], refs[8].at[i]) for i in (1, 2, 0, 3)]
    for copy in copies:
        copy.start()
    for copy in copies:
        copy.wait()


def kernel(
    nz,
    ny,
    chunks,
    tokens,
    weight_in,
    bias_in,
    weight_out,
    out_grad,
    grad_tokens,
    grad_weight_in,
    grad_weight_out,
    grad_bias,
    tok_half,
    og_half,
    tok_other,
    og_other,
    stage,
    own_right,
    w_in,
    w_out,
    part,
    ring_out,
    ring_in,
    act_all,
    gp_all,
    g_full,
    g_send,
    lx_in,
    lz_sum,
    lz_out,
    lz_in,
    rz_out,
    rz_in,
    rx_sum,
    rx_in,
    send_sems,
    recv_sems,
    slot_sems,
    local_sems,
):
    nx = X
    nxs = nx // 2
    rows, feat = tokens.shape
    hid = w_in.shape[-1]
    cut = stage.shape[-1]
    rest = feat - cut
    pr = nz * rows // ny
    hz, hy = nz // 2, ny // 2
    per = nxs // chunks
    spans = [pl.ds(k * per, per) for k in range(chunks)]
    turns = range(chunks - 1, -1, -1)
    row, col = lax.axis_index("row"), lax.axis_index("col")
    z, x = lax.div(row, nx), lax.rem(row, nx)
    y, c = lax.div(col, 2), lax.rem(col, 2)
    first_core, second_core = c == 0, c == 1

    def yn(d):
        return lax.rem(y + (ny + d), ny)

    def to_z(d):
        return (lax.rem(z + (nz + d), nz) * nx + x, col)

    def to_x(j, core):
        return (z * nx + lax.rem(x + j, nx), y * 2 + core)

    def to_y(d):
        return (row, yn(d) * 2 + c)

    partner = (row, y * 2 + (1 - c))
    pending = []
    slot_ids = {}

    def slot_id(key, count):
        if key not in slot_ids:
            slot_ids[key] = sum(n for _, n in slot_ids.values()), count
        return slot_ids[key][0]

    def send(src, dst, device, recv_sem=None, only=None):
        i = len(pending)
        copy = pltpu.make_async_remote_copy(
            src_ref=src,
            dst_ref=dst,
            send_sem=send_sems.at[i],
            recv_sem=recv_sems.at[i] if recv_sem is None else recv_sem,
            device_id=device,
            device_id_type=MESH,
        )
        if only is None:
            copy.start()
        else:
            pl.when(only)(copy.start)
        pending.append((copy, only))
        return copy

    def landed(dst, sem, only=None):
        copy = pltpu.make_async_remote_copy(
            src_ref=dst,
            dst_ref=dst,
            send_sem=send_sems.at[0],
            recv_sem=sem,
            device_id=partner,
            device_id_type=MESH,
        )
        if only is None:
            copy.wait_recv()
        else:
            pl.when(only)(copy.wait_recv)

    def local(src, dst, i):
        copy = pltpu.make_async_copy(src, dst, local_sems.at[i])
        copy.start()
        return copy

    left, right = pl.ds(0, cut), pl.ds(cut, rest)
    slot = {d: i for i, d in enumerate(around(nz))}
    slot[-hz] = slot[hz]
    near = 2 * min(hz, 3) - 1
    batches = [pl.ds(0, near)] + [pl.ds(near, nz - near)] * (near < nz)

    def direct(h, side):
        out = []
        for d in (2, 1):
            if d < h:
                out += [d, -d]
            elif d == h:
                out.append(d * side)
        return out

    def relayed(h, side):
        return [(sgn, d) for sgn in (1, -1) for d in (3, 4) if d < h or (d == h and sgn == side)]

    sources = ((tokens, tok_half), (out_grad, og_half))
    sides = (1, -1)
    own = []
    for a, (src, _) in enumerate(sources):
        own.append(local(src.at[:, left], stage.at[a, 0], 2 * a))
        own.append(local(src.at[:, right], own_right.at[a], 2 * a + 1))
    load_in = local(weight_in, w_in.at[c], 4)
    load_out = local(weight_out, w_out.at[c], 5)

    barrier = pltpu.get_barrier_semaphore()
    friends = [to_x(j, core) for j in range(1, nx) for core in (0, 1)] + [partner]
    for d in (1, -1, 2, -2):
        friends += [to_z(d)] * (abs(d) <= hz) + [to_y(d)] * (abs(d) <= hy)
    for device in friends:
        pl.semaphore_signal(barrier, inc=1, device_id=device, device_id_type=MESH)
    pl.semaphore_wait(barrier, len(friends))
    for copy in own:
        copy.wait()

    lz, rz = {}, {}
    hops = sorted(range(1, nx), key=lambda j: (nx - j) % nxs)

    def far_relay(kind):
        return nx == 4 and kind != "r"

    holders = ((second_core, first_core), (first_core, second_core))

    def relay_x(a, kind, zs):
        if not far_relay(kind):
            return
        buf = sources[a][1]
        holder = holders[a][0]
        for block in (0, 1):
            landed(buf.at[1, block, zs, :, left], x_sem(a, kind, 1, block), holder)
        send(
            buf.at[1, :, zs, :, left],
            buf.at[0, :, zs, :, left],
            to_x(1 if a == 0 else nx - 1, 1),
            slot_sems.at[slot_id((a, kind, "far"), 1)],
            holder,
        )

    def x_sem(a, kind, xs, block):
        return slot_sems.at[slot_id((a, kind, xs), 2) + block]

    def over_x(a, kind, src, dst):
        for j in [0] + hops:
            core, xs = divmod((nx - j) % nx, nxs)
            if far_relay(kind) and j == nx // 2:
                continue
            if j == 0:
                send(src, dst(0, 1), partner, x_sem(a, kind, 0, 1), second_core)
            else:
                send(src, dst(xs, c), to_x(j, core), x_sem(a, kind, xs, c))

    def from_x(a, kind, xs, dst):
        if far_relay(kind):
            if xs == 0:
                landed(dst(0, 1), x_sem(a, kind, 0, 1), first_core)
                landed(dst(0, slice(None)), slot_sems.at[slot_id((a, kind, "far"), 1)], second_core)
            else:
                for block in (0, 1):
                    landed(dst(xs, block), x_sem(a, kind, xs, block), holders[a][1])
            return
        for block in (0, 1):
            only = second_core if (xs, block) == (0, 0) else None
            landed(dst(xs, block), x_sem(a, kind, xs, block), only)

    def right_at(a):
        buf = sources[a][1]
        return lambda xs, block: buf.at[xs, block, 0, :, right]

    def left_at(a, zs):
        buf = sources[a][1]
        return lambda xs, block: buf.at[xs, block, zs, :, left]

    def right_block(a, k, s):
        return sources[a][1].at[spans[k], :, s, :, right]

    for a in (0, 1):
        over_x(a, "r", own_right.at[a], right_at(a))
        for d in direct(hz, sides[a]):
            lz[a, d] = send(stage.at[a, 0], stage.at[a, slot[-d]], to_z(d))

    @pl.when(first_core)
    def _():
        for a, (_, buf) in enumerate(sources):
            buf[0, 0, 0, :, right] = own_right[a]

    for k in turns:
        for a in (0, 1):
            for xs in range(k * per, (k + 1) * per):
                from_x(a, "r", xs, right_at(a))
            for d in direct(hz, sides[a]):
                rz[a, k, d] = send(right_block(a, k, 0), right_block(a, k, slot[-d]), to_z(d))
    load_in.wait()
    send_in = send(w_in.at[c], w_in.at[c], partner)
    for a in (0, 1):
        for sgn, d in relayed(hz, sides[a]):
            if d == 3:
                lz[a, 2 * sgn].wait_recv()
            lz[a, d * sgn] = send(
                stage.at[a, slot[-2 * sgn]], stage.at[a, slot[-d * sgn]], to_z((d - 2) * sgn)
            )
        for d in direct(hz, sides[a]):
            if not (hz > 2 and abs(d) == 2):
                lz[a, d].wait_recv()
        over_x(a, 0, stage.at[a, batches[0]], left_at(a, batches[0]))
    load_out.wait()
    send_out = send(w_out.at[c], w_out.at[c], partner)
    for k in turns:
        for a in (0, 1):
            for sgn, d in relayed(hz, sides[a]):
                if d == 3:
                    rz[a, k, 2 * sgn].wait_recv()
                rz[a, k, d * sgn] = send(
                    right_block(a, k, slot[-2 * sgn]),
                    right_block(a, k, slot[-d * sgn]),
                    to_z((d - 2) * sgn),
                )
    for a in (0, 1):
        for sgn, d in relayed(hz, sides[a]):
            lz[a, d * sgn].wait_recv()
        if near < nz:
            over_x(a, 1, stage.at[a, batches[1]], left_at(a, batches[1]))
        relay_x(a, 0, batches[0])

    @pl.when(first_core)
    def _():
        for a, (_, buf) in enumerate(sources):
            buf[0, 0, :, :, left] = stage[a]

    if near < nz:
        for a in (0, 1):
            relay_x(a, 1, batches[1])

    def gathered(a, k):
        for d in direct(hz, sides[a]):
            if not (hz > 2 and abs(d) == 2):
                rz[a, k, d].wait_recv()
        for sgn, d in relayed(hz, sides[a]):
            rz[a, k, d * sgn].wait_recv()
        for xs in range(k * per, (k + 1) * per):
            for i, zs in enumerate(batches):
                from_x(a, i, xs, left_at(a, zs))

    def product(a, k):
        total = 0
        for block in (0, 1):
            lhs = sources[a][1][spans[k], block].reshape(per * nz * rows, feat)
            if a == 0:
                out = jnp.dot(lhs, w_in[block], preferred_element_type=F32)
            else:
                out = lax.dot_general(
                    lhs, w_out[block], (((1,), (1,)), ((), ())), preferred_element_type=F32
                )
            total = out if block == 0 else total + out
        part[a, spans[k]] = total.reshape(per, ny, pr, hid)

    ring = {}

    def ring_send(a, k, o, value, d):
        i = len([key for key in ring if key[:2] == (a, k)])
        ring_out[a, k, i] = value.astype(BF16)
        ring[a, k, o] = (send(ring_out.at[a, k, i], ring_in.at[a, k, i], to_y(d)), i)

    def ring_got(a, k, o):
        copy, i = ring[a, k, o]
        copy.wait_recv()
        return ring_in[a, k, i].astype(F32)

    def ring_first(a, k):
        for sgn, d in relayed(hy, sides[a]):
            ring_send(a, k, d * sgn, part[a, spans[k], yn(d * sgn)], (d - 2) * sgn)
        for d in direct(hy, sides[a]):
            if abs(d) == 1:
                ring_send(a, k, d, part[a, spans[k], yn(d)], d)

    def ring_second(a, k):
        for d in direct(hy, sides[a]):
            if abs(d) == 2:
                value = part[a, spans[k], yn(d)]
                for sgn, far in relayed(hy, sides[a]):
                    if sgn * d > 0:
                        value = value + ring_got(a, k, far * sgn)
                ring_send(a, k, d, value, d)

    def ring_end(a, k):
        value = part[a, spans[k], y]
        for d in reversed(direct(hy, sides[a])):
            value = value + ring_got(a, k, d)
        return value

    for k in turns:
        for a in (0, 1):
            gathered(a, k)
            if k == turns[0]:
                (send_in, send_out)[a].wait_recv()
            product(a, k)
            ring_first(a, k)
    shared = []
    for a, other in enumerate((tok_other, og_other)):
        shared.append(send(sources[a][1].at[:, 1 - c], other, partner))
    for k in turns:
        ring_second(0, k)
        ring_second(1, k)

    spread = {}

    def spread_first(buf, a, k):
        for d in direct(hy, sides[a]):
            block = buf.at[c, spans[k], y]
            spread[a, k, d] = send(block, block, to_y(d))

    def spread_second(buf, a, k):
        for d in direct(hy, sides[a]):
            spread[a, k, d].wait_recv()
            block = buf.at[c, spans[k], yn(-d)]
            for sgn, far in relayed(hy, sides[a]):
                if d == 2 * sgn:
                    spread[a, k, far * sgn] = send(block, block, to_y((far - 2) * sgn))

    def spread_end(a, k):
        for sgn, far in relayed(hy, sides[a]):
            spread[a, k, far * sgn].wait_recv()

    for k in turns:
        preact = ring_end(0, k) + bias_in[...][None, None, :]
        act_all[c, spans[k], y] = gelu_value(preact).astype(BF16)
        slope = gelu_slope(preact)
        gp_all[c, spans[k], y] = (ring_end(1, k) * slope).astype(BF16)
        spread_first(gp_all, 1, k)
    for k in turns:
        spread_second(gp_all, 1, k)
    for k in turns:
        spread_first(act_all, 0, k)

    def row_terms(k, span):
        grads = gp_all[c, spans[k]].reshape(per * nz * rows, hid)
        for block in (0, 1):
            out = lax.dot_general(
                grads, w_in[block, span, :], (((1,), (1,)), ((), ())), preferred_element_type=F32
            ).reshape(per, nz, rows, span.size)
            g_full[spans[k], block, :, :, span] = out
            g_send[spans[k], block, :, :, span] = out.astype(BF16)

    tl, tr = {}, {}

    def home(kind, k, src, dst):
        for xs in range(k * per, (k + 1) * per):
            s = c * nxs + xs
            for block in (0, 1):
                sem = slot_sems.at[slot_id(kind, nx) + s]
                only = second_core if (xs, block) == (0, 0) else None
                send(src(xs, block), dst.at[s], to_x(s, block), sem, only)

    def at_home(kind, dst):
        for s in range(nx):
            sem = slot_sems.at[slot_id(kind, nx) + s]
            landed(dst.at[s], sem, second_core if s == 0 else None)

    def right_put(k, o, src, d):
        i = len([key for key in tr if key[0] == k])
        tr[k, o] = (send(src, rz_in.at[k, i], to_z(d)), i)

    def right_got(k, o):
        copy, i = tr[k, o]
        copy.wait_recv()
        return rz_in[k, i].astype(F32)

    def right_first(k):
        for sgn, d in relayed(hz, 1):
            o = d * sgn
            right_put(k, o, g_send.at[spans[k], :, slot[o], :, right], (d - 2) * sgn)
        for o in direct(hz, 1):
            if abs(o) == 1:
                right_put(k, o, g_send.at[spans[k], :, slot[o], :, right], o)

    def right_second(k):
        for i, o in enumerate(d for d in direct(hz, 1) if abs(d) == 2):
            value = g_full[spans[k], :, slot[o], :, right]
            for sgn, d in relayed(hz, 1):
                if sgn * o > 0:
                    value = value + right_got(k, d * sgn)
            rz_out[k, i] = value.astype(BF16)
            right_put(k, o, rz_out.at[k, i], o)

    def right_end(k):
        value = g_full[spans[k], :, 0, :, right]
        for o in reversed(direct(hz, 1)):
            value = value + right_got(k, o)
        rx_sum[spans[k]] = value
        home("right", k, lambda xs, block: rx_sum.at[xs, block], rx_in)

    def left_put(o, src, d):
        tl[o] = (send(src, lz_in.at[len(tl)], to_z(d)), len(tl))

    def left_got(o):
        copy, i = tl[o]
        copy.wait_recv()
        return lz_in[i]

    def left_first():
        at_home("left", lx_in)

        @pl.when(first_core)
        def _():
            lx_in[0] = g_send[0, 0, :, :, left]

        value = lx_in[0].astype(F32)
        for s in range(1, nx):
            value = value + lx_in[s].astype(F32)
        lz_sum[...] = value
        for sgn, d in relayed(hz, -1):
            left_put(d * sgn, lz_sum.at[slot[d * sgn]], (d - 2) * sgn)
        for o in direct(hz, -1):
            if abs(o) == 1:
                left_put(o, lz_sum.at[slot[o]], o)

    def left_second():
        for i, o in enumerate(d for d in direct(hz, -1) if abs(d) == 2):
            value = lz_sum[slot[o]]
            for sgn, d in relayed(hz, -1):
                if sgn * o > 0:
                    value = value + left_got(d * sgn)
            lz_out[i] = value
            left_put(o, lz_out.at[i], o)

    def left_end():
        value = lz_sum[0]
        for o in reversed(direct(hz, -1)):
            value = value + left_got(o)
        grad_tokens[:, left] = value.astype(BF16)

    half = nxs * nz * rows

    def weight_in_grad(i, n):
        step = feat // n
        span = pl.ds(i * step, step)
        out = lax.dot_general(
            tok_half[:, c, :, :, span].reshape(half, step),
            gp_all[c].reshape(half, hid),
            (((0,), (0,)), ((), ())),
            preferred_element_type=F32,
        ) + lax.dot_general(
            tok_other[:, :, :, span].reshape(half, step),
            gp_all[1 - c].reshape(half, hid),
            (((0,), (0,)), ((), ())),
            preferred_element_type=F32,
        )
        grad_weight_in[span, :] = out.astype(BF16)

    def weight_out_grad(i, n):
        step = hid // n
        span = pl.ds(i * step, step)
        out = lax.dot_general(
            act_all[c, :, :, :, span].reshape(half, step),
            og_half[:, c].reshape(half, feat),
            (((0,), (0,)), ((), ())),
            preferred_element_type=F32,
        ) + lax.dot_general(
            act_all[1 - c, :, :, :, span].reshape(half, step),
            og_other[...].reshape(half, feat),
            (((0,), (0,)), ((), ())),
            preferred_element_type=F32,
        )
        grad_weight_out[span, :] = out.astype(BF16)

    for k in turns:
        spread_end(1, k)
        row_terms(k, right)
        right_first(k)
        row_terms(k, left)
        home("left", k, lambda xs, block: g_send.at[xs, block, :, :, left], lx_in)
    shared.append(send(gp_all.at[c], gp_all.at[c], partner))
    for k in turns:
        spread_second(act_all, 0, k)
    for k in turns:
        right_second(k)
    left_first()
    for copy in shared:
        copy.wait_recv()
    weight_in_grad(0, 3)
    for k in turns:
        spread_end(0, k)
    share_act = send(act_all.at[c], act_all.at[c], partner)
    for k in turns:
        right_end(k)
    left_second()
    for i in (1, 2):
        weight_in_grad(i, 3)
    grad_bias[...] = jnp.sum(gp_all[...].astype(F32).reshape(2 * half, hid), axis=0)
    share_act.wait_recv()
    for i in range(3):
        weight_out_grad(i, 3)
    left_end()
    at_home("right", rx_in)

    @pl.when(first_core)
    def _():
        rx_in[0] = rx_sum[0, 0]

    value = rx_in[0]
    for s in range(1, nx):
        value = value + rx_in[s]
    grad_tokens[:, right] = value.astype(BF16)
    for copy, only in pending:
        if only is None:
            copy.wait_send()
        else:
            pl.when(only)(copy.wait_send)


def body(nz, ny, tokens, weight_in, bias_in, weight_out, out_grad):
    rows, feat = tokens.shape
    hid = weight_in.shape[1]
    cut = feat // 3 * 2
    rest = feat - cut
    nx = X
    nxs = nx // 2
    chunks = min(CHUNKS, nxs)
    per = nxs // chunks
    pr = nz * rows // ny
    vmem, anywhere = pl.BlockSpec(memory_space=pltpu.VMEM), pl.BlockSpec(memory_space=pl.ANY)
    out = pl.pallas_call(
        functools.partial(kernel, nz, ny, chunks),
        out_shape=(
            pltpu.VMEM((rows, feat), BF16),
            pltpu.VMEM((feat, hid), BF16),
            pltpu.VMEM((hid, feat), BF16),
            pltpu.VMEM((hid,), F32),
        ),
        in_specs=[anywhere, anywhere, vmem, anywhere, anywhere],
        out_specs=(vmem, vmem, vmem, vmem),
        scratch_shapes=[
            pltpu.VMEM((nxs, 2, nz, rows, feat), BF16),
            pltpu.VMEM((nxs, 2, nz, rows, feat), BF16),
            pltpu.VMEM((nxs, nz, rows, feat), BF16),
            pltpu.VMEM((nxs, nz, rows, feat), BF16),
            pltpu.VMEM((2, nz, rows, cut), BF16),
            pltpu.VMEM((2, rows, rest), BF16),
            pltpu.VMEM((2, feat, hid), BF16),
            pltpu.VMEM((2, hid, feat), BF16),
            pltpu.VMEM((2, nxs, ny, pr, hid), F32),
            pltpu.VMEM((2, chunks, ny - 1, per, pr, hid), BF16),
            pltpu.VMEM((2, chunks, ny - 1, per, pr, hid), BF16),
            pltpu.VMEM((2, nxs, ny, pr, hid), BF16),
            pltpu.VMEM((2, nxs, ny, pr, hid), BF16),
            pltpu.VMEM((nxs, 2, nz, rows, feat), F32),
            pltpu.VMEM((nxs, 2, nz, rows, feat), BF16),
            pltpu.VMEM((nx, nz, rows, cut), BF16),
            pltpu.VMEM((nz, rows, cut), F32),
            pltpu.VMEM((2, rows, cut), F32),
            pltpu.VMEM((nz - 1, rows, cut), F32),
            pltpu.VMEM((chunks, 2, per, 2, rows, rest), BF16),
            pltpu.VMEM((chunks, nz - 1, per, 2, rows, rest), BF16),
            pltpu.VMEM((nxs, 2, rows, rest), F32),
            pltpu.VMEM((nx, rows, rest), F32),
            pltpu.SemaphoreType.DMA((N_SEMS,)),
            pltpu.SemaphoreType.DMA((N_SEMS,)),
            pltpu.SemaphoreType.DMA((64,)),
            pltpu.SemaphoreType.DMA((6,)),
        ],
        compiler_params=pltpu.CompilerParams(
            collective_id=0, has_side_effects=True, vmem_limit_bytes=LIMIT
        ),
    )(tokens, weight_in, bias_in, weight_out, out_grad)
    return pl.pallas_call(
        copy_out,
        out_shape=tuple(jax.ShapeDtypeStruct(v.shape, v.dtype) for v in out),
        in_specs=[vmem] * 4,
        out_specs=(anywhere,) * 4,
        scratch_shapes=[pltpu.SemaphoreType.DMA((4,))],
        compiler_params=pltpu.CompilerParams(vmem_limit_bytes=1024 * 1024),
    )(*(pltpu.with_memory_space_constraint(v, pltpu.VMEM) for v in out))


def solution(mesh):
    nz, ny = mesh.shape["row"] // X, mesh.shape["col"] // 2
    in_specs = (P("row", "col"), P("col", "row"), P("row"), P("row", "col"), P("row", "col"))
    out_specs = (P("row", "col"), P("col", "row"), P("row", "col"), P("row"))
    return jax.shard_map(
        functools.partial(body, nz, ny),
        mesh=mesh,
        in_specs=in_specs,
        out_specs=out_specs,
        check_vma=False,
    )
```

```python
import functools

import jax
import jax.numpy as jnp
from jax import lax
from jax.experimental import pallas as pl
from jax.experimental.pallas import tpu as pltpu
from jax.sharding import PartitionSpec as P

SQRT_HALF = 0.7071067811865476
INV_ROOT_TWO_PI = 0.3989422804014327
X = 4
N_SEMS = 192
CHUNKS = 2
LIMIT = 56 * 1024 * 1024
BF16, F32 = jnp.bfloat16, jnp.float32
MESH = pl.DeviceIdType.MESH


def gelu_value(preact):
    return preact * 0.5 * (1.0 + lax.erf(preact * SQRT_HALF))


def gelu_slope(preact):
    return 0.5 * (1.0 + lax.erf(preact * SQRT_HALF)) + preact * INV_ROOT_TWO_PI * jnp.exp(
        -0.5 * preact * preact
    )


def around(n):
    out = [0]
    for d in range(1, n // 2):
        out += [d, -d]
    return out + [n // 2]


def copy_out(*refs):
    copies = [pltpu.make_async_copy(refs[i], refs[4 + i], refs[8].at[i]) for i in (1, 2, 0, 3)]
    for copy in copies:
        copy.start()
    for copy in copies:
        copy.wait()


def kernel(
    nz,
    ny,
    chunks,
    tokens,
    weight_in,
    bias_in,
    weight_out,
    out_grad,
    grad_tokens,
    grad_weight_in,
    grad_weight_out,
    grad_bias,
    tok_half,
    og_half,
    tok_other,
    og_other,
    stage,
    own_right,
    w_in,
    w_out,
    part,
    ring_out,
    ring_in,
    act_all,
    gp_all,
    g_full,
    g_send,
    lx_in,
    lz_sum,
    lz_out,
    lz_in,
    rz_out,
    rz_in,
    rx_sum,
    rx_in,
    send_sems,
    recv_sems,
    slot_sems,
    local_sems,
):
    nx = X
    nxs = nx // 2
    rows, feat = tokens.shape
    hid = w_in.shape[-1]
    cut = stage.shape[-1]
    rest = feat - cut
    pr = nz * rows // ny
    hz, hy = nz // 2, ny // 2
    per = nxs // chunks
    spans = [pl.ds(k * per, per) for k in range(chunks)]
    turns = range(chunks - 1, -1, -1)
    row, col = lax.axis_index("row"), lax.axis_index("col")
    z, x = lax.div(row, nx), lax.rem(row, nx)
    y, c = lax.div(col, 2), lax.rem(col, 2)
    first_core, second_core = c == 0, c == 1

    def yn(d):
        return lax.rem(y + (ny + d), ny)

    def to_z(d):
        return (lax.rem(z + (nz + d), nz) * nx + x, col)

    def to_x(j, core):
        return (z * nx + lax.rem(x + j, nx), y * 2 + core)

    def to_y(d):
        return (row, yn(d) * 2 + c)

    partner = (row, y * 2 + (1 - c))
    pending = []
    slot_ids = {}

    def slot_id(key, count):
        if key not in slot_ids:
            slot_ids[key] = sum(n for _, n in slot_ids.values()), count
        return slot_ids[key][0]

    def send(src, dst, device, recv_sem=None, only=None):
        i = len(pending)
        copy = pltpu.make_async_remote_copy(
            src_ref=src,
            dst_ref=dst,
            send_sem=send_sems.at[i],
            recv_sem=recv_sems.at[i] if recv_sem is None else recv_sem,
            device_id=device,
            device_id_type=MESH,
        )
        if only is None:
            copy.start()
        else:
            pl.when(only)(copy.start)
        pending.append((copy, only))
        return copy

    def landed(dst, sem, only=None):
        copy = pltpu.make_async_remote_copy(
            src_ref=dst,
            dst_ref=dst,
            send_sem=send_sems.at[0],
            recv_sem=sem,
            device_id=partner,
            device_id_type=MESH,
        )
        if only is None:
            copy.wait_recv()
        else:
            pl.when(only)(copy.wait_recv)

    def local(src, dst, i):
        copy = pltpu.make_async_copy(src, dst, local_sems.at[i])
        copy.start()
        return copy

    left, right = pl.ds(0, cut), pl.ds(cut, rest)
    slot = {d: i for i, d in enumerate(around(nz))}
    slot[-hz] = slot[hz]
    near = 2 * min(hz, 3) - 1
    batches = [pl.ds(0, near)] + [pl.ds(near, nz - near)] * (near < nz)

    def direct(h, side):
        out = []
        for d in (2, 1):
            if d < h:
                out += [d, -d]
            elif d == h:
                out.append(d * side)
        return out

    def relayed(h, side):
        return [(sgn, d) for sgn in (1, -1) for d in (3, 4) if d < h or (d == h and sgn == side)]

    sources = ((tokens, tok_half), (out_grad, og_half))
    sides = (1, -1)
    own = []
    for a, (src, _) in enumerate(sources):
        own.append(local(src.at[:, left], stage.at[a, 0], 2 * a))
        own.append(local(src.at[:, right], own_right.at[a], 2 * a + 1))
    load_in = local(weight_in, w_in.at[c], 4)
    load_out = local(weight_out, w_out.at[c], 5)

    barrier = pltpu.get_barrier_semaphore()
    friends = [to_x(j, core) for j in range(1, nx) for core in (0, 1)] + [partner]
    for d in (1, -1, 2, -2):
        friends += [to_z(d)] * (abs(d) <= hz) + [to_y(d)] * (abs(d) <= hy)
    for device in friends:
        pl.semaphore_signal(barrier, inc=1, device_id=device, device_id_type=MESH)
    pl.semaphore_wait(barrier, len(friends))
    for copy in own:
        copy.wait()

    lz, rz = {}, {}
    hops = sorted(range(1, nx), key=lambda j: -((nx - j) % nxs))

    def far_relay(kind):
        return nx == 4 and kind != "r"

    holders = ((second_core, first_core), (first_core, second_core))

    def relay_x(a, kind, zs):
        if not far_relay(kind):
            return
        buf = sources[a][1]
        holder = holders[a][0]
        for block in (0, 1):
            landed(buf.at[1, block, zs, :, left], x_sem(a, kind, 1, block), holder)
        send(
            buf.at[1, :, zs, :, left],
            buf.at[0, :, zs, :, left],
            to_x(1 if a == 0 else nx - 1, 1),
            slot_sems.at[slot_id((a, kind, "far"), 1)],
            holder,
        )

    def x_sem(a, kind, xs, block):
        return slot_sems.at[slot_id((a, kind, xs), 2) + block]

    def over_x(a, kind, src, dst):
        for j in hops + [0]:
            core, xs = divmod((nx - j) % nx, nxs)
            if far_relay(kind) and j == nx // 2:
                continue
            if j == 0:
                send(src, dst(0, 1), partner, x_sem(a, kind, 0, 1), second_core)
            else:
                send(src, dst(xs, c), to_x(j, core), x_sem(a, kind, xs, c))

    def from_x(a, kind, xs, dst):
        if far_relay(kind):
            if xs == 0:
                landed(dst(0, 1), x_sem(a, kind, 0, 1), first_core)
                landed(dst(0, slice(None)), slot_sems.at[slot_id((a, kind, "far"), 1)], second_core)
            else:
                for block in (0, 1):
                    landed(dst(xs, block), x_sem(a, kind, xs, block), holders[a][1])
            return
        for block in (0, 1):
            only = second_core if (xs, block) == (0, 0) else None
            landed(dst(xs, block), x_sem(a, kind, xs, block), only)

    def right_at(a):
        buf = sources[a][1]
        return lambda xs, block: buf.at[xs, block, 0, :, right]

    def left_at(a, zs):
        buf = sources[a][1]
        return lambda xs, block: buf.at[xs, block, zs, :, left]

    def right_block(a, k, s):
        return sources[a][1].at[spans[k], :, s, :, right]

    for a in (0, 1):
        over_x(a, "r", own_right.at[a], right_at(a))
        for d in direct(hz, sides[a]):
            lz[a, d] = send(stage.at[a, 0], stage.at[a, slot[-d]], to_z(d))

    @pl.when(first_core)
    def _():
        for a, (_, buf) in enumerate(sources):
            buf[0, 0, 0, :, right] = own_right[a]

    def right_start(k):
        for a in (0, 1):
            for xs in range(k * per, (k + 1) * per):
                from_x(a, "r", xs, right_at(a))
            for d in direct(hz, sides[a]):
                rz[a, k, d] = send(right_block(a, k, 0), right_block(a, k, slot[-d]), to_z(d))

    def right_relay(k):
        for a in (0, 1):
            for sgn, d in relayed(hz, sides[a]):
                if d == 3:
                    rz[a, k, 2 * sgn].wait_recv()
                rz[a, k, d * sgn] = send(
                    right_block(a, k, slot[-2 * sgn]),
                    right_block(a, k, slot[-d * sgn]),
                    to_z((d - 2) * sgn),
                )

    def left_relay(a):
        for sgn, d in relayed(hz, sides[a]):
            if d == 3:
                lz[a, 2 * sgn].wait_recv()
            lz[a, d * sgn] = send(
                stage.at[a, slot[-2 * sgn]], stage.at[a, slot[-d * sgn]], to_z((d - 2) * sgn)
            )
        for d in direct(hz, sides[a]):
            if not (hz > 2 and abs(d) == 2):
                lz[a, d].wait_recv()
        over_x(a, 0, stage.at[a, batches[0]], left_at(a, batches[0]))

    def left_rest(a):
        for sgn, d in relayed(hz, sides[a]):
            lz[a, d * sgn].wait_recv()
        if near < nz:
            over_x(a, 1, stage.at[a, batches[1]], left_at(a, batches[1]))

    right_start(turns[0])
    load_in.wait()
    send_in = send(w_in.at[c], w_in.at[c], partner)
    for a in (0, 1):
        left_relay(a)
    load_out.wait()
    send_out = send(w_out.at[c], w_out.at[c], partner)
    right_relay(turns[0])
    for k in turns[1:]:
        right_start(k)
    for a in (0, 1):
        left_rest(a)
        relay_x(a, 0, batches[0])

    @pl.when(first_core)
    def _():
        for a, (_, buf) in enumerate(sources):
            buf[0, 0, :, :, left] = stage[a]

    def gathered(a, k):
        for d in direct(hz, sides[a]):
            if not (hz > 2 and abs(d) == 2):
                rz[a, k, d].wait_recv()
        for sgn, d in relayed(hz, sides[a]):
            rz[a, k, d * sgn].wait_recv()
        for xs in range(k * per, (k + 1) * per):
            for i, zs in enumerate(batches):
                from_x(a, i, xs, left_at(a, zs))

    def product(a, k):
        total = 0
        for block in (0, 1):
            lhs = sources[a][1][spans[k], block].reshape(per * nz * rows, feat)
            if a == 0:
                out = jnp.dot(lhs, w_in[block], preferred_element_type=F32)
            else:
                out = lax.dot_general(
                    lhs, w_out[block], (((1,), (1,)), ((), ())), preferred_element_type=F32
                )
            total = out if block == 0 else total + out
        part[a, spans[k]] = total.reshape(per, ny, pr, hid)

    ring = {}

    def ring_send(a, k, o, value, d):
        i = len([key for key in ring if key[:2] == (a, k)])
        ring_out[a, k, i] = value.astype(BF16)
        ring[a, k, o] = (send(ring_out.at[a, k, i], ring_in.at[a, k, i], to_y(d)), i)

    def ring_got(a, k, o):
        copy, i = ring[a, k, o]
        copy.wait_recv()
        return ring_in[a, k, i].astype(F32)

    def ring_first(a, k):
        for sgn, d in relayed(hy, sides[a]):
            ring_send(a, k, d * sgn, part[a, spans[k], yn(d * sgn)], (d - 2) * sgn)
        for d in direct(hy, sides[a]):
            if abs(d) == 1:
                ring_send(a, k, d, part[a, spans[k], yn(d)], d)

    def ring_second(a, k):
        for d in direct(hy, sides[a]):
            if abs(d) == 2:
                value = part[a, spans[k], yn(d)]
                for sgn, far in relayed(hy, sides[a]):
                    if sgn * d > 0:
                        value = value + ring_got(a, k, far * sgn)
                ring_send(a, k, d, value, d)

    def ring_end(a, k):
        value = part[a, spans[k], y]
        for d in reversed(direct(hy, sides[a])):
            value = value + ring_got(a, k, d)
        return value

    flushed = [0]

    def flush():
        for copy, only in pending[flushed[0] :]:
            if only is None:
                copy.wait_send()
            else:
                pl.when(only)(copy.wait_send)
        flushed[0] = len(pending)

    def multiply(k):
        for a in (0, 1):
            gathered(a, k)
            if k == turns[0]:
                (send_in, send_out)[a].wait_recv()
            product(a, k)
            ring_first(a, k)

    spread = {}

    def spread_first(buf, a, k):
        for d in direct(hy, sides[a]):
            block = buf.at[c, spans[k], y]
            spread[a, k, d] = send(block, block, to_y(d))

    def spread_second(buf, a, k):
        for d in direct(hy, sides[a]):
            spread[a, k, d].wait_recv()
            block = buf.at[c, spans[k], yn(-d)]
            for sgn, far in relayed(hy, sides[a]):
                if d == 2 * sgn:
                    spread[a, k, far * sgn] = send(block, block, to_y((far - 2) * sgn))

    def spread_end(a, k):
        for sgn, far in relayed(hy, sides[a]):
            spread[a, k, far * sgn].wait_recv()

    def pointwise(k):
        preact = ring_end(0, k) + bias_in[...][None, None, :]
        act_all[c, spans[k], y] = gelu_value(preact).astype(BF16)
        slope = gelu_slope(preact)
        gp_all[c, spans[k], y] = (ring_end(1, k) * slope).astype(BF16)
        spread_first(gp_all, 1, k)

    def row_terms(k, span):
        grads = gp_all[c, spans[k]].reshape(per * nz * rows, hid)
        for block in (0, 1):
            out = lax.dot_general(
                grads, w_in[block, span, :], (((1,), (1,)), ((), ())), preferred_element_type=F32
            ).reshape(per, nz, rows, span.size)
            g_full[spans[k], block, :, :, span] = out
            g_send[spans[k], block, :, :, span] = out.astype(BF16)

    tl, tr = {}, {}

    def home(kind, k, src, dst):
        for xs in range(k * per, (k + 1) * per):
            s = c * nxs + xs
            for block in (0, 1):
                sem = slot_sems.at[slot_id(kind, nx) + s]
                only = second_core if (xs, block) == (0, 0) else None
                send(src(xs, block), dst.at[s], to_x(s, block), sem, only)

    def at_home(kind, dst):
        for s in range(nx):
            sem = slot_sems.at[slot_id(kind, nx) + s]
            landed(dst.at[s], sem, second_core if s == 0 else None)

    def right_put(k, o, src, d):
        i = len([key for key in tr if key[0] == k])
        tr[k, o] = (send(src, rz_in.at[k, i], to_z(d)), i)

    def right_got(k, o):
        copy, i = tr[k, o]
        copy.wait_recv()
        return rz_in[k, i].astype(F32)

    def right_first(k):
        for sgn, d in relayed(hz, 1):
            o = d * sgn
            right_put(k, o, g_send.at[spans[k], :, slot[o], :, right], (d - 2) * sgn)
        for o in direct(hz, 1):
            if abs(o) == 1:
                right_put(k, o, g_send.at[spans[k], :, slot[o], :, right], o)

    def right_second(k):
        for i, o in enumerate(d for d in direct(hz, 1) if abs(d) == 2):
            value = g_full[spans[k], :, slot[o], :, right]
            for sgn, d in relayed(hz, 1):
                if sgn * o > 0:
                    value = value + right_got(k, d * sgn)
            rz_out[k, i] = value.astype(BF16)
            right_put(k, o, rz_out.at[k, i], o)

    def right_end(k):
        value = g_full[spans[k], :, 0, :, right]
        for o in reversed(direct(hz, 1)):
            value = value + right_got(k, o)
        rx_sum[spans[k]] = value
        home("right", k, lambda xs, block: rx_sum.at[xs, block], rx_in)

    def left_put(o, src, d):
        tl[o] = (send(src, lz_in.at[len(tl)], to_z(d)), len(tl))

    def left_got(o):
        copy, i = tl[o]
        copy.wait_recv()
        return lz_in[i]

    def left_first():
        at_home("left", lx_in)

        @pl.when(first_core)
        def _():
            lx_in[0] = g_send[0, 0, :, :, left]

        value = lx_in[0].astype(F32)
        for s in range(1, nx):
            value = value + lx_in[s].astype(F32)
        lz_sum[...] = value
        for sgn, d in relayed(hz, -1):
            left_put(d * sgn, lz_sum.at[slot[d * sgn]], (d - 2) * sgn)
        for o in direct(hz, -1):
            if abs(o) == 1:
                left_put(o, lz_sum.at[slot[o]], o)

    def left_second():
        for i, o in enumerate(d for d in direct(hz, -1) if abs(d) == 2):
            value = lz_sum[slot[o]]
            for sgn, d in relayed(hz, -1):
                if sgn * o > 0:
                    value = value + left_got(d * sgn)
            lz_out[i] = value
            left_put(o, lz_out.at[i], o)

    def left_end():
        value = lz_sum[0]
        for o in reversed(direct(hz, -1)):
            value = value + left_got(o)
        grad_tokens[:, left] = value.astype(BF16)

    half = nxs * nz * rows

    def weight_in_grad(i, n):
        step = feat // n
        span = pl.ds(i * step, step)
        out = lax.dot_general(
            tok_half[:, c, :, :, span].reshape(half, step),
            gp_all[c].reshape(half, hid),
            (((0,), (0,)), ((), ())),
            preferred_element_type=F32,
        ) + lax.dot_general(
            tok_other[:, :, :, span].reshape(half, step),
            gp_all[1 - c].reshape(half, hid),
            (((0,), (0,)), ((), ())),
            preferred_element_type=F32,
        )
        grad_weight_in[span, :] = out.astype(BF16)

    def weight_out_grad(i, n):
        step = hid // n
        span = pl.ds(i * step, step)
        out = lax.dot_general(
            act_all[c, :, :, :, span].reshape(half, step),
            og_half[:, c].reshape(half, feat),
            (((0,), (0,)), ((), ())),
            preferred_element_type=F32,
        ) + lax.dot_general(
            act_all[1 - c, :, :, :, span].reshape(half, step),
            og_other[...].reshape(half, feat),
            (((0,), (0,)), ((), ())),
            preferred_element_type=F32,
        )
        grad_weight_out[span, :] = out.astype(BF16)

    shared = []

    def row_start(k):
        spread_end(1, k)
        row_terms(k, right)
        right_first(k)
        row_terms(k, left)
        home("left", k, lambda xs, block: g_send.at[xs, block, :, :, left], lx_in)
        block = gp_all.at[c, spans[k]]
        shared.append(send(block, block, partner))

    def share_act(k):
        spread_end(0, k)
        block = act_all.at[c, spans[k]]
        shared.append(send(block, block, partner))

    one, rest_turns = turns[0], list(turns[1:])
    for a in (0, 1):
        if near < nz:
            relay_x(a, 1, batches[1])
    multiply(one)
    for k in rest_turns:
        right_relay(k)
    ring_second(0, one)
    ring_second(1, one)
    for k in rest_turns:
        multiply(k)
    pointwise(one)
    for a, other in enumerate((tok_other, og_other)):
        shared.append(send(sources[a][1].at[:, 1 - c], other, partner))
    for k in rest_turns:
        ring_second(0, k)
        ring_second(1, k)
    spread_second(gp_all, 1, one)
    for k in rest_turns:
        pointwise(k)
    row_start(one)
    for k in rest_turns:
        spread_second(gp_all, 1, k)
    for k in turns:
        spread_first(act_all, 0, k)
    flush()
    right_second(one)
    for k in rest_turns:
        row_start(k)
    for k in turns:
        spread_second(act_all, 0, k)
    for copy in shared:
        copy.wait_recv()
    shared.clear()
    weight_in_grad(0, 3)
    for k in rest_turns:
        right_second(k)
    left_first()
    weight_in_grad(1, 3)
    for k in turns:
        right_end(k)
    left_second()
    for k in turns:
        share_act(k)
    weight_in_grad(2, 3)
    grad_bias[...] = jnp.sum(gp_all[...].astype(F32).reshape(2 * half, hid), axis=0)
    flush()
    for copy in shared:
        copy.wait_recv()
    for i in range(3):
        weight_out_grad(i, 3)
    left_end()
    at_home("right", rx_in)

    @pl.when(first_core)
    def _():
        rx_in[0] = rx_sum[0, 0]

    value = rx_in[0]
    for s in range(1, nx):
        value = value + rx_in[s]
    grad_tokens[:, right] = value.astype(BF16)
    flush()


def body(nz, ny, tokens, weight_in, bias_in, weight_out, out_grad):
    rows, feat = tokens.shape
    hid = weight_in.shape[1]
    cut = feat // 3 * 2
    rest = feat - cut
    nx = X
    nxs = nx // 2
    chunks = min(CHUNKS, nxs)
    per = nxs // chunks
    pr = nz * rows // ny
    vmem, anywhere = pl.BlockSpec(memory_space=pltpu.VMEM), pl.BlockSpec(memory_space=pl.ANY)
    out = pl.pallas_call(
        functools.partial(kernel, nz, ny, chunks),
        out_shape=(
            pltpu.VMEM((rows, feat), BF16),
            pltpu.VMEM((feat, hid), BF16),
            pltpu.VMEM((hid, feat), BF16),
            pltpu.VMEM((hid,), F32),
        ),
        in_specs=[anywhere, anywhere, vmem, anywhere, anywhere],
        out_specs=(vmem, vmem, vmem, vmem),
        scratch_shapes=[
            pltpu.VMEM((nxs, 2, nz, rows, feat), BF16),
            pltpu.VMEM((nxs, 2, nz, rows, feat), BF16),
            pltpu.VMEM((nxs, nz, rows, feat), BF16),
            pltpu.VMEM((nxs, nz, rows, feat), BF16),
            pltpu.VMEM((2, nz, rows, cut), BF16),
            pltpu.VMEM((2, rows, rest), BF16),
            pltpu.VMEM((2, feat, hid), BF16),
            pltpu.VMEM((2, hid, feat), BF16),
            pltpu.VMEM((2, nxs, ny, pr, hid), F32),
            pltpu.VMEM((2, chunks, ny - 1, per, pr, hid), BF16),
            pltpu.VMEM((2, chunks, ny - 1, per, pr, hid), BF16),
            pltpu.VMEM((2, nxs, ny, pr, hid), BF16),
            pltpu.VMEM((2, nxs, ny, pr, hid), BF16),
            pltpu.VMEM((nxs, 2, nz, rows, feat), F32),
            pltpu.VMEM((nxs, 2, nz, rows, feat), BF16),
            pltpu.VMEM((nx, nz, rows, cut), BF16),
            pltpu.VMEM((nz, rows, cut), F32),
            pltpu.VMEM((2, rows, cut), F32),
            pltpu.VMEM((nz - 1, rows, cut), F32),
            pltpu.VMEM((chunks, 2, per, 2, rows, rest), BF16),
            pltpu.VMEM((chunks, nz - 1, per, 2, rows, rest), BF16),
            pltpu.VMEM((nxs, 2, rows, rest), F32),
            pltpu.VMEM((nx, rows, rest), F32),
            pltpu.SemaphoreType.DMA((N_SEMS,)),
            pltpu.SemaphoreType.DMA((N_SEMS,)),
            pltpu.SemaphoreType.DMA((64,)),
            pltpu.SemaphoreType.DMA((6,)),
        ],
        compiler_params=pltpu.CompilerParams(
            collective_id=0, has_side_effects=True, vmem_limit_bytes=LIMIT
        ),
    )(tokens, weight_in, bias_in, weight_out, out_grad)
    return pl.pallas_call(
        copy_out,
        out_shape=tuple(jax.ShapeDtypeStruct(v.shape, v.dtype) for v in out),
        in_specs=[vmem] * 4,
        out_specs=(anywhere,) * 4,
        scratch_shapes=[pltpu.SemaphoreType.DMA((4,))],
        compiler_params=pltpu.CompilerParams(vmem_limit_bytes=1024 * 1024),
    )(*(pltpu.with_memory_space_constraint(v, pltpu.VMEM) for v in out))


def solution(mesh):
    nz, ny = mesh.shape["row"] // X, mesh.shape["col"] // 2
    in_specs = (P("row", "col"), P("col", "row"), P("row"), P("row", "col"), P("row", "col"))
    out_specs = (P("row", "col"), P("col", "row"), P("row", "col"), P("row"))
    return jax.shard_map(
        functools.partial(body, nz, ny),
        mesh=mesh,
        in_specs=in_specs,
        out_specs=out_specs,
        check_vma=False,
    )
```

```python
import functools

import jax
import jax.numpy as jnp
from jax import lax
from jax.experimental import pallas as pl
from jax.experimental.pallas import tpu as pltpu
from jax.sharding import PartitionSpec as P

SQRT_HALF = 0.7071067811865476
INV_ROOT_TWO_PI = 0.3989422804014327
X = 4
N_SEMS = 192
CHUNKS = 1
LIMIT = 56 * 1024 * 1024
BF16, F32 = jnp.bfloat16, jnp.float32
MESH = pl.DeviceIdType.MESH


def gelu_value(preact):
    return preact * 0.5 * (1.0 + lax.erf(preact * SQRT_HALF))


def gelu_slope(preact):
    return 0.5 * (1.0 + lax.erf(preact * SQRT_HALF)) + preact * INV_ROOT_TWO_PI * jnp.exp(
        -0.5 * preact * preact
    )


def around(n):
    out = [0]
    for d in range(1, n // 2):
        out += [d, -d]
    return out + [n // 2]


def copy_out(*refs):
    copies = [pltpu.make_async_copy(refs[i], refs[4 + i], refs[8].at[i]) for i in (1, 2, 0, 3)]
    for copy in copies:
        copy.start()
    for copy in copies:
        copy.wait()


def kernel(
    nz,
    ny,
    chunks,
    tokens,
    weight_in,
    bias_in,
    weight_out,
    out_grad,
    grad_tokens,
    grad_weight_in,
    grad_weight_out,
    grad_bias,
    tok_half,
    og_half,
    tok_other,
    og_other,
    stage,
    own_right,
    w_in,
    w_out,
    part,
    ring_out,
    ring_in,
    act_all,
    gp_all,
    g_full,
    g_send,
    lx_in,
    lz_sum,
    lz_out,
    lz_in,
    rz_out,
    rz_in,
    rx_sum,
    rx_in,
    send_sems,
    recv_sems,
    slot_sems,
    local_sems,
):
    nx = X
    nxs = nx // 2
    rows, feat = tokens.shape
    hid = w_in.shape[-1]
    cut = stage.shape[-1]
    rest = feat - cut
    pr = nz * rows // ny
    hz, hy = nz // 2, ny // 2
    per = nxs // chunks
    spans = [pl.ds(k * per, per) for k in range(chunks)]
    turns = range(chunks - 1, -1, -1)
    row, col = lax.axis_index("row"), lax.axis_index("col")
    z, x = lax.div(row, nx), lax.rem(row, nx)
    y, c = lax.div(col, 2), lax.rem(col, 2)
    first_core, second_core = c == 0, c == 1

    def yn(d):
        return lax.rem(y + (ny + d), ny)

    def to_z(d):
        return (lax.rem(z + (nz + d), nz) * nx + x, col)

    def to_x(j, core):
        return (z * nx + lax.rem(x + j, nx), y * 2 + core)

    def to_y(d):
        return (row, yn(d) * 2 + c)

    partner = (row, y * 2 + (1 - c))
    pending = []
    slot_ids = {}

    def slot_id(key, count):
        if key not in slot_ids:
            slot_ids[key] = sum(n for _, n in slot_ids.values()), count
        return slot_ids[key][0]

    def send(src, dst, device, recv_sem=None, only=None):
        i = len(pending)
        copy = pltpu.make_async_remote_copy(
            src_ref=src,
            dst_ref=dst,
            send_sem=send_sems.at[i],
            recv_sem=recv_sems.at[i] if recv_sem is None else recv_sem,
            device_id=device,
            device_id_type=MESH,
        )
        if only is None:
            copy.start()
        else:
            pl.when(only)(copy.start)
        pending.append((copy, only))
        return copy

    def landed(dst, sem, only=None):
        copy = pltpu.make_async_remote_copy(
            src_ref=dst,
            dst_ref=dst,
            send_sem=send_sems.at[0],
            recv_sem=sem,
            device_id=partner,
            device_id_type=MESH,
        )
        if only is None:
            copy.wait_recv()
        else:
            pl.when(only)(copy.wait_recv)

    def local(src, dst, i):
        copy = pltpu.make_async_copy(src, dst, local_sems.at[i])
        copy.start()
        return copy

    left, right = pl.ds(0, cut), pl.ds(cut, rest)
    slot = {d: i for i, d in enumerate(around(nz))}
    slot[-hz] = slot[hz]
    near = 2 * min(hz, 3) - 1
    batches = [pl.ds(0, near)] + [pl.ds(near, nz - near)] * (near < nz)

    def direct(h, side):
        out = []
        for d in (2, 1):
            if d < h:
                out += [d, -d]
            elif d == h:
                out.append(d * side)
        return out

    def relayed(h, side):
        return [(sgn, d) for sgn in (1, -1) for d in (3, 4) if d < h or (d == h and sgn == side)]

    sources = ((tokens, tok_half), (out_grad, og_half))
    sides = (1, -1)
    own = []
    for a, (src, _) in enumerate(sources):
        own.append(local(src.at[:, left], stage.at[a, 0], 2 * a))
        own.append(local(src.at[:, right], own_right.at[a], 2 * a + 1))
    load_in = local(weight_in, w_in.at[c], 4)
    load_out = local(weight_out, w_out.at[c], 5)

    barrier = pltpu.get_barrier_semaphore()
    friends = [to_x(j, core) for j in range(1, nx) for core in (0, 1)] + [partner]
    for d in (1, -1, 2, -2):
        friends += [to_z(d)] * (abs(d) <= hz) + [to_y(d)] * (abs(d) <= hy)
    for device in friends:
        pl.semaphore_signal(barrier, inc=1, device_id=device, device_id_type=MESH)
    pl.semaphore_wait(barrier, len(friends))
    for copy in own:
        copy.wait()

    lz, rz = {}, {}
    hops = sorted(range(1, nx), key=lambda j: -((nx - j) % nxs))

    def far_relay(kind):
        return nx == 4 and kind != "r"

    holders = ((second_core, first_core), (first_core, second_core))

    def relay_x(a, kind, zs):
        if not far_relay(kind):
            return
        buf = sources[a][1]
        holder = holders[a][0]
        for block in (0, 1):
            landed(buf.at[1, block, zs, :, left], x_sem(a, kind, 1, block), holder)
        send(
            buf.at[1, :, zs, :, left],
            buf.at[0, :, zs, :, left],
            to_x(1 if a == 0 else nx - 1, 1),
            slot_sems.at[slot_id((a, kind, "far"), 1)],
            holder,
        )

    def x_sem(a, kind, xs, block):
        return slot_sems.at[slot_id((a, kind, xs), 2) + block]

    def over_x(a, kind, src, dst):
        for j in hops + [0]:
            core, xs = divmod((nx - j) % nx, nxs)
            if far_relay(kind) and j == nx // 2:
                continue
            if j == 0:
                send(src, dst(0, 1), partner, x_sem(a, kind, 0, 1), second_core)
            else:
                send(src, dst(xs, c), to_x(j, core), x_sem(a, kind, xs, c))

    def from_x(a, kind, xs, dst):
        if far_relay(kind):
            if xs == 0:
                landed(dst(0, 1), x_sem(a, kind, 0, 1), first_core)
                landed(dst(0, slice(None)), slot_sems.at[slot_id((a, kind, "far"), 1)], second_core)
            else:
                for block in (0, 1):
                    landed(dst(xs, block), x_sem(a, kind, xs, block), holders[a][1])
            return
        for block in (0, 1):
            only = second_core if (xs, block) == (0, 0) else None
            landed(dst(xs, block), x_sem(a, kind, xs, block), only)

    def right_at(a):
        buf = sources[a][1]
        return lambda xs, block: buf.at[xs, block, 0, :, right]

    def left_at(a, zs):
        buf = sources[a][1]
        return lambda xs, block: buf.at[xs, block, zs, :, left]

    def right_block(a, k, s):
        return sources[a][1].at[spans[k], :, s, :, right]

    for a in (0, 1):
        over_x(a, "r", own_right.at[a], right_at(a))
        for d in direct(hz, sides[a]):
            lz[a, d] = send(stage.at[a, 0], stage.at[a, slot[-d]], to_z(d))

    @pl.when(first_core)
    def _():
        for a, (_, buf) in enumerate(sources):
            buf[0, 0, 0, :, right] = own_right[a]

    def right_start(k):
        for a in (0, 1):
            for xs in range(k * per, (k + 1) * per):
                from_x(a, "r", xs, right_at(a))
            for d in direct(hz, sides[a]):
                rz[a, k, d] = send(right_block(a, k, 0), right_block(a, k, slot[-d]), to_z(d))

    def right_relay(k):
        for a in (0, 1):
            for sgn, d in relayed(hz, sides[a]):
                if d == 3:
                    rz[a, k, 2 * sgn].wait_recv()
                rz[a, k, d * sgn] = send(
                    right_block(a, k, slot[-2 * sgn]),
                    right_block(a, k, slot[-d * sgn]),
                    to_z((d - 2) * sgn),
                )

    def left_relay(a):
        for sgn, d in relayed(hz, sides[a]):
            if d == 3:
                lz[a, 2 * sgn].wait_recv()
            lz[a, d * sgn] = send(
                stage.at[a, slot[-2 * sgn]], stage.at[a, slot[-d * sgn]], to_z((d - 2) * sgn)
            )
        for d in direct(hz, sides[a]):
            if not (hz > 2 and abs(d) == 2):
                lz[a, d].wait_recv()
        over_x(a, 0, stage.at[a, batches[0]], left_at(a, batches[0]))

    def left_rest(a):
        for sgn, d in relayed(hz, sides[a]):
            lz[a, d * sgn].wait_recv()
        if near < nz:
            over_x(a, 1, stage.at[a, batches[1]], left_at(a, batches[1]))

    right_start(turns[0])
    load_in.wait()
    send_in = send(w_in.at[c], w_in.at[c], partner)
    for a in (0, 1):
        left_relay(a)
    load_out.wait()
    send_out = send(w_out.at[c], w_out.at[c], partner)
    right_relay(turns[0])
    for k in turns[1:]:
        right_start(k)
    for a in (0, 1):
        left_rest(a)
        relay_x(a, 0, batches[0])

    @pl.when(first_core)
    def _():
        for a, (_, buf) in enumerate(sources):
            buf[0, 0, :, :, left] = stage[a]

    def gathered(a, k):
        for d in direct(hz, sides[a]):
            if not (hz > 2 and abs(d) == 2):
                rz[a, k, d].wait_recv()
        for sgn, d in relayed(hz, sides[a]):
            rz[a, k, d * sgn].wait_recv()
        for xs in range(k * per, (k + 1) * per):
            for i, zs in enumerate(batches):
                from_x(a, i, xs, left_at(a, zs))

    def product(a, k):
        total = 0
        for block in (0, 1):
            lhs = sources[a][1][spans[k], block].reshape(per * nz * rows, feat)
            if a == 0:
                out = jnp.dot(lhs, w_in[block], preferred_element_type=F32)
            else:
                out = lax.dot_general(
                    lhs, w_out[block], (((1,), (1,)), ((), ())), preferred_element_type=F32
                )
            total = out if block == 0 else total + out
        part[a, spans[k]] = total.reshape(per, ny, pr, hid)

    ring = {}

    def ring_send(a, k, o, value, d):
        i = len([key for key in ring if key[:2] == (a, k)])
        ring_out[a, k, i] = value.astype(BF16)
        ring[a, k, o] = (send(ring_out.at[a, k, i], ring_in.at[a, k, i], to_y(d)), i)

    def ring_got(a, k, o):
        copy, i = ring[a, k, o]
        copy.wait_recv()
        return ring_in[a, k, i].astype(F32)

    def ring_first(a, k):
        for sgn, d in relayed(hy, sides[a]):
            ring_send(a, k, d * sgn, part[a, spans[k], yn(d * sgn)], (d - 2) * sgn)
        for d in direct(hy, sides[a]):
            if abs(d) == 1:
                ring_send(a, k, d, part[a, spans[k], yn(d)], d)

    def ring_second(a, k):
        for d in direct(hy, sides[a]):
            if abs(d) == 2:
                value = part[a, spans[k], yn(d)]
                for sgn, far in relayed(hy, sides[a]):
                    if sgn * d > 0:
                        value = value + ring_got(a, k, far * sgn)
                ring_send(a, k, d, value, d)

    def ring_end(a, k):
        value = part[a, spans[k], y]
        for d in reversed(direct(hy, sides[a])):
            value = value + ring_got(a, k, d)
        return value

    flushed = [0]

    def flush():
        for copy, only in pending[flushed[0] :]:
            if only is None:
                copy.wait_send()
            else:
                pl.when(only)(copy.wait_send)
        flushed[0] = len(pending)

    def multiply(k):
        for a in (0, 1):
            gathered(a, k)
            if k == turns[0]:
                (send_in, send_out)[a].wait_recv()
            product(a, k)
            ring_first(a, k)

    spread = {}

    def spread_first(buf, a, k):
        for d in direct(hy, sides[a]):
            block = buf.at[c, spans[k], y]
            spread[a, k, d] = send(block, block, to_y(d))

    def spread_second(buf, a, k):
        for d in direct(hy, sides[a]):
            spread[a, k, d].wait_recv()
            block = buf.at[c, spans[k], yn(-d)]
            for sgn, far in relayed(hy, sides[a]):
                if d == 2 * sgn:
                    spread[a, k, far * sgn] = send(block, block, to_y((far - 2) * sgn))

    def spread_end(a, k):
        for sgn, far in relayed(hy, sides[a]):
            spread[a, k, far * sgn].wait_recv()

    def pointwise(k):
        preact = ring_end(0, k) + bias_in[...][None, None, :]
        act_all[c, spans[k], y] = gelu_value(preact).astype(BF16)
        slope = gelu_slope(preact)
        gp_all[c, spans[k], y] = (ring_end(1, k) * slope).astype(BF16)
        spread_first(gp_all, 1, k)

    def row_terms(k, span):
        grads = gp_all[c, spans[k]].reshape(per * nz * rows, hid)
        for block in (0, 1):
            out = lax.dot_general(
                grads, w_in[block, span, :], (((1,), (1,)), ((), ())), preferred_element_type=F32
            ).reshape(per, nz, rows, span.size)
            g_full[spans[k], block, :, :, span] = out
            g_send[spans[k], block, :, :, span] = out.astype(BF16)

    tl, tr = {}, {}

    def home(kind, k, src, dst):
        for xs in range(k * per, (k + 1) * per):
            s = c * nxs + xs
            for block in (0, 1):
                sem = slot_sems.at[slot_id(kind, nx) + s]
                only = second_core if (xs, block) == (0, 0) else None
                send(src(xs, block), dst.at[s], to_x(s, block), sem, only)

    def at_home(kind, dst):
        for s in range(nx):
            sem = slot_sems.at[slot_id(kind, nx) + s]
            landed(dst.at[s], sem, second_core if s == 0 else None)

    def right_put(k, o, src, d):
        i = len([key for key in tr if key[0] == k])
        tr[k, o] = (send(src, rz_in.at[k, i], to_z(d)), i)

    def right_got(k, o):
        copy, i = tr[k, o]
        copy.wait_recv()
        return rz_in[k, i].astype(F32)

    def right_first(k):
        for sgn, d in relayed(hz, 1):
            o = d * sgn
            right_put(k, o, g_send.at[spans[k], :, slot[o], :, right], (d - 2) * sgn)
        for o in direct(hz, 1):
            if abs(o) == 1:
                right_put(k, o, g_send.at[spans[k], :, slot[o], :, right], o)

    def right_second(k):
        for i, o in enumerate(d for d in direct(hz, 1) if abs(d) == 2):
            value = g_full[spans[k], :, slot[o], :, right]
            for sgn, d in relayed(hz, 1):
                if sgn * o > 0:
                    value = value + right_got(k, d * sgn)
            rz_out[k, i] = value.astype(BF16)
            right_put(k, o, rz_out.at[k, i], o)

    def right_end(k):
        value = g_full[spans[k], :, 0, :, right]
        for o in reversed(direct(hz, 1)):
            value = value + right_got(k, o)
        rx_sum[spans[k]] = value
        home("right", k, lambda xs, block: rx_sum.at[xs, block], rx_in)

    def left_put(o, src, d):
        tl[o] = (send(src, lz_in.at[len(tl)], to_z(d)), len(tl))

    def left_got(o):
        copy, i = tl[o]
        copy.wait_recv()
        return lz_in[i]

    def left_first():
        at_home("left", lx_in)

        @pl.when(first_core)
        def _():
            lx_in[0] = g_send[0, 0, :, :, left]

        value = lx_in[0].astype(F32)
        for s in range(1, nx):
            value = value + lx_in[s].astype(F32)
        lz_sum[...] = value
        for sgn, d in relayed(hz, -1):
            left_put(d * sgn, lz_sum.at[slot[d * sgn]], (d - 2) * sgn)
        for o in direct(hz, -1):
            if abs(o) == 1:
                left_put(o, lz_sum.at[slot[o]], o)

    def left_second():
        for i, o in enumerate(d for d in direct(hz, -1) if abs(d) == 2):
            value = lz_sum[slot[o]]
            for sgn, d in relayed(hz, -1):
                if sgn * o > 0:
                    value = value + left_got(d * sgn)
            lz_out[i] = value
            left_put(o, lz_out.at[i], o)

    def left_end():
        value = lz_sum[0]
        for o in reversed(direct(hz, -1)):
            value = value + left_got(o)
        grad_tokens[:, left] = value.astype(BF16)

    half = nxs * nz * rows

    def weight_in_grad(i, n):
        step = feat // n
        span = pl.ds(i * step, step)
        out = lax.dot_general(
            tok_half[:, c, :, :, span].reshape(half, step),
            gp_all[c].reshape(half, hid),
            (((0,), (0,)), ((), ())),
            preferred_element_type=F32,
        ) + lax.dot_general(
            tok_other[:, :, :, span].reshape(half, step),
            gp_all[1 - c].reshape(half, hid),
            (((0,), (0,)), ((), ())),
            preferred_element_type=F32,
        )
        grad_weight_in[span, :] = out.astype(BF16)

    def weight_out_grad(i, n):
        step = hid // n
        span = pl.ds(i * step, step)
        out = lax.dot_general(
            act_all[c, :, :, :, span].reshape(half, step),
            og_half[:, c].reshape(half, feat),
            (((0,), (0,)), ((), ())),
            preferred_element_type=F32,
        ) + lax.dot_general(
            act_all[1 - c, :, :, :, span].reshape(half, step),
            og_other[...].reshape(half, feat),
            (((0,), (0,)), ((), ())),
            preferred_element_type=F32,
        )
        grad_weight_out[span, :] = out.astype(BF16)

    shared = []

    def row_start(k):
        spread_end(1, k)
        row_terms(k, right)
        right_first(k)
        row_terms(k, left)
        home("left", k, lambda xs, block: g_send.at[xs, block, :, :, left], lx_in)
        block = gp_all.at[c, spans[k]]
        shared.append(send(block, block, partner))

    def share_act(k):
        spread_end(0, k)
        block = act_all.at[c, spans[k]]
        shared.append(send(block, block, partner))

    one, rest_turns = turns[0], list(turns[1:])
    for a in (0, 1):
        if near < nz:
            relay_x(a, 1, batches[1])
    multiply(one)
    for k in rest_turns:
        right_relay(k)
    ring_second(0, one)
    ring_second(1, one)
    for k in rest_turns:
        multiply(k)
    pointwise(one)
    for a, other in enumerate((tok_other, og_other)):
        shared.append(send(sources[a][1].at[:, 1 - c], other, partner))
    for k in rest_turns:
        ring_second(0, k)
        ring_second(1, k)
    spread_second(gp_all, 1, one)
    for k in rest_turns:
        pointwise(k)
    row_start(one)
    for k in rest_turns:
        spread_second(gp_all, 1, k)
    for k in turns:
        spread_first(act_all, 0, k)
    flush()
    right_second(one)
    for k in rest_turns:
        row_start(k)
    for k in turns:
        spread_second(act_all, 0, k)
    for copy in shared:
        copy.wait_recv()
    shared.clear()
    weight_in_grad(0, 3)
    for k in rest_turns:
        right_second(k)
    left_first()
    weight_in_grad(1, 3)
    for k in turns:
        right_end(k)
    left_second()
    for k in turns:
        share_act(k)
    weight_in_grad(2, 3)
    grad_bias[...] = jnp.sum(gp_all[...].astype(F32).reshape(2 * half, hid), axis=0)
    flush()
    for copy in shared:
        copy.wait_recv()
    for i in range(3):
        weight_out_grad(i, 3)
    left_end()
    at_home("right", rx_in)

    @pl.when(first_core)
    def _():
        rx_in[0] = rx_sum[0, 0]

    value = rx_in[0]
    for s in range(1, nx):
        value = value + rx_in[s]
    grad_tokens[:, right] = value.astype(BF16)
    flush()


def body(nz, ny, tokens, weight_in, bias_in, weight_out, out_grad):
    rows, feat = tokens.shape
    hid = weight_in.shape[1]
    cut = feat // 3 * 2
    rest = feat - cut
    nx = X
    nxs = nx // 2
    chunks = min(CHUNKS, nxs)
    per = nxs // chunks
    pr = nz * rows // ny
    vmem, anywhere = pl.BlockSpec(memory_space=pltpu.VMEM), pl.BlockSpec(memory_space=pl.ANY)
    out = pl.pallas_call(
        functools.partial(kernel, nz, ny, chunks),
        out_shape=(
            pltpu.VMEM((rows, feat), BF16),
            pltpu.VMEM((feat, hid), BF16),
            pltpu.VMEM((hid, feat), BF16),
            pltpu.VMEM((hid,), F32),
        ),
        in_specs=[anywhere, anywhere, vmem, anywhere, anywhere],
        out_specs=(vmem, vmem, vmem, vmem),
        scratch_shapes=[
            pltpu.VMEM((nxs, 2, nz, rows, feat), BF16),
            pltpu.VMEM((nxs, 2, nz, rows, feat), BF16),
            pltpu.VMEM((nxs, nz, rows, feat), BF16),
            pltpu.VMEM((nxs, nz, rows, feat), BF16),
            pltpu.VMEM((2, nz, rows, cut), BF16),
            pltpu.VMEM((2, rows, rest), BF16),
            pltpu.VMEM((2, feat, hid), BF16),
            pltpu.VMEM((2, hid, feat), BF16),
            pltpu.VMEM((2, nxs, ny, pr, hid), F32),
            pltpu.VMEM((2, chunks, ny - 1, per, pr, hid), BF16),
            pltpu.VMEM((2, chunks, ny - 1, per, pr, hid), BF16),
            pltpu.VMEM((2, nxs, ny, pr, hid), BF16),
            pltpu.VMEM((2, nxs, ny, pr, hid), BF16),
            pltpu.VMEM((nxs, 2, nz, rows, feat), F32),
            pltpu.VMEM((nxs, 2, nz, rows, feat), BF16),
            pltpu.VMEM((nx, nz, rows, cut), BF16),
            pltpu.VMEM((nz, rows, cut), F32),
            pltpu.VMEM((2, rows, cut), F32),
            pltpu.VMEM((nz - 1, rows, cut), F32),
            pltpu.VMEM((chunks, 2, per, 2, rows, rest), BF16),
            pltpu.VMEM((chunks, nz - 1, per, 2, rows, rest), BF16),
            pltpu.VMEM((nxs, 2, rows, rest), F32),
            pltpu.VMEM((nx, rows, rest), F32),
            pltpu.SemaphoreType.DMA((N_SEMS,)),
            pltpu.SemaphoreType.DMA((N_SEMS,)),
            pltpu.SemaphoreType.DMA((64,)),
            pltpu.SemaphoreType.DMA((6,)),
        ],
        compiler_params=pltpu.CompilerParams(
            collective_id=0, has_side_effects=True, vmem_limit_bytes=LIMIT
        ),
    )(tokens, weight_in, bias_in, weight_out, out_grad)
    return pl.pallas_call(
        copy_out,
        out_shape=tuple(jax.ShapeDtypeStruct(v.shape, v.dtype) for v in out),
        in_specs=[vmem] * 4,
        out_specs=(anywhere,) * 4,
        scratch_shapes=[pltpu.SemaphoreType.DMA((4,))],
        compiler_params=pltpu.CompilerParams(vmem_limit_bytes=1024 * 1024),
    )(*(pltpu.with_memory_space_constraint(v, pltpu.VMEM) for v in out))


def solution(mesh):
    nz, ny = mesh.shape["row"] // X, mesh.shape["col"] // 2
    in_specs = (P("row", "col"), P("col", "row"), P("row"), P("row", "col"), P("row", "col"))
    out_specs = (P("row", "col"), P("col", "row"), P("row", "col"), P("row"))
    return jax.shard_map(
        functools.partial(body, nz, ny),
        mesh=mesh,
        in_specs=in_specs,
        out_specs=out_specs,
        check_vma=False,
    )
```

```python
import functools

import jax
import jax.numpy as jnp
from jax import lax
from jax.experimental import pallas as pl
from jax.experimental.pallas import tpu as pltpu
from jax.sharding import PartitionSpec as P

SQRT_HALF = 0.7071067811865476
INV_ROOT_TWO_PI = 0.3989422804014327
X = 4
N_SEMS = 192
CHUNKS = 2
LIMIT = 56 * 1024 * 1024
BF16, F32 = jnp.bfloat16, jnp.float32
MESH = pl.DeviceIdType.MESH


def gelu_value(preact):
    return preact * 0.5 * (1.0 + lax.erf(preact * SQRT_HALF))


def gelu_slope(preact):
    return 0.5 * (1.0 + lax.erf(preact * SQRT_HALF)) + preact * INV_ROOT_TWO_PI * jnp.exp(
        -0.5 * preact * preact
    )


def around(n):
    out = [0]
    for d in range(1, n // 2):
        out += [d, -d]
    return out + [n // 2]


def copy_out(*refs):
    copies = [pltpu.make_async_copy(refs[i], refs[4 + i], refs[8].at[i]) for i in (1, 2, 0, 3)]
    for copy in copies:
        copy.start()
    for copy in copies:
        copy.wait()


def kernel(
    nz,
    ny,
    chunks,
    tokens,
    weight_in,
    bias_in,
    weight_out,
    out_grad,
    grad_tokens,
    grad_weight_in,
    grad_weight_out,
    grad_bias,
    tok_half,
    og_half,
    tok_other,
    og_other,
    tok_t,
    stage,
    own_right,
    w_in,
    w_out,
    part,
    ring_out,
    ring_in,
    act_all,
    gp_all,
    g_full,
    g_send,
    lx_in,
    lz_sum,
    lz_out,
    lz_in,
    rz_out,
    rz_in,
    rx_sum,
    rx_in,
    send_sems,
    recv_sems,
    slot_sems,
    local_sems,
):
    nx = X
    nxs = nx // 2
    rows, feat = tokens.shape
    hid = w_in.shape[-1]
    cut = stage.shape[-1]
    rest = feat - cut
    pr = nz * rows // ny
    hz, hy = nz // 2, ny // 2
    per = nxs // chunks
    spans = [pl.ds(k * per, per) for k in range(chunks)]
    turns = range(chunks - 1, -1, -1)
    row, col = lax.axis_index("row"), lax.axis_index("col")
    z, x = lax.div(row, nx), lax.rem(row, nx)
    y, c = lax.div(col, 2), lax.rem(col, 2)
    first_core, second_core = c == 0, c == 1

    def yn(d):
        return lax.rem(y + (ny + d), ny)

    def to_z(d):
        return (lax.rem(z + (nz + d), nz) * nx + x, col)

    def to_x(j, core):
        return (z * nx + lax.rem(x + j, nx), y * 2 + core)

    def to_y(d):
        return (row, yn(d) * 2 + c)

    partner = (row, y * 2 + (1 - c))
    pending = []
    slot_ids = {}

    def slot_id(key, count):
        if key not in slot_ids:
            slot_ids[key] = sum(n for _, n in slot_ids.values()), count
        return slot_ids[key][0]

    def send(src, dst, device, recv_sem=None, only=None):
        i = len(pending)
        copy = pltpu.make_async_remote_copy(
            src_ref=src,
            dst_ref=dst,
            send_sem=send_sems.at[i],
            recv_sem=recv_sems.at[i] if recv_sem is None else recv_sem,
            device_id=device,
            device_id_type=MESH,
        )
        if only is None:
            copy.start()
        else:
            pl.when(only)(copy.start)
        pending.append((copy, only))
        return copy

    def landed(dst, sem, only=None):
        copy = pltpu.make_async_remote_copy(
            src_ref=dst,
            dst_ref=dst,
            send_sem=send_sems.at[0],
            recv_sem=sem,
            device_id=partner,
            device_id_type=MESH,
        )
        if only is None:
            copy.wait_recv()
        else:
            pl.when(only)(copy.wait_recv)

    def local(src, dst, i):
        copy = pltpu.make_async_copy(src, dst, local_sems.at[i])
        copy.start()
        return copy

    left, right = pl.ds(0, cut), pl.ds(cut, rest)
    low = lx_in.shape[-1]
    west, east = pl.ds(0, low), pl.ds(low, feat - low)
    slot = {d: i for i, d in enumerate(around(nz))}
    slot[-hz] = slot[hz]
    near = 2 * min(hz, 3) - 1
    batches = [pl.ds(0, near)] + [pl.ds(near, nz - near)] * (near < nz)

    def direct(h, side):
        out = []
        for d in (2, 1):
            if d < h:
                out += [d, -d]
            elif d == h:
                out.append(d * side)
        return out

    def relayed(h, side):
        return [(sgn, d) for sgn in (1, -1) for d in (3, 4) if d < h or (d == h and sgn == side)]

    sources = ((tokens, tok_half), (out_grad, og_half))
    sides = (1, -1)
    own = []
    for a, (src, _) in enumerate(sources):
        own.append(local(src.at[:, left], stage.at[a, 0], 2 * a))
        own.append(local(src.at[:, right], own_right.at[a], 2 * a + 1))
    load_in = local(weight_in, w_in.at[c], 4)
    load_out = local(weight_out, w_out.at[c], 5)

    barrier = pltpu.get_barrier_semaphore()
    friends = [to_x(j, core) for j in range(1, nx) for core in (0, 1)] + [partner]
    for d in (1, -1, 2, -2):
        friends += [to_z(d)] * (abs(d) <= hz) + [to_y(d)] * (abs(d) <= hy)
    for device in friends:
        pl.semaphore_signal(barrier, inc=1, device_id=device, device_id_type=MESH)
    pl.semaphore_wait(barrier, len(friends))
    for copy in own:
        copy.wait()

    lz, rz = {}, {}
    hops = sorted(range(1, nx), key=lambda j: -((nx - j) % nxs))

    def far_relay(kind):
        return nx == 4 and kind != "r"

    holders = ((second_core, first_core), (first_core, second_core))

    def relay_x(a, kind, zs):
        if not far_relay(kind):
            return
        buf = sources[a][1]
        holder = holders[a][0]
        for block in (0, 1):
            landed(buf.at[1, block, zs, :, left], x_sem(a, kind, 1, block), holder)
        send(
            buf.at[1, :, zs, :, left],
            buf.at[0, :, zs, :, left],
            to_x(1 if a == 0 else nx - 1, 1),
            slot_sems.at[slot_id((a, kind, "far"), 1)],
            holder,
        )

    def x_sem(a, kind, xs, block):
        return slot_sems.at[slot_id((a, kind, xs), 2) + block]

    def over_x(a, kind, src, dst):
        for j in hops + [0]:
            core, xs = divmod((nx - j) % nx, nxs)
            if far_relay(kind) and j == nx // 2:
                continue
            if j == 0:
                send(src, dst(0, 1), partner, x_sem(a, kind, 0, 1), second_core)
            else:
                send(src, dst(xs, c), to_x(j, core), x_sem(a, kind, xs, c))

    def from_x(a, kind, xs, dst):
        if far_relay(kind):
            if xs == 0:
                landed(dst(0, 1), x_sem(a, kind, 0, 1), first_core)
                landed(dst(0, slice(None)), slot_sems.at[slot_id((a, kind, "far"), 1)], second_core)
            else:
                for block in (0, 1):
                    landed(dst(xs, block), x_sem(a, kind, xs, block), holders[a][1])
            return
        for block in (0, 1):
            only = second_core if (xs, block) == (0, 0) else None
            landed(dst(xs, block), x_sem(a, kind, xs, block), only)

    def right_at(a):
        buf = sources[a][1]
        return lambda xs, block: buf.at[xs, block, 0, :, right]

    def left_at(a, zs):
        buf = sources[a][1]
        return lambda xs, block: buf.at[xs, block, zs, :, left]

    def right_block(a, k, s):
        return sources[a][1].at[spans[k], :, s, :, right]

    for a in (0, 1):
        over_x(a, "r", own_right.at[a], right_at(a))
        for d in direct(hz, sides[a]):
            lz[a, d] = send(stage.at[a, 0], stage.at[a, slot[-d]], to_z(d))

    @pl.when(first_core)
    def _():
        for a, (_, buf) in enumerate(sources):
            buf[0, 0, 0, :, right] = own_right[a]

    def right_start(k):
        for a in (0, 1):
            for xs in range(k * per, (k + 1) * per):
                from_x(a, "r", xs, right_at(a))
            for d in direct(hz, sides[a]):
                rz[a, k, d] = send(right_block(a, k, 0), right_block(a, k, slot[-d]), to_z(d))

    def right_relay(k):
        for a in (0, 1):
            for sgn, d in relayed(hz, sides[a]):
                if d == 3:
                    rz[a, k, 2 * sgn].wait_recv()
                rz[a, k, d * sgn] = send(
                    right_block(a, k, slot[-2 * sgn]),
                    right_block(a, k, slot[-d * sgn]),
                    to_z((d - 2) * sgn),
                )

    def left_relay(a):
        for sgn, d in relayed(hz, sides[a]):
            if d == 3:
                lz[a, 2 * sgn].wait_recv()
            lz[a, d * sgn] = send(
                stage.at[a, slot[-2 * sgn]], stage.at[a, slot[-d * sgn]], to_z((d - 2) * sgn)
            )
        for d in direct(hz, sides[a]):
            if not (hz > 2 and abs(d) == 2):
                lz[a, d].wait_recv()
        over_x(a, 0, stage.at[a, batches[0]], left_at(a, batches[0]))

    def left_rest(a):
        for sgn, d in relayed(hz, sides[a]):
            lz[a, d * sgn].wait_recv()
        if near < nz:
            over_x(a, 1, stage.at[a, batches[1]], left_at(a, batches[1]))

    right_start(turns[0])
    load_in.wait()
    send_in = send(w_in.at[c], w_in.at[c], partner)
    for a in (0, 1):
        left_relay(a)
    load_out.wait()
    send_out = send(w_out.at[c], w_out.at[c], partner)
    right_relay(turns[0])
    for k in turns[1:]:
        right_start(k)
    for a in (0, 1):
        left_rest(a)
        relay_x(a, 0, batches[0])

    @pl.when(first_core)
    def _():
        for a, (_, buf) in enumerate(sources):
            buf[0, 0, :, :, left] = stage[a]

    def gathered(a, k):
        for d in direct(hz, sides[a]):
            if not (hz > 2 and abs(d) == 2):
                rz[a, k, d].wait_recv()
        for sgn, d in relayed(hz, sides[a]):
            rz[a, k, d * sgn].wait_recv()
        for xs in range(k * per, (k + 1) * per):
            for i, zs in enumerate(batches):
                from_x(a, i, xs, left_at(a, zs))

    def product(a, k):
        total = 0
        for block in (0, 1):
            lhs = sources[a][1][spans[k], block].reshape(per * nz * rows, feat)
            if a == 0:
                out = jnp.dot(lhs, w_in[block], preferred_element_type=F32)
            else:
                out = lax.dot_general(
                    lhs, w_out[block], (((1,), (1,)), ((), ())), preferred_element_type=F32
                )
            total = out if block == 0 else total + out
        part[a, spans[k]] = total.reshape(per, ny, pr, hid)

    ring = {}

    def ring_send(a, k, o, value, d):
        i = len([key for key in ring if key[:2] == (a, k)])
        ring_out[a, k, i] = value.astype(BF16)
        ring[a, k, o] = (send(ring_out.at[a, k, i], ring_in.at[a, k, i], to_y(d)), i)

    def ring_got(a, k, o):
        copy, i = ring[a, k, o]
        copy.wait_recv()
        return ring_in[a, k, i].astype(F32)

    def ring_first(a, k):
        for sgn, d in relayed(hy, sides[a]):
            ring_send(a, k, d * sgn, part[a, spans[k], yn(d * sgn)], (d - 2) * sgn)
        for d in direct(hy, sides[a]):
            if abs(d) == 1:
                ring_send(a, k, d, part[a, spans[k], yn(d)], d)

    def ring_second(a, k):
        for d in direct(hy, sides[a]):
            if abs(d) == 2:
                value = part[a, spans[k], yn(d)]
                for sgn, far in relayed(hy, sides[a]):
                    if sgn * d > 0:
                        value = value + ring_got(a, k, far * sgn)
                ring_send(a, k, d, value, d)

    def ring_end(a, k):
        value = part[a, spans[k], y]
        for d in reversed(direct(hy, sides[a])):
            value = value + ring_got(a, k, d)
        return value

    flushed = [0]

    def flush():
        for copy, only in pending[flushed[0] :]:
            if only is None:
                copy.wait_send()
            else:
                pl.when(only)(copy.wait_send)
        flushed[0] = len(pending)

    def multiply(k):
        for a in (0, 1):
            gathered(a, k)
            if k == turns[0]:
                (send_in, send_out)[a].wait_recv()
            product(a, k)
            ring_first(a, k)

    spread = {}

    def spread_first(buf, a, k):
        for d in direct(hy, sides[a]):
            block = buf.at[c, spans[k], y]
            spread[a, k, d] = send(block, block, to_y(d))

    def spread_second(buf, a, k):
        for d in direct(hy, sides[a]):
            spread[a, k, d].wait_recv()
            block = buf.at[c, spans[k], yn(-d)]
            for sgn, far in relayed(hy, sides[a]):
                if d == 2 * sgn:
                    spread[a, k, far * sgn] = send(block, block, to_y((far - 2) * sgn))

    def spread_end(a, k):
        for sgn, far in relayed(hy, sides[a]):
            spread[a, k, far * sgn].wait_recv()

    def pointwise(k):
        preact = ring_end(0, k) + bias_in[...][None, None, :]
        act_all[c, spans[k], y] = gelu_value(preact).astype(BF16)
        slope = gelu_slope(preact)
        gp_all[c, spans[k], y] = (ring_end(1, k) * slope).astype(BF16)
        spread_first(gp_all, 1, k)

    def row_terms(k, span):
        grads = gp_all[c, spans[k]].reshape(per * nz * rows, hid)
        for block in (0, 1):
            out = lax.dot_general(
                grads, w_in[block, span, :], (((1,), (1,)), ((), ())), preferred_element_type=F32
            ).reshape(per, nz, rows, span.size)
            g_full[spans[k], block, :, :, span] = out
            g_send[spans[k], block, :, :, span] = out.astype(BF16)

    tl, tr = {}, {}

    def home(kind, k, src, dst):
        for xs in range(k * per, (k + 1) * per):
            s = c * nxs + xs
            for block in (0, 1):
                sem = slot_sems.at[slot_id(kind, nx) + s]
                only = second_core if (xs, block) == (0, 0) else None
                send(src(xs, block), dst.at[s], to_x(s, block), sem, only)

    def at_home(kind, dst):
        for s in range(nx):
            sem = slot_sems.at[slot_id(kind, nx) + s]
            landed(dst.at[s], sem, second_core if s == 0 else None)

    def right_put(k, o, src, d):
        i = len([key for key in tr if key[0] == k])
        tr[k, o] = (send(src, rz_in.at[k, i], to_z(d)), i)

    def right_got(k, o):
        copy, i = tr[k, o]
        copy.wait_recv()
        return rz_in[k, i].astype(F32)

    def right_first(k):
        for sgn, d in relayed(hz, 1):
            o = d * sgn
            right_put(k, o, g_send.at[spans[k], :, slot[o], :, east], (d - 2) * sgn)
        for o in direct(hz, 1):
            if abs(o) == 1:
                right_put(k, o, g_send.at[spans[k], :, slot[o], :, east], o)

    def right_second(k):
        for i, o in enumerate(d for d in direct(hz, 1) if abs(d) == 2):
            value = g_full[spans[k], :, slot[o], :, east]
            for sgn, d in relayed(hz, 1):
                if sgn * o > 0:
                    value = value + right_got(k, d * sgn)
            rz_out[k, i] = value.astype(BF16)
            right_put(k, o, rz_out.at[k, i], o)

    def right_end(k):
        value = g_full[spans[k], :, 0, :, east]
        for o in reversed(direct(hz, 1)):
            value = value + right_got(k, o)
        rx_sum[spans[k]] = value
        home("right", k, lambda xs, block: rx_sum.at[xs, block], rx_in)

    def left_put(o, src, d):
        tl[o] = (send(src, lz_in.at[len(tl)], to_z(d)), len(tl))

    def left_got(o):
        copy, i = tl[o]
        copy.wait_recv()
        return lz_in[i]

    def left_first():
        at_home("left", lx_in)

        @pl.when(first_core)
        def _():
            lx_in[0] = g_send[0, 0, :, :, west]

        value = lx_in[0].astype(F32)
        for s in range(1, nx):
            value = value + lx_in[s].astype(F32)
        lz_sum[...] = value
        for sgn, d in relayed(hz, -1):
            left_put(d * sgn, lz_sum.at[slot[d * sgn]], (d - 2) * sgn)
        for o in direct(hz, -1):
            if abs(o) == 1:
                left_put(o, lz_sum.at[slot[o]], o)

    def left_second():
        for i, o in enumerate(d for d in direct(hz, -1) if abs(d) == 2):
            value = lz_sum[slot[o]]
            for sgn, d in relayed(hz, -1):
                if sgn * o > 0:
                    value = value + left_got(d * sgn)
            lz_out[i] = value
            left_put(o, lz_out.at[i], o)

    def left_end():
        value = lz_sum[0]
        for o in reversed(direct(hz, -1)):
            value = value + left_got(o)
        grad_tokens[:, west] = value.astype(BF16)

    half = nxs * nz * rows

    def weight_in_grad(i, n):
        step = feat // n
        span = pl.ds(i * step, step)
        out = jnp.dot(
            tok_t[0, span], gp_all[c].reshape(half, hid), preferred_element_type=F32
        ) + jnp.dot(
            tok_t[1, span], gp_all[1 - c].reshape(half, hid), preferred_element_type=F32
        )
        grad_weight_in[span, :] = out.astype(BF16)

    def weight_out_grad(i, n):
        step = hid // n
        span = pl.ds(i * step, step)
        out = lax.dot_general(
            act_all[c, :, :, :, span].reshape(half, step),
            og_half[:, c].reshape(half, feat),
            (((0,), (0,)), ((), ())),
            preferred_element_type=F32,
        ) + lax.dot_general(
            act_all[1 - c, :, :, :, span].reshape(half, step),
            og_other[...].reshape(half, feat),
            (((0,), (0,)), ((), ())),
            preferred_element_type=F32,
        )
        grad_weight_out[span, :] = out.astype(BF16)

    shared = []

    def row_start(k):
        spread_end(1, k)
        row_terms(k, east)
        right_first(k)
        row_terms(k, west)
        home("left", k, lambda xs, block: g_send.at[xs, block, :, :, west], lx_in)
        block = gp_all.at[c, spans[k]]
        shared.append(send(block, block, partner))

    def share_act(k):
        spread_end(0, k)
        block = act_all.at[c, spans[k]]
        shared.append(send(block, block, partner))

    def all_shared():
        for copy in shared:
            copy.wait_recv()
        shared.clear()

    one, rest_turns = turns[0], list(turns[1:])
    for a in (0, 1):
        if near < nz:
            relay_x(a, 1, batches[1])
    multiply(one)
    for k in rest_turns:
        right_relay(k)
    ring_second(0, one)
    ring_second(1, one)
    for k in rest_turns:
        multiply(k)
    pointwise(one)
    for a, other in enumerate((tok_other, og_other)):
        shared.append(send(sources[a][1].at[:, 1 - c], other, partner))
    for k in rest_turns:
        ring_second(0, k)
        ring_second(1, k)
    spread_second(gp_all, 1, one)
    tok_t[0] = tok_half[:, c].reshape(half, feat).T
    for k in rest_turns:
        pointwise(k)
    row_start(one)
    for k in rest_turns:
        spread_second(gp_all, 1, k)
    for k in turns:
        spread_first(act_all, 0, k)
    shared[0].wait_recv()
    tok_t[1] = tok_other[...].reshape(half, feat).T
    right_second(one)
    for k in rest_turns:
        row_start(k)
    for k in turns:
        spread_second(act_all, 0, k)
    flush()
    for copy in shared[1:]:
        copy.wait_recv()
    shared.clear()
    weight_in_grad(0, 3)
    for k in rest_turns:
        right_second(k)
    left_first()
    for k in turns:
        share_act(k)
    weight_in_grad(1, 3)
    weight_in_grad(2, 3)
    for k in turns:
        right_end(k)
    left_second()
    grad_bias[...] = jnp.sum(gp_all[...].astype(F32).reshape(2 * half, hid), axis=0)
    all_shared()
    for i in range(3):
        weight_out_grad(i, 3)
    left_end()
    at_home("right", rx_in)

    @pl.when(first_core)
    def _():
        rx_in[0] = rx_sum[0, 0]

    value = rx_in[0]
    for s in range(1, nx):
        value = value + rx_in[s]
    grad_tokens[:, east] = value.astype(BF16)
    flush()


def body(nz, ny, tokens, weight_in, bias_in, weight_out, out_grad):
    rows, feat = tokens.shape
    hid = weight_in.shape[1]
    cut = feat // 3 * 2
    rest = feat - cut
    low = feat // 3
    high = feat - low
    nx = X
    nxs = nx // 2
    chunks = min(CHUNKS, nxs)
    per = nxs // chunks
    pr = nz * rows // ny
    vmem, anywhere = pl.BlockSpec(memory_space=pltpu.VMEM), pl.BlockSpec(memory_space=pl.ANY)
    out = pl.pallas_call(
        functools.partial(kernel, nz, ny, chunks),
        out_shape=(
            pltpu.VMEM((rows, feat), BF16),
            pltpu.VMEM((feat, hid), BF16),
            pltpu.VMEM((hid, feat), BF16),
            pltpu.VMEM((hid,), F32),
        ),
        in_specs=[anywhere, anywhere, vmem, anywhere, anywhere],
        out_specs=(vmem, vmem, vmem, vmem),
        scratch_shapes=[
            pltpu.VMEM((nxs, 2, nz, rows, feat), BF16),
            pltpu.VMEM((nxs, 2, nz, rows, feat), BF16),
            pltpu.VMEM((nxs, nz, rows, feat), BF16),
            pltpu.VMEM((nxs, nz, rows, feat), BF16),
            pltpu.VMEM((2, feat, nxs * nz * rows), BF16),
            pltpu.VMEM((2, nz, rows, cut), BF16),
            pltpu.VMEM((2, rows, rest), BF16),
            pltpu.VMEM((2, feat, hid), BF16),
            pltpu.VMEM((2, hid, feat), BF16),
            pltpu.VMEM((2, nxs, ny, pr, hid), F32),
            pltpu.VMEM((2, chunks, ny - 1, per, pr, hid), BF16),
            pltpu.VMEM((2, chunks, ny - 1, per, pr, hid), BF16),
            pltpu.VMEM((2, nxs, ny, pr, hid), BF16),
            pltpu.VMEM((2, nxs, ny, pr, hid), BF16),
            pltpu.VMEM((nxs, 2, nz, rows, feat), F32),
            pltpu.VMEM((nxs, 2, nz, rows, feat), BF16),
            pltpu.VMEM((nx, nz, rows, low), BF16),
            pltpu.VMEM((nz, rows, low), F32),
            pltpu.VMEM((2, rows, low), F32),
            pltpu.VMEM((nz - 1, rows, low), F32),
            pltpu.VMEM((chunks, 2, per, 2, rows, high), BF16),
            pltpu.VMEM((chunks, nz - 1, per, 2, rows, high), BF16),
            pltpu.VMEM((nxs, 2, rows, high), F32),
            pltpu.VMEM((nx, rows, high), F32),
            pltpu.SemaphoreType.DMA((N_SEMS,)),
            pltpu.SemaphoreType.DMA((N_SEMS,)),
            pltpu.SemaphoreType.DMA((64,)),
            pltpu.SemaphoreType.DMA((6,)),
        ],
        compiler_params=pltpu.CompilerParams(
            collective_id=0, has_side_effects=True, vmem_limit_bytes=LIMIT
        ),
    )(tokens, weight_in, bias_in, weight_out, out_grad)
    return pl.pallas_call(
        copy_out,
        out_shape=tuple(jax.ShapeDtypeStruct(v.shape, v.dtype) for v in out),
        in_specs=[vmem] * 4,
        out_specs=(anywhere,) * 4,
        scratch_shapes=[pltpu.SemaphoreType.DMA((4,))],
        compiler_params=pltpu.CompilerParams(vmem_limit_bytes=1024 * 1024),
    )(*(pltpu.with_memory_space_constraint(v, pltpu.VMEM) for v in out))


def solution(mesh):
    nz, ny = mesh.shape["row"] // X, mesh.shape["col"] // 2
    in_specs = (P("row", "col"), P("col", "row"), P("row"), P("row", "col"), P("row", "col"))
    out_specs = (P("row", "col"), P("col", "row"), P("row", "col"), P("row"))
    return jax.shard_map(
        functools.partial(body, nz, ny),
        mesh=mesh,
        in_specs=in_specs,
        out_specs=out_specs,
        check_vma=False,
    )
```

```python
import functools

import jax
import jax.numpy as jnp
from jax import lax
from jax.experimental import pallas as pl
from jax.experimental.pallas import tpu as pltpu
from jax.sharding import PartitionSpec as P

SQRT_HALF = 0.7071067811865476
INV_ROOT_TWO_PI = 0.3989422804014327
X = 4
N_SEMS = 192
CHUNKS = 2
LIMIT = 56 * 1024 * 1024
BF16, F32 = jnp.bfloat16, jnp.float32
MESH = pl.DeviceIdType.MESH


def gelu_value(preact):
    return preact * 0.5 * (1.0 + lax.erf(preact * SQRT_HALF))


def gelu_slope(preact):
    return 0.5 * (1.0 + lax.erf(preact * SQRT_HALF)) + preact * INV_ROOT_TWO_PI * jnp.exp(
        -0.5 * preact * preact
    )


def around(n):
    out = [0]
    for d in range(1, n // 2):
        out += [d, -d]
    return out + [n // 2]


def copy_out(*refs):
    copies = [pltpu.make_async_copy(refs[i], refs[4 + i], refs[8].at[i]) for i in (1, 2, 0, 3)]
    for copy in copies:
        copy.start()
    for copy in copies:
        copy.wait()


def kernel(
    nz,
    ny,
    chunks,
    tokens,
    weight_in,
    bias_in,
    weight_out,
    out_grad,
    grad_tokens,
    grad_weight_in,
    grad_weight_out,
    grad_bias,
    tok_half,
    og_half,
    tok_other,
    og_other,
    tok_t,
    stage,
    own_right,
    w_in,
    w_out,
    part,
    ring_out,
    ring_in,
    act_all,
    gp_all,
    g_full,
    g_send,
    lx_in,
    lz_sum,
    lz_out,
    lz_in,
    rz_out,
    rz_in,
    rx_sum,
    rx_in,
    send_sems,
    recv_sems,
    slot_sems,
    local_sems,
):
    nx = X
    nxs = nx // 2
    rows, feat = tokens.shape
    hid = w_in.shape[-1]
    cut = stage.shape[-1]
    rest = feat - cut
    pr = nz * rows // ny
    hz, hy = nz // 2, ny // 2
    per = nxs // chunks
    spans = [pl.ds(k * per, per) for k in range(chunks)]
    turns = range(chunks - 1, -1, -1)
    row, col = lax.axis_index("row"), lax.axis_index("col")
    z, x = lax.div(row, nx), lax.rem(row, nx)
    y, c = lax.div(col, 2), lax.rem(col, 2)
    first_core, second_core = c == 0, c == 1

    def yn(d):
        return lax.rem(y + (ny + d), ny)

    def to_z(d):
        return (lax.rem(z + (nz + d), nz) * nx + x, col)

    def to_x(j, core):
        return (z * nx + lax.rem(x + j, nx), y * 2 + core)

    def to_y(d):
        return (row, yn(d) * 2 + c)

    partner = (row, y * 2 + (1 - c))
    pending = []
    slot_ids = {}

    def slot_id(key, count):
        if key not in slot_ids:
            slot_ids[key] = sum(n for _, n in slot_ids.values()), count
        return slot_ids[key][0]

    def send(src, dst, device, recv_sem=None, only=None):
        i = len(pending)
        copy = pltpu.make_async_remote_copy(
            src_ref=src,
            dst_ref=dst,
            send_sem=send_sems.at[i],
            recv_sem=recv_sems.at[i] if recv_sem is None else recv_sem,
            device_id=device,
            device_id_type=MESH,
        )
        if only is None:
            copy.start()
        else:
            pl.when(only)(copy.start)
        pending.append((copy, only))
        return copy

    def landed(dst, sem, only=None):
        copy = pltpu.make_async_remote_copy(
            src_ref=dst,
            dst_ref=dst,
            send_sem=send_sems.at[0],
            recv_sem=sem,
            device_id=partner,
            device_id_type=MESH,
        )
        if only is None:
            copy.wait_recv()
        else:
            pl.when(only)(copy.wait_recv)

    def local(src, dst, i):
        copy = pltpu.make_async_copy(src, dst, local_sems.at[i])
        copy.start()
        return copy

    left, right = pl.ds(0, cut), pl.ds(cut, rest)
    low = lx_in.shape[-1]
    west, east = pl.ds(0, low), pl.ds(low, feat - low)
    slot = {d: i for i, d in enumerate(around(nz))}
    slot[-hz] = slot[hz]
    near = 2 * min(hz, 3) - 1
    batches = [pl.ds(0, near)] + [pl.ds(near, nz - near)] * (near < nz)

    def direct(h, side):
        out = []
        for d in (2, 1):
            if d < h:
                out += [d, -d]
            elif d == h:
                out.append(d * side)
        return out

    def relayed(h, side):
        return [(sgn, d) for sgn in (1, -1) for d in (3, 4) if d < h or (d == h and sgn == side)]

    sources = ((tokens, tok_half), (out_grad, og_half))
    sides = (1, -1)
    own = []
    for a, (src, _) in enumerate(sources):
        own.append(local(src.at[:, left], stage.at[a, 0], 2 * a))
        own.append(local(src.at[:, right], own_right.at[a], 2 * a + 1))
    load_in = local(weight_in, w_in.at[c], 4)
    load_out = local(weight_out, w_out.at[c], 5)

    barrier = pltpu.get_barrier_semaphore()
    friends = [to_x(j, core) for j in range(1, nx) for core in (0, 1)] + [partner]
    for d in (1, -1, 2, -2):
        friends += [to_z(d)] * (abs(d) <= hz) + [to_y(d)] * (abs(d) <= hy)
    for device in friends:
        pl.semaphore_signal(barrier, inc=1, device_id=device, device_id_type=MESH)
    pl.semaphore_wait(barrier, len(friends))
    for copy in own:
        copy.wait()

    lz, rz = {}, {}
    hops = sorted(range(1, nx), key=lambda j: -((nx - j) % nxs))

    def far_relay(kind):
        return nx == 4 and kind != "r"

    holders = ((second_core, first_core), (first_core, second_core))

    def relay_x(a, kind, zs):
        if not far_relay(kind):
            return
        buf = sources[a][1]
        holder = holders[a][0]
        for block in (0, 1):
            landed(buf.at[1, block, zs, :, left], x_sem(a, kind, 1, block), holder)
        send(
            buf.at[1, :, zs, :, left],
            buf.at[0, :, zs, :, left],
            to_x(1 if a == 0 else nx - 1, 1),
            slot_sems.at[slot_id((a, kind, "far"), 1)],
            holder,
        )

    def x_sem(a, kind, xs, block):
        return slot_sems.at[slot_id((a, kind, xs), 2) + block]

    def over_x(a, kind, src, dst):
        for j in hops + [0]:
            core, xs = divmod((nx - j) % nx, nxs)
            if far_relay(kind) and j == nx // 2:
                continue
            if j == 0:
                send(src, dst(0, 1), partner, x_sem(a, kind, 0, 1), second_core)
            else:
                send(src, dst(xs, c), to_x(j, core), x_sem(a, kind, xs, c))

    def from_x(a, kind, xs, dst):
        if far_relay(kind):
            if xs == 0:
                landed(dst(0, 1), x_sem(a, kind, 0, 1), first_core)
                landed(dst(0, slice(None)), slot_sems.at[slot_id((a, kind, "far"), 1)], second_core)
            else:
                for block in (0, 1):
                    landed(dst(xs, block), x_sem(a, kind, xs, block), holders[a][1])
            return
        for block in (0, 1):
            only = second_core if (xs, block) == (0, 0) else None
            landed(dst(xs, block), x_sem(a, kind, xs, block), only)

    def right_at(a):
        buf = sources[a][1]
        return lambda xs, block: buf.at[xs, block, 0, :, right]

    def left_at(a, zs):
        buf = sources[a][1]
        return lambda xs, block: buf.at[xs, block, zs, :, left]

    def right_block(a, k, s):
        return sources[a][1].at[spans[k], :, s, :, right]

    for a in (0, 1):
        over_x(a, "r", own_right.at[a], right_at(a))
        for d in direct(hz, sides[a]):
            lz[a, d] = send(stage.at[a, 0], stage.at[a, slot[-d]], to_z(d))

    @pl.when(first_core)
    def _():
        for a, (_, buf) in enumerate(sources):
            buf[0, 0, 0, :, right] = own_right[a]

    def right_start(k):
        for a in (0, 1):
            for xs in range(k * per, (k + 1) * per):
                from_x(a, "r", xs, right_at(a))
            for d in direct(hz, sides[a]):
                rz[a, k, d] = send(right_block(a, k, 0), right_block(a, k, slot[-d]), to_z(d))

    def right_relay(k):
        for a in (0, 1):
            for sgn, d in relayed(hz, sides[a]):
                if d == 3:
                    rz[a, k, 2 * sgn].wait_recv()
                rz[a, k, d * sgn] = send(
                    right_block(a, k, slot[-2 * sgn]),
                    right_block(a, k, slot[-d * sgn]),
                    to_z((d - 2) * sgn),
                )

    def left_relay(a):
        for sgn, d in relayed(hz, sides[a]):
            if d == 3:
                lz[a, 2 * sgn].wait_recv()
            lz[a, d * sgn] = send(
                stage.at[a, slot[-2 * sgn]], stage.at[a, slot[-d * sgn]], to_z((d - 2) * sgn)
            )
        for d in direct(hz, sides[a]):
            if not (hz > 2 and abs(d) == 2):
                lz[a, d].wait_recv()
        over_x(a, 0, stage.at[a, batches[0]], left_at(a, batches[0]))

    def left_rest(a):
        for sgn, d in relayed(hz, sides[a]):
            lz[a, d * sgn].wait_recv()
        if near < nz:
            over_x(a, 1, stage.at[a, batches[1]], left_at(a, batches[1]))

    right_start(turns[0])
    load_in.wait()
    send_in = send(w_in.at[c], w_in.at[c], partner)
    for a in (0, 1):
        left_relay(a)
    load_out.wait()
    send_out = send(w_out.at[c], w_out.at[c], partner)
    right_relay(turns[0])
    for k in turns[1:]:
        right_start(k)
    for a in (0, 1):
        left_rest(a)
        relay_x(a, 0, batches[0])

    @pl.when(first_core)
    def _():
        for a, (_, buf) in enumerate(sources):
            buf[0, 0, :, :, left] = stage[a]

    def gathered(a, k):
        for d in direct(hz, sides[a]):
            if not (hz > 2 and abs(d) == 2):
                rz[a, k, d].wait_recv()
        for sgn, d in relayed(hz, sides[a]):
            rz[a, k, d * sgn].wait_recv()
        for xs in range(k * per, (k + 1) * per):
            for i, zs in enumerate(batches):
                from_x(a, i, xs, left_at(a, zs))

    def tiles(extent, width=256):
        width = min(width, extent)

        def run(f):
            def step(i, carry):
                f(pl.ds(pl.multiple_of(i * width, width), width))
                return carry

            lax.fori_loop(0, extent // width, step, 0)

        return run

    def product(a, k):
        @tiles(hid)
        def _(span):
            total = 0
            for block in (0, 1):
                lhs = sources[a][1][spans[k], block].reshape(per * nz * rows, feat)
                if a == 0:
                    out = jnp.dot(lhs, w_in[block, :, span], preferred_element_type=F32)
                else:
                    out = lax.dot_general(
                        lhs, w_out[block, span, :], (((1,), (1,)), ((), ())), preferred_element_type=F32
                    )
                total = out if block == 0 else total + out
            part[a, spans[k], :, :, span] = total.reshape(per, ny, pr, span.size)

    ring = {}

    def ring_send(a, k, o, value, d):
        i = len([key for key in ring if key[:2] == (a, k)])
        ring_out[a, k, i] = value.astype(BF16)
        ring[a, k, o] = (send(ring_out.at[a, k, i], ring_in.at[a, k, i], to_y(d)), i)

    def ring_got(a, k, o):
        copy, i = ring[a, k, o]
        copy.wait_recv()
        return ring_in[a, k, i].astype(F32)

    def ring_first(a, k):
        for sgn, d in relayed(hy, sides[a]):
            ring_send(a, k, d * sgn, part[a, spans[k], yn(d * sgn)], (d - 2) * sgn)
        for d in direct(hy, sides[a]):
            if abs(d) == 1:
                ring_send(a, k, d, part[a, spans[k], yn(d)], d)

    def ring_second(a, k):
        for d in direct(hy, sides[a]):
            if abs(d) == 2:
                value = part[a, spans[k], yn(d)]
                for sgn, far in relayed(hy, sides[a]):
                    if sgn * d > 0:
                        value = value + ring_got(a, k, far * sgn)
                ring_send(a, k, d, value, d)

    def ring_end(a, k):
        value = part[a, spans[k], y]
        for d in reversed(direct(hy, sides[a])):
            value = value + ring_got(a, k, d)
        return value

    flushed = [0]

    def flush():
        for copy, only in pending[flushed[0] :]:
            if only is None:
                copy.wait_send()
            else:
                pl.when(only)(copy.wait_send)
        flushed[0] = len(pending)

    def multiply(k):
        for a in (0, 1):
            gathered(a, k)
            if k == turns[0]:
                (send_in, send_out)[a].wait_recv()
            product(a, k)
            ring_first(a, k)

    spread = {}

    def spread_first(buf, a, k):
        for d in direct(hy, sides[a]):
            block = buf.at[c, spans[k], y]
            spread[a, k, d] = send(block, block, to_y(d))

    def spread_second(buf, a, k):
        for d in direct(hy, sides[a]):
            spread[a, k, d].wait_recv()
            block = buf.at[c, spans[k], yn(-d)]
            for sgn, far in relayed(hy, sides[a]):
                if d == 2 * sgn:
                    spread[a, k, far * sgn] = send(block, block, to_y((far - 2) * sgn))

    def spread_end(a, k):
        for sgn, far in relayed(hy, sides[a]):
            spread[a, k, far * sgn].wait_recv()

    def pointwise(k):
        preact = ring_end(0, k) + bias_in[...][None, None, :]
        act_all[c, spans[k], y] = gelu_value(preact).astype(BF16)
        slope = gelu_slope(preact)
        gp_all[c, spans[k], y] = (ring_end(1, k) * slope).astype(BF16)
        spread_first(gp_all, 1, k)

    def row_terms(k, start, extent):
        def step(i, carry):
            block = lax.rem(i, 2)
            span = pl.ds(pl.multiple_of(start + lax.div(i, 2) * low, low), low)
            grads = gp_all[c, spans[k]].reshape(per * nz * rows, hid)
            out = lax.dot_general(
                grads, w_in[block, span, :], (((1,), (1,)), ((), ())), preferred_element_type=F32
            ).reshape(per, nz, rows, low)
            g_full[spans[k], block, :, :, span] = out
            g_send[spans[k], block, :, :, span] = out.astype(BF16)
            return carry

        lax.fori_loop(0, 2 * (extent // low), step, 0)

    tl, tr = {}, {}

    def home(kind, k, src, dst):
        for xs in range(k * per, (k + 1) * per):
            s = c * nxs + xs
            for block in (0, 1):
                sem = slot_sems.at[slot_id(kind, nx) + s]
                only = second_core if (xs, block) == (0, 0) else None
                send(src(xs, block), dst.at[s], to_x(s, block), sem, only)

    def at_home(kind, dst):
        for s in range(nx):
            sem = slot_sems.at[slot_id(kind, nx) + s]
            landed(dst.at[s], sem, second_core if s == 0 else None)

    def right_put(k, o, src, d):
        i = len([key for key in tr if key[0] == k])
        tr[k, o] = (send(src, rz_in.at[k, i], to_z(d)), i)

    def right_got(k, o):
        copy, i = tr[k, o]
        copy.wait_recv()
        return rz_in[k, i].astype(F32)

    def right_first(k):
        for sgn, d in relayed(hz, 1):
            o = d * sgn
            right_put(k, o, g_send.at[spans[k], :, slot[o], :, east], (d - 2) * sgn)
        for o in direct(hz, 1):
            if abs(o) == 1:
                right_put(k, o, g_send.at[spans[k], :, slot[o], :, east], o)

    def right_second(k):
        for i, o in enumerate(d for d in direct(hz, 1) if abs(d) == 2):
            value = g_full[spans[k], :, slot[o], :, east]
            for sgn, d in relayed(hz, 1):
                if sgn * o > 0:
                    value = value + right_got(k, d * sgn)
            rz_out[k, i] = value.astype(BF16)
            right_put(k, o, rz_out.at[k, i], o)

    def right_end(k):
        value = g_full[spans[k], :, 0, :, east]
        for o in reversed(direct(hz, 1)):
            value = value + right_got(k, o)
        rx_sum[spans[k]] = value
        home("right", k, lambda xs, block: rx_sum.at[xs, block], rx_in)

    def left_put(o, src, d):
        tl[o] = (send(src, lz_in.at[len(tl)], to_z(d)), len(tl))

    def left_got(o):
        copy, i = tl[o]
        copy.wait_recv()
        return lz_in[i]

    def left_first():
        at_home("left", lx_in)

        @pl.when(first_core)
        def _():
            lx_in[0] = g_send[0, 0, :, :, west]

        value = lx_in[0].astype(F32)
        for s in range(1, nx):
            value = value + lx_in[s].astype(F32)
        lz_sum[...] = value
        for sgn, d in relayed(hz, -1):
            left_put(d * sgn, lz_sum.at[slot[d * sgn]], (d - 2) * sgn)
        for o in direct(hz, -1):
            if abs(o) == 1:
                left_put(o, lz_sum.at[slot[o]], o)

    def left_second():
        for i, o in enumerate(d for d in direct(hz, -1) if abs(d) == 2):
            value = lz_sum[slot[o]]
            for sgn, d in relayed(hz, -1):
                if sgn * o > 0:
                    value = value + left_got(d * sgn)
            lz_out[i] = value
            left_put(o, lz_out.at[i], o)

    def left_end():
        value = lz_sum[0]
        for o in reversed(direct(hz, -1)):
            value = value + left_got(o)
        grad_tokens[:, west] = value.astype(BF16)

    half = nxs * nz * rows

    def weight_in_grad(i, n):
        step = feat // n
        rows_out = pl.ds(i * step, step)

        @tiles(hid)
        def _(span):
            out = jnp.dot(
                tok_t[0, rows_out],
                gp_all[c, :, :, :, span].reshape(half, span.size),
                preferred_element_type=F32,
            ) + jnp.dot(
                tok_t[1, rows_out],
                gp_all[1 - c, :, :, :, span].reshape(half, span.size),
                preferred_element_type=F32,
            )
            grad_weight_in[rows_out, span] = out.astype(BF16)

    def weight_out_grad():
        @tiles(hid)
        def _(span):
            out = lax.dot_general(
                act_all[c, :, :, :, span].reshape(half, span.size),
                og_half[:, c].reshape(half, feat),
                (((0,), (0,)), ((), ())),
                preferred_element_type=F32,
            ) + lax.dot_general(
                act_all[1 - c, :, :, :, span].reshape(half, span.size),
                og_other[...].reshape(half, feat),
                (((0,), (0,)), ((), ())),
                preferred_element_type=F32,
            )
            grad_weight_out[span, :] = out.astype(BF16)

    def turn(i, src):
        @tiles(feat)
        def _(span):
            tok_t[i, span, :] = src(span).reshape(half, span.size).T

    shared = []

    def row_start(k):
        spread_end(1, k)
        row_terms(k, low, feat - low)
        right_first(k)
        row_terms(k, 0, low)
        home("left", k, lambda xs, block: g_send.at[xs, block, :, :, west], lx_in)
        block = gp_all.at[c, spans[k]]
        shared.append(send(block, block, partner))

    def share_act(k):
        spread_end(0, k)
        block = act_all.at[c, spans[k]]
        shared.append(send(block, block, partner))

    def all_shared():
        for copy in shared:
            copy.wait_recv()
        shared.clear()

    one, rest_turns = turns[0], list(turns[1:])
    for a in (0, 1):
        if near < nz:
            relay_x(a, 1, batches[1])
    multiply(one)
    for k in rest_turns:
        right_relay(k)
    ring_second(0, one)
    ring_second(1, one)
    for k in rest_turns:
        multiply(k)
    pointwise(one)
    for a, other in enumerate((tok_other, og_other)):
        shared.append(send(sources[a][1].at[:, 1 - c], other, partner))
    for k in rest_turns:
        ring_second(0, k)
        ring_second(1, k)
    spread_second(gp_all, 1, one)
    turn(0, lambda span: tok_half[:, c, :, :, span])
    for k in rest_turns:
        pointwise(k)
    row_start(one)
    for k in rest_turns:
        spread_second(gp_all, 1, k)
    for k in turns:
        spread_first(act_all, 0, k)
    shared[0].wait_recv()
    turn(1, lambda span: tok_other[:, :, :, span])
    right_second(one)
    for k in rest_turns:
        row_start(k)
    for k in turns:
        spread_second(act_all, 0, k)
    flush()
    for copy in shared[1:]:
        copy.wait_recv()
    shared.clear()
    weight_in_grad(0, 3)
    for k in rest_turns:
        right_second(k)
    left_first()
    for k in turns:
        share_act(k)
    weight_in_grad(1, 3)
    weight_in_grad(2, 3)
    for k in turns:
        right_end(k)
    left_second()
    grad_bias[...] = jnp.sum(gp_all[...].astype(F32).reshape(2 * half, hid), axis=0)
    all_shared()
    weight_out_grad()
    left_end()
    at_home("right", rx_in)

    @pl.when(first_core)
    def _():
        rx_in[0] = rx_sum[0, 0]

    value = rx_in[0]
    for s in range(1, nx):
        value = value + rx_in[s]
    grad_tokens[:, east] = value.astype(BF16)
    flush()


def body(nz, ny, tokens, weight_in, bias_in, weight_out, out_grad):
    rows, feat = tokens.shape
    hid = weight_in.shape[1]
    cut = feat // 3 * 2
    rest = feat - cut
    low = feat // 3
    high = feat - low
    nx = X
    nxs = nx // 2
    chunks = min(CHUNKS, nxs)
    per = nxs // chunks
    pr = nz * rows // ny
    vmem, anywhere = pl.BlockSpec(memory_space=pltpu.VMEM), pl.BlockSpec(memory_space=pl.ANY)
    out = pl.pallas_call(
        functools.partial(kernel, nz, ny, chunks),
        out_shape=(
            pltpu.VMEM((rows, feat), BF16),
            pltpu.VMEM((feat, hid), BF16),
            pltpu.VMEM((hid, feat), BF16),
            pltpu.VMEM((hid,), F32),
        ),
        in_specs=[anywhere, anywhere, vmem, anywhere, anywhere],
        out_specs=(vmem, vmem, vmem, vmem),
        scratch_shapes=[
            pltpu.VMEM((nxs, 2, nz, rows, feat), BF16),
            pltpu.VMEM((nxs, 2, nz, rows, feat), BF16),
            pltpu.VMEM((nxs, nz, rows, feat), BF16),
            pltpu.VMEM((nxs, nz, rows, feat), BF16),
            pltpu.VMEM((2, feat, nxs * nz * rows), BF16),
            pltpu.VMEM((2, nz, rows, cut), BF16),
            pltpu.VMEM((2, rows, rest), BF16),
            pltpu.VMEM((2, feat, hid), BF16),
            pltpu.VMEM((2, hid, feat), BF16),
            pltpu.VMEM((2, nxs, ny, pr, hid), F32),
            pltpu.VMEM((2, chunks, ny - 1, per, pr, hid), BF16),
            pltpu.VMEM((2, chunks, ny - 1, per, pr, hid), BF16),
            pltpu.VMEM((2, nxs, ny, pr, hid), BF16),
            pltpu.VMEM((2, nxs, ny, pr, hid), BF16),
            pltpu.VMEM((nxs, 2, nz, rows, feat), F32),
            pltpu.VMEM((nxs, 2, nz, rows, feat), BF16),
            pltpu.VMEM((nx, nz, rows, low), BF16),
            pltpu.VMEM((nz, rows, low), F32),
            pltpu.VMEM((2, rows, low), F32),
            pltpu.VMEM((nz - 1, rows, low), F32),
            pltpu.VMEM((chunks, 2, per, 2, rows, high), BF16),
            pltpu.VMEM((chunks, nz - 1, per, 2, rows, high), BF16),
            pltpu.VMEM((nxs, 2, rows, high), F32),
            pltpu.VMEM((nx, rows, high), F32),
            pltpu.SemaphoreType.DMA((N_SEMS,)),
            pltpu.SemaphoreType.DMA((N_SEMS,)),
            pltpu.SemaphoreType.DMA((64,)),
            pltpu.SemaphoreType.DMA((6,)),
        ],
        compiler_params=pltpu.CompilerParams(
            collective_id=0, has_side_effects=True, vmem_limit_bytes=LIMIT
        ),
    )(tokens, weight_in, bias_in, weight_out, out_grad)
    return pl.pallas_call(
        copy_out,
        out_shape=tuple(jax.ShapeDtypeStruct(v.shape, v.dtype) for v in out),
        in_specs=[vmem] * 4,
        out_specs=(anywhere,) * 4,
        scratch_shapes=[pltpu.SemaphoreType.DMA((4,))],
        compiler_params=pltpu.CompilerParams(vmem_limit_bytes=1024 * 1024),
    )(*(pltpu.with_memory_space_constraint(v, pltpu.VMEM) for v in out))


def solution(mesh):
    nz, ny = mesh.shape["row"] // X, mesh.shape["col"] // 2
    in_specs = (P("row", "col"), P("col", "row"), P("row"), P("row", "col"), P("row", "col"))
    out_specs = (P("row", "col"), P("col", "row"), P("row", "col"), P("row"))
    return jax.shard_map(
        functools.partial(body, nz, ny),
        mesh=mesh,
        in_specs=in_specs,
        out_specs=out_specs,
        check_vma=False,
    )
```

```python
import functools

import jax
import jax.numpy as jnp
from jax import lax
from jax.experimental import pallas as pl
from jax.experimental.pallas import tpu as pltpu
from jax.sharding import PartitionSpec as P

SQRT_HALF = 0.7071067811865476
INV_ROOT_TWO_PI = 0.3989422804014327
X = 4
N_SEMS = 192
CHUNKS = 2
LIMIT = 56 * 1024 * 1024
BF16, F32 = jnp.bfloat16, jnp.float32
MESH = pl.DeviceIdType.MESH


def gelu_value(preact):
    return preact * 0.5 * (1.0 + lax.erf(preact * SQRT_HALF))


def gelu_slope(preact):
    return 0.5 * (1.0 + lax.erf(preact * SQRT_HALF)) + preact * INV_ROOT_TWO_PI * jnp.exp(
        -0.5 * preact * preact
    )


def around(n):
    out = [0]
    for d in range(1, n // 2):
        out += [d, -d]
    return out + [n // 2]


def copy_out(*refs):
    copies = [pltpu.make_async_copy(refs[i], refs[4 + i], refs[8].at[i]) for i in (1, 2, 0, 3)]
    for copy in copies:
        copy.start()
    for copy in copies:
        copy.wait()


def kernel(
    nz,
    ny,
    chunks,
    tokens,
    weight_in,
    bias_in,
    weight_out,
    out_grad,
    grad_tokens,
    grad_weight_in,
    grad_weight_out,
    grad_bias,
    both,
    tok_other,
    og_other,
    stage,
    own_right,
    w_in,
    w_out,
    part,
    ring_out,
    ring_in,
    act_all,
    gp_all,
    g_full,
    g_send,
    lx_in,
    lz_sum,
    lz_out,
    lz_in,
    rz_out,
    rz_in,
    rx_sum,
    rx_in,
    send_sems,
    recv_sems,
    slot_sems,
    local_sems,
):
    nx = X
    nxs = nx // 2
    rows, feat = tokens.shape
    hid = w_in.shape[-1]
    cut = stage.shape[-1]
    rest = feat - cut
    pr = nz * rows // ny
    hz, hy = nz // 2, ny // 2
    per = nxs // chunks
    spans = [pl.ds(k * per, per) for k in range(chunks)]
    turns = range(chunks - 1, -1, -1)
    row, col = lax.axis_index("row"), lax.axis_index("col")
    z, x = lax.div(row, nx), lax.rem(row, nx)
    y, c = lax.div(col, 2), lax.rem(col, 2)
    first_core, second_core = c == 0, c == 1

    def yn(d):
        return lax.rem(y + (ny + d), ny)

    def to_z(d):
        return (lax.rem(z + (nz + d), nz) * nx + x, col)

    def to_x(j, core):
        return (z * nx + lax.rem(x + j, nx), y * 2 + core)

    def to_y(d):
        return (row, yn(d) * 2 + c)

    partner = (row, y * 2 + (1 - c))
    pending = []
    slot_ids = {}

    def slot_id(key, count):
        if key not in slot_ids:
            slot_ids[key] = sum(n for _, n in slot_ids.values()), count
        return slot_ids[key][0]

    def send(src, dst, device, recv_sem=None, only=None):
        i = len(pending)
        copy = pltpu.make_async_remote_copy(
            src_ref=src,
            dst_ref=dst,
            send_sem=send_sems.at[i],
            recv_sem=recv_sems.at[i] if recv_sem is None else recv_sem,
            device_id=device,
            device_id_type=MESH,
        )
        if only is None:
            copy.start()
        else:
            pl.when(only)(copy.start)
        pending.append((copy, only))
        return copy

    def landed(dst, sem, only=None):
        copy = pltpu.make_async_remote_copy(
            src_ref=dst,
            dst_ref=dst,
            send_sem=send_sems.at[0],
            recv_sem=sem,
            device_id=partner,
            device_id_type=MESH,
        )
        if only is None:
            copy.wait_recv()
        else:
            pl.when(only)(copy.wait_recv)

    def local(src, dst, i):
        copy = pltpu.make_async_copy(src, dst, local_sems.at[i])
        copy.start()
        return copy

    left, right = pl.ds(0, cut), pl.ds(cut, rest)
    slot = {d: i for i, d in enumerate(around(nz))}
    slot[-hz] = slot[hz]
    near = 2 * min(hz, 3) - 1
    batches = [pl.ds(0, near)] + [pl.ds(near, nz - near)] * (near < nz)

    def direct(h, side):
        out = []
        for d in (2, 1):
            if d < h:
                out += [d, -d]
            elif d == h:
                out.append(d * side)
        return out

    def relayed(h, side):
        return [(sgn, d) for sgn in (1, -1) for d in (3, 4) if d < h or (d == h and sgn == side)]

    tok_half, og_half = both.at[0], both.at[1]
    sources = ((tokens, tok_half), (out_grad, og_half))
    sides = (1, -1)
    own = []
    for a, (src, _) in enumerate(sources):
        own.append(local(src.at[:, left], stage.at[a, 0], 2 * a))
        own.append(local(src.at[:, right], own_right.at[a], 2 * a + 1))
    load_in = local(weight_in, w_in.at[c], 4)
    load_out = local(weight_out, w_out.at[c], 5)

    barrier = pltpu.get_barrier_semaphore()
    friends = [to_x(j, core) for j in range(1, nx) for core in (0, 1)] + [partner]
    for d in (1, -1, 2, -2):
        friends += [to_z(d)] * (abs(d) <= hz) + [to_y(d)] * (abs(d) <= hy)
    for device in friends:
        pl.semaphore_signal(barrier, inc=1, device_id=device, device_id_type=MESH)
    pl.semaphore_wait(barrier, len(friends))
    for copy in own:
        copy.wait()

    lz, rz = {}, {}
    hops = sorted(range(1, nx), key=lambda j: -((nx - j) % nxs))

    def far_relay(kind):
        return nx == 4 and kind != "r"

    def x_sem(kind, xs, block):
        return slot_sems.at[slot_id((kind, xs), 2) + block]

    def over_x(kind, src, dst):
        for j in hops + [0]:
            core, xs = divmod((nx - j) % nx, nxs)
            if far_relay(kind) and j == nx // 2:
                continue
            if j == 0:
                send(src, dst(0, 1), partner, x_sem(kind, 0, 1), second_core)
            else:
                send(src, dst(xs, c), to_x(j, core), x_sem(kind, xs, c))

    def from_x(kind, xs, dst):
        for block in (0, 1):
            only = second_core if (xs, block) == (0, 0) else None
            landed(dst(xs, block), x_sem(kind, xs, block), only)

    def left_at(zs):
        return lambda xs, block: both.at[:, xs, block, zs, :, left]

    def right_at(xs, block):
        return both.at[:, xs, block, 0, :, right]

    def relay_x(kind, zs):
        if not far_relay(kind):
            return
        for block in (0, 1):
            landed(left_at(zs)(1, block), x_sem(kind, 1, block))
        a = 1 - c
        send(
            both.at[a, 1, :, zs, :, left],
            both.at[a, 0, :, zs, :, left],
            to_x(c + (nx - 1) * (1 - c), 1),
            slot_sems.at[slot_id((kind, "far"), 2) + a],
        )

    def from_x_left(kind, zs, xs):
        if not far_relay(kind):
            from_x(kind, xs, left_at(zs))
        elif xs == 0:
            landed(left_at(zs)(0, 1), x_sem(kind, 0, 1), first_core)
            for a in (0, 1):
                sem = slot_sems.at[slot_id((kind, "far"), 2) + a]
                landed(both.at[a, 0, :, zs, :, left], sem, second_core)

    far_side = [(sgn, hz, a) for a, sgn in enumerate(sides)] if hz > 2 else []
    relays = [(1, 3, None), (-1, 3, None)] * (hz > 3) + far_side

    def right_block(k, s, a=None):
        return both.at[slice(None) if a is None else a, spans[k], :, s, :, right]

    def stage_block(s, a=None):
        return stage.at[slice(None) if a is None else a, s]

    over_x("r", own_right, right_at)
    for d in direct(hz, 1):
        lz[d] = send(stage_block(0), stage_block(slot[-d]), to_z(d))

    @pl.when(first_core)
    def _():
        for a, (_, buf) in enumerate(sources):
            buf[0, 0, 0, :, right] = own_right[a]

    def right_start(k):
        for xs in range(k * per, (k + 1) * per):
            from_x("r", xs, right_at)
        for d in direct(hz, 1):
            rz[k, d] = send(right_block(k, 0), right_block(k, slot[-d]), to_z(d))

    def right_relay(k):
        for sgn, d, a in relays:
            if d == 3:
                rz[k, 2 * sgn].wait_recv()
            rz[k, d * sgn, a] = send(
                right_block(k, slot[-2 * sgn], a), right_block(k, slot[-d * sgn], a), to_z((d - 2) * sgn)
            )

    def left_relay():
        for sgn, d, a in relays:
            if d == 3:
                lz[2 * sgn].wait_recv()
            lz[d * sgn, a] = send(
                stage_block(slot[-2 * sgn], a), stage_block(slot[-d * sgn], a), to_z((d - 2) * sgn)
            )
        for d in direct(hz, 1):
            if not (hz > 2 and abs(d) == 2):
                lz[d].wait_recv()
        over_x(0, stage.at[:, batches[0]], left_at(batches[0]))

    def left_rest():
        for sgn, d, a in relays:
            lz[d * sgn, a].wait_recv()
        if near < nz:
            over_x(1, stage.at[:, batches[1]], left_at(batches[1]))

    right_start(turns[0])
    load_in.wait()
    send_in = send(w_in.at[c], w_in.at[c], partner)
    left_relay()
    load_out.wait()
    send_out = send(w_out.at[c], w_out.at[c], partner)
    right_relay(turns[0])
    for k in turns[1:]:
        right_start(k)
    left_rest()
    relay_x(0, batches[0])

    @pl.when(first_core)
    def _():
        for a, (_, buf) in enumerate(sources):
            buf[0, 0, :, :, left] = stage[a]

    def gathered(k):
        for d in direct(hz, 1):
            if not (hz > 2 and abs(d) == 2):
                rz[k, d].wait_recv()
        for sgn, d, a in relays:
            rz[k, d * sgn, a].wait_recv()
        for xs in range(k * per, (k + 1) * per):
            for i, zs in enumerate(batches):
                from_x_left(i, zs, xs)

    def product(a, k):
        total = 0
        for block in (0, 1):
            lhs = sources[a][1][spans[k], block].reshape(per * nz * rows, feat)
            if a == 0:
                out = jnp.dot(lhs, w_in[block], preferred_element_type=F32)
            else:
                out = lax.dot_general(
                    lhs, w_out[block], (((1,), (1,)), ((), ())), preferred_element_type=F32
                )
            total = out if block == 0 else total + out
        part[a, spans[k]] = total.reshape(per, ny, pr, hid)

    ring = {}

    def ring_send(a, k, o, value, d):
        i = len([key for key in ring if key[:2] == (a, k)])
        ring_out[a, k, i] = value.astype(BF16)
        ring[a, k, o] = (send(ring_out.at[a, k, i], ring_in.at[a, k, i], to_y(d)), i)

    def ring_got(a, k, o):
        copy, i = ring[a, k, o]
        copy.wait_recv()
        return ring_in[a, k, i].astype(F32)

    def ring_first(a, k):
        for sgn, d in relayed(hy, sides[a]):
            ring_send(a, k, d * sgn, part[a, spans[k], yn(d * sgn)], (d - 2) * sgn)
        for d in direct(hy, sides[a]):
            if abs(d) == 1:
                ring_send(a, k, d, part[a, spans[k], yn(d)], d)

    def ring_second(a, k):
        for d in direct(hy, sides[a]):
            if abs(d) == 2:
                value = part[a, spans[k], yn(d)]
                for sgn, far in relayed(hy, sides[a]):
                    if sgn * d > 0:
                        value = value + ring_got(a, k, far * sgn)
                ring_send(a, k, d, value, d)

    def ring_end(a, k):
        value = part[a, spans[k], y]
        for d in reversed(direct(hy, sides[a])):
            value = value + ring_got(a, k, d)
        return value

    flushed = [0]

    def flush():
        for copy, only in pending[flushed[0] :]:
            if only is None:
                copy.wait_send()
            else:
                pl.when(only)(copy.wait_send)
        flushed[0] = len(pending)

    def multiply(k):
        gathered(k)
        for a in (0, 1):
            if k == turns[0]:
                (send_in, send_out)[a].wait_recv()
            product(a, k)
            ring_first(a, k)

    spread = {}

    def spread_first(buf, a, k):
        for d in direct(hy, sides[a]):
            block = buf.at[c, spans[k], y]
            spread[a, k, d] = send(block, block, to_y(d))

    def spread_second(buf, a, k):
        for d in direct(hy, sides[a]):
            spread[a, k, d].wait_recv()
            block = buf.at[c, spans[k], yn(-d)]
            for sgn, far in relayed(hy, sides[a]):
                if d == 2 * sgn:
                    spread[a, k, far * sgn] = send(block, block, to_y((far - 2) * sgn))

    def spread_end(a, k):
        for sgn, far in relayed(hy, sides[a]):
            spread[a, k, far * sgn].wait_recv()

    def pointwise(k):
        preact = ring_end(0, k) + bias_in[...][None, None, :]
        act_all[c, spans[k], y] = gelu_value(preact).astype(BF16)
        slope = gelu_slope(preact)
        gp_all[c, spans[k], y] = (ring_end(1, k) * slope).astype(BF16)
        spread_first(gp_all, 1, k)

    def row_terms(k, span):
        grads = gp_all[c, spans[k]].reshape(per * nz * rows, hid)
        for block in (0, 1):
            out = lax.dot_general(
                grads, w_in[block, span, :], (((1,), (1,)), ((), ())), preferred_element_type=F32
            ).reshape(per, nz, rows, span.size)
            g_full[spans[k], block, :, :, span] = out
            g_send[spans[k], block, :, :, span] = out.astype(BF16)

    tl, tr = {}, {}

    def home(kind, k, src, dst):
        for xs in range(k * per, (k + 1) * per):
            s = c * nxs + xs
            for block in (0, 1):
                sem = slot_sems.at[slot_id(kind, nx) + s]
                only = second_core if (xs, block) == (0, 0) else None
                send(src(xs, block), dst.at[s], to_x(s, block), sem, only)

    def at_home(kind, dst):
        for s in range(nx):
            sem = slot_sems.at[slot_id(kind, nx) + s]
            landed(dst.at[s], sem, second_core if s == 0 else None)

    def right_put(k, o, src, d):
        i = len([key for key in tr if key[0] == k])
        tr[k, o] = (send(src, rz_in.at[k, i], to_z(d)), i)

    def right_got(k, o):
        copy, i = tr[k, o]
        copy.wait_recv()
        return rz_in[k, i].astype(F32)

    def right_first(k):
        for sgn, d in relayed(hz, 1):
            o = d * sgn
            right_put(k, o, g_send.at[spans[k], :, slot[o], :, right], (d - 2) * sgn)
        for o in direct(hz, 1):
            if abs(o) == 1:
                right_put(k, o, g_send.at[spans[k], :, slot[o], :, right], o)

    def right_second(k):
        for i, o in enumerate(d for d in direct(hz, 1) if abs(d) == 2):
            value = g_full[spans[k], :, slot[o], :, right]
            for sgn, d in relayed(hz, 1):
                if sgn * o > 0:
                    value = value + right_got(k, d * sgn)
            rz_out[k, i] = value.astype(BF16)
            right_put(k, o, rz_out.at[k, i], o)

    def right_end(k):
        value = g_full[spans[k], :, 0, :, right]
        for o in reversed(direct(hz, 1)):
            value = value + right_got(k, o)
        rx_sum[spans[k]] = value
        home("right", k, lambda xs, block: rx_sum.at[xs, block], rx_in)

    def left_put(o, src, d):
        tl[o] = (send(src, lz_in.at[len(tl)], to_z(d)), len(tl))

    def left_got(o):
        copy, i = tl[o]
        copy.wait_recv()
        return lz_in[i]

    def left_first():
        at_home("left", lx_in)

        @pl.when(first_core)
        def _():
            lx_in[0] = g_send[0, 0, :, :, left]

        value = lx_in[0].astype(F32)
        for s in range(1, nx):
            value = value + lx_in[s].astype(F32)
        lz_sum[...] = value
        for sgn, d in relayed(hz, -1):
            left_put(d * sgn, lz_sum.at[slot[d * sgn]], (d - 2) * sgn)
        for o in direct(hz, -1):
            if abs(o) == 1:
                left_put(o, lz_sum.at[slot[o]], o)

    def left_second():
        for i, o in enumerate(d for d in direct(hz, -1) if abs(d) == 2):
            value = lz_sum[slot[o]]
            for sgn, d in relayed(hz, -1):
                if sgn * o > 0:
                    value = value + left_got(d * sgn)
            lz_out[i] = value
            left_put(o, lz_out.at[i], o)

    def left_end():
        value = lz_sum[0]
        for o in reversed(direct(hz, -1)):
            value = value + left_got(o)
        grad_tokens[:, left] = value.astype(BF16)

    half = nxs * nz * rows

    def weight_in_grad(i, n):
        step = feat // n
        span = pl.ds(i * step, step)
        out = lax.dot_general(
            tok_half[:, c, :, :, span].reshape(half, step),
            gp_all[c].reshape(half, hid),
            (((0,), (0,)), ((), ())),
            preferred_element_type=F32,
        ) + lax.dot_general(
            tok_other[:, :, :, span].reshape(half, step),
            gp_all[1 - c].reshape(half, hid),
            (((0,), (0,)), ((), ())),
            preferred_element_type=F32,
        )
        grad_weight_in[span, :] = out.astype(BF16)

    def weight_out_grad(i, n):
        step = hid // n
        span = pl.ds(i * step, step)
        out = lax.dot_general(
            act_all[c, :, :, :, span].reshape(half, step),
            og_half[:, c].reshape(half, feat),
            (((0,), (0,)), ((), ())),
            preferred_element_type=F32,
        ) + lax.dot_general(
            act_all[1 - c, :, :, :, span].reshape(half, step),
            og_other[...].reshape(half, feat),
            (((0,), (0,)), ((), ())),
            preferred_element_type=F32,
        )
        grad_weight_out[span, :] = out.astype(BF16)

    shared = []

    def row_start(k):
        spread_end(1, k)
        row_terms(k, right)
        right_first(k)
        row_terms(k, left)
        home("left", k, lambda xs, block: g_send.at[xs, block, :, :, left], lx_in)
        block = gp_all.at[c, spans[k]]
        shared.append(send(block, block, partner))

    def share_act(k):
        spread_end(0, k)
        block = act_all.at[c, spans[k]]
        shared.append(send(block, block, partner))

    one, rest_turns = turns[0], list(turns[1:])
    if near < nz:
        relay_x(1, batches[1])
    multiply(one)
    for k in rest_turns:
        right_relay(k)
    ring_second(0, one)
    ring_second(1, one)
    for k in rest_turns:
        multiply(k)
    pointwise(one)
    for a, other in enumerate((tok_other, og_other)):
        shared.append(send(sources[a][1].at[:, 1 - c], other, partner))
    for k in rest_turns:
        ring_second(0, k)
        ring_second(1, k)
    spread_second(gp_all, 1, one)
    for k in rest_turns:
        pointwise(k)
    row_start(one)
    for k in rest_turns:
        spread_second(gp_all, 1, k)
    for k in turns:
        spread_first(act_all, 0, k)
    flush()
    right_second(one)
    for k in rest_turns:
        row_start(k)
    for k in turns:
        spread_second(act_all, 0, k)
    for copy in shared:
        copy.wait_recv()
    shared.clear()
    weight_in_grad(0, 3)
    for k in rest_turns:
        right_second(k)
    left_first()
    weight_in_grad(1, 3)
    for k in turns:
        right_end(k)
    left_second()
    for k in turns:
        share_act(k)
    weight_in_grad(2, 3)
    grad_bias[...] = jnp.sum(gp_all[...].astype(F32).reshape(2 * half, hid), axis=0)
    flush()
    for copy in shared:
        copy.wait_recv()
    for i in range(3):
        weight_out_grad(i, 3)
    left_end()
    at_home("right", rx_in)

    @pl.when(first_core)
    def _():
        rx_in[0] = rx_sum[0, 0]

    value = rx_in[0]
    for s in range(1, nx):
        value = value + rx_in[s]
    grad_tokens[:, right] = value.astype(BF16)
    flush()


def body(nz, ny, tokens, weight_in, bias_in, weight_out, out_grad):
    rows, feat = tokens.shape
    hid = weight_in.shape[1]
    cut = feat // 3 * 2
    rest = feat - cut
    nx = X
    nxs = nx // 2
    chunks = min(CHUNKS, nxs)
    per = nxs // chunks
    pr = nz * rows // ny
    vmem, anywhere = pl.BlockSpec(memory_space=pltpu.VMEM), pl.BlockSpec(memory_space=pl.ANY)
    out = pl.pallas_call(
        functools.partial(kernel, nz, ny, chunks),
        out_shape=(
            pltpu.VMEM((rows, feat), BF16),
            pltpu.VMEM((feat, hid), BF16),
            pltpu.VMEM((hid, feat), BF16),
            pltpu.VMEM((hid,), F32),
        ),
        in_specs=[anywhere, anywhere, vmem, anywhere, anywhere],
        out_specs=(vmem, vmem, vmem, vmem),
        scratch_shapes=[
            pltpu.VMEM((2, nxs, 2, nz, rows, feat), BF16),
            pltpu.VMEM((nxs, nz, rows, feat), BF16),
            pltpu.VMEM((nxs, nz, rows, feat), BF16),
            pltpu.VMEM((2, nz, rows, cut), BF16),
            pltpu.VMEM((2, rows, rest), BF16),
            pltpu.VMEM((2, feat, hid), BF16),
            pltpu.VMEM((2, hid, feat), BF16),
            pltpu.VMEM((2, nxs, ny, pr, hid), F32),
            pltpu.VMEM((2, chunks, ny - 1, per, pr, hid), BF16),
            pltpu.VMEM((2, chunks, ny - 1, per, pr, hid), BF16),
            pltpu.VMEM((2, nxs, ny, pr, hid), BF16),
            pltpu.VMEM((2, nxs, ny, pr, hid), BF16),
            pltpu.VMEM((nxs, 2, nz, rows, feat), F32),
            pltpu.VMEM((nxs, 2, nz, rows, feat), BF16),
            pltpu.VMEM((nx, nz, rows, cut), BF16),
            pltpu.VMEM((nz, rows, cut), F32),
            pltpu.VMEM((2, rows, cut), F32),
            pltpu.VMEM((nz - 1, rows, cut), F32),
            pltpu.VMEM((chunks, 2, per, 2, rows, rest), BF16),
            pltpu.VMEM((chunks, nz - 1, per, 2, rows, rest), BF16),
            pltpu.VMEM((nxs, 2, rows, rest), F32),
            pltpu.VMEM((nx, rows, rest), F32),
            pltpu.SemaphoreType.DMA((N_SEMS,)),
            pltpu.SemaphoreType.DMA((N_SEMS,)),
            pltpu.SemaphoreType.DMA((64,)),
            pltpu.SemaphoreType.DMA((6,)),
        ],
        compiler_params=pltpu.CompilerParams(
            collective_id=0, has_side_effects=True, vmem_limit_bytes=LIMIT
        ),
    )(tokens, weight_in, bias_in, weight_out, out_grad)
    return pl.pallas_call(
        copy_out,
        out_shape=tuple(jax.ShapeDtypeStruct(v.shape, v.dtype) for v in out),
        in_specs=[vmem] * 4,
        out_specs=(anywhere,) * 4,
        scratch_shapes=[pltpu.SemaphoreType.DMA((4,))],
        compiler_params=pltpu.CompilerParams(vmem_limit_bytes=1024 * 1024),
    )(*(pltpu.with_memory_space_constraint(v, pltpu.VMEM) for v in out))


def solution(mesh):
    nz, ny = mesh.shape["row"] // X, mesh.shape["col"] // 2
    in_specs = (P("row", "col"), P("col", "row"), P("row"), P("row", "col"), P("row", "col"))
    out_specs = (P("row", "col"), P("col", "row"), P("row", "col"), P("row"))
    return jax.shard_map(
        functools.partial(body, nz, ny),
        mesh=mesh,
        in_specs=in_specs,
        out_specs=out_specs,
        check_vma=False,
    )
```

```python
import functools

import jax
import jax.numpy as jnp
from jax import lax
from jax.experimental import pallas as pl
from jax.experimental.pallas import tpu as pltpu
from jax.sharding import PartitionSpec as P

SQRT_HALF = 0.7071067811865476
INV_ROOT_TWO_PI = 0.3989422804014327
X = 4
N_SEMS = 192
CHUNKS = 2
LIMIT = 56 * 1024 * 1024
BF16, F32 = jnp.bfloat16, jnp.float32
MESH = pl.DeviceIdType.MESH


def gelu_value(preact):
    return preact * 0.5 * (1.0 + lax.erf(preact * SQRT_HALF))


def gelu_slope(preact):
    return 0.5 * (1.0 + lax.erf(preact * SQRT_HALF)) + preact * INV_ROOT_TWO_PI * jnp.exp(
        -0.5 * preact * preact
    )


def around(n):
    out = [0]
    for d in range(1, n // 2):
        out += [d, -d]
    return out + [n // 2]


def copy_out(*refs):
    copies = [pltpu.make_async_copy(refs[i], refs[4 + i], refs[8].at[i]) for i in (1, 2, 0, 3)]
    for copy in copies:
        copy.start()
    for copy in copies:
        copy.wait()


def kernel(
    nz,
    ny,
    chunks,
    tokens,
    weight_in,
    bias_in,
    weight_out,
    out_grad,
    grad_tokens,
    grad_weight_in,
    grad_weight_out,
    grad_bias,
    both,
    tok_other,
    og_other,
    stage,
    own_right,
    w_in,
    w_out,
    part,
    ring_out,
    ring_in,
    act_all,
    gp_all,
    g_full,
    g_send,
    lx_in,
    lz_sum,
    lz_out,
    lz_in,
    rz_out,
    rz_in,
    rx_sum,
    rx_in,
    send_sems,
    recv_sems,
    slot_sems,
    local_sems,
):
    nx = X
    nxs = nx // 2
    rows, feat = tokens.shape
    hid = w_in.shape[-1]
    cut = stage.shape[-1]
    rest = feat - cut
    pr = nz * rows // ny
    hz, hy = nz // 2, ny // 2
    per = nxs // chunks
    spans = [pl.ds(k * per, per) for k in range(chunks)]
    turns = range(chunks - 1, -1, -1)
    row, col = lax.axis_index("row"), lax.axis_index("col")
    z, x = lax.div(row, nx), lax.rem(row, nx)
    y, c = lax.div(col, 2), lax.rem(col, 2)
    first_core, second_core = c == 0, c == 1

    def yn(d):
        return lax.rem(y + (ny + d), ny)

    def to_z(d):
        return (lax.rem(z + (nz + d), nz) * nx + x, col)

    def to_x(j, core):
        return (z * nx + lax.rem(x + j, nx), y * 2 + core)

    def to_y(d):
        return (row, yn(d) * 2 + c)

    partner = (row, y * 2 + (1 - c))
    pending = []
    slot_ids = {}

    def slot_id(key, count):
        if key not in slot_ids:
            slot_ids[key] = sum(n for _, n in slot_ids.values()), count
        return slot_ids[key][0]

    def send(src, dst, device, recv_sem=None, only=None):
        i = len(pending)
        copy = pltpu.make_async_remote_copy(
            src_ref=src,
            dst_ref=dst,
            send_sem=send_sems.at[i],
            recv_sem=recv_sems.at[i] if recv_sem is None else recv_sem,
            device_id=device,
            device_id_type=MESH,
        )
        if only is None:
            copy.start()
        else:
            pl.when(only)(copy.start)
        pending.append((copy, only))
        return copy

    def landed(dst, sem, only=None):
        copy = pltpu.make_async_remote_copy(
            src_ref=dst,
            dst_ref=dst,
            send_sem=send_sems.at[0],
            recv_sem=sem,
            device_id=partner,
            device_id_type=MESH,
        )
        if only is None:
            copy.wait_recv()
        else:
            pl.when(only)(copy.wait_recv)

    def local(src, dst, i):
        copy = pltpu.make_async_copy(src, dst, local_sems.at[i])
        copy.start()
        return copy

    left, right = pl.ds(0, cut), pl.ds(cut, rest)
    slot = {d: i for i, d in enumerate(around(nz))}
    slot[-hz] = slot[hz]
    near = 2 * min(hz, 3) - 1
    batches = [pl.ds(0, near)] + [pl.ds(near, nz - near)] * (near < nz)

    def direct(h, side):
        out = []
        for d in (2, 1):
            if d < h:
                out += [d, -d]
            elif d == h:
                out.append(d * side)
        return out

    def relayed(h, side):
        return [(sgn, d) for sgn in (1, -1) for d in (3, 4) if d < h or (d == h and sgn == side)]

    tok_half, og_half = both.at[0], both.at[1]
    sources = ((tokens, tok_half), (out_grad, og_half))
    sides = (1, -1)
    own = []
    for a, (src, _) in enumerate(sources):
        own.append(local(src.at[:, left], stage.at[a, 0], 2 * a))
        own.append(local(src.at[:, right], own_right.at[a], 2 * a + 1))
    load_in = local(weight_in, w_in.at[c], 4)
    load_out = local(weight_out, w_out.at[c], 5)

    barrier = pltpu.get_barrier_semaphore()
    friends = [to_x(j, core) for j in range(1, nx) for core in (0, 1)] + [partner]
    for d in (1, -1, 2, -2):
        friends += [to_z(d)] * (abs(d) <= hz) + [to_y(d)] * (abs(d) <= hy)
    for device in friends:
        pl.semaphore_signal(barrier, inc=1, device_id=device, device_id_type=MESH)
    pl.semaphore_wait(barrier, len(friends))
    for copy in own:
        copy.wait()

    lz, rz = {}, {}
    hops = sorted(range(1, nx), key=lambda j: -((nx - j) % nxs))

    def far_relay(kind):
        return nx == 4 and kind != "r"

    def x_sem(kind, xs, block):
        return slot_sems.at[slot_id((kind, xs), 2) + block]

    def over_x(kind, src, dst):
        for j in hops + [0]:
            core, xs = divmod((nx - j) % nx, nxs)
            if far_relay(kind) and j == nx // 2:
                continue
            if j == 0:
                send(src, dst(0, 1), partner, x_sem(kind, 0, 1), second_core)
            else:
                send(src, dst(xs, c), to_x(j, core), x_sem(kind, xs, c))

    def from_x(kind, xs, dst):
        for block in (0, 1):
            only = second_core if (xs, block) == (0, 0) else None
            landed(dst(xs, block), x_sem(kind, xs, block), only)

    def left_at(zs):
        return lambda xs, block: both.at[:, xs, block, zs, :, left]

    def right_at(xs, block):
        return both.at[:, xs, block, 0, :, right]

    def relay_x(kind, zs):
        if not far_relay(kind):
            return
        for block in (0, 1):
            landed(left_at(zs)(1, block), x_sem(kind, 1, block))
        a = 1 - c
        send(
            both.at[a, 1, :, zs, :, left],
            both.at[a, 0, :, zs, :, left],
            to_x(c + (nx - 1) * (1 - c), 1),
            slot_sems.at[slot_id((kind, "far"), 2) + a],
        )

    def from_x_left(kind, zs, xs):
        if not far_relay(kind):
            from_x(kind, xs, left_at(zs))
        elif xs == 0:
            landed(left_at(zs)(0, 1), x_sem(kind, 0, 1), first_core)
            for a in (0, 1):
                sem = slot_sems.at[slot_id((kind, "far"), 2) + a]
                landed(both.at[a, 0, :, zs, :, left], sem, second_core)

    far_side = [(sgn, hz, a) for a, sgn in enumerate(sides)] if hz > 2 else []
    relays = [(1, 3, None), (-1, 3, None)] * (hz > 3) + far_side

    def right_block(k, s, a=None):
        return both.at[slice(None) if a is None else a, spans[k], :, s, :, right]

    def stage_block(s, a=None):
        return stage.at[slice(None) if a is None else a, s]

    over_x("r", own_right, right_at)
    for d in direct(hz, 1):
        lz[d] = send(stage_block(0), stage_block(slot[-d]), to_z(d))

    @pl.when(first_core)
    def _():
        for a, (_, buf) in enumerate(sources):
            buf[0, 0, 0, :, right] = own_right[a]

    def right_start(k):
        for xs in range(k * per, (k + 1) * per):
            from_x("r", xs, right_at)
        for d in direct(hz, 1):
            rz[k, d] = send(right_block(k, 0), right_block(k, slot[-d]), to_z(d))

    def right_relay(k):
        for sgn, d, a in relays:
            if d == 3:
                rz[k, 2 * sgn].wait_recv()
            rz[k, d * sgn, a] = send(
                right_block(k, slot[-2 * sgn], a), right_block(k, slot[-d * sgn], a), to_z((d - 2) * sgn)
            )

    def left_relay():
        for sgn, d, a in relays:
            if d == 3:
                lz[2 * sgn].wait_recv()
            lz[d * sgn, a] = send(
                stage_block(slot[-2 * sgn], a), stage_block(slot[-d * sgn], a), to_z((d - 2) * sgn)
            )
        for d in direct(hz, 1):
            if not (hz > 2 and abs(d) == 2):
                lz[d].wait_recv()
        over_x(0, stage.at[:, batches[0]], left_at(batches[0]))

    def left_rest():
        for sgn, d, a in relays:
            lz[d * sgn, a].wait_recv()
        if near < nz:
            over_x(1, stage.at[:, batches[1]], left_at(batches[1]))

    right_start(turns[0])
    load_in.wait()
    send_in = send(w_in.at[c], w_in.at[c], partner)
    left_relay()
    load_out.wait()
    send_out = send(w_out.at[c], w_out.at[c], partner)
    right_relay(turns[0])
    for k in turns[1:]:
        right_start(k)
    left_rest()
    relay_x(0, batches[0])

    @pl.when(first_core)
    def _():
        for a, (_, buf) in enumerate(sources):
            buf[0, 0, :, :, left] = stage[a]

    def gathered(k):
        for d in direct(hz, 1):
            if not (hz > 2 and abs(d) == 2):
                rz[k, d].wait_recv()
        for sgn, d, a in relays:
            rz[k, d * sgn, a].wait_recv()
        for xs in range(k * per, (k + 1) * per):
            for i, zs in enumerate(batches):
                from_x_left(i, zs, xs)

    def product(a, k):
        total = 0
        for block in (0, 1):
            lhs = sources[a][1][spans[k], block].reshape(per * nz * rows, feat)
            if a == 0:
                out = jnp.dot(lhs, w_in[block], preferred_element_type=F32)
            else:
                out = lax.dot_general(
                    lhs, w_out[block], (((1,), (1,)), ((), ())), preferred_element_type=F32
                )
            total = out if block == 0 else total + out
        part[a, spans[k]] = total.reshape(per, ny, pr, hid)

    ring = {}

    def ring_send(a, k, o, value, d):
        i = len([key for key in ring if key[:2] == (a, k)])
        ring_out[a, k, i] = value.astype(BF16)
        ring[a, k, o] = (send(ring_out.at[a, k, i], ring_in.at[a, k, i], to_y(d)), i)

    def ring_got(a, k, o):
        copy, i = ring[a, k, o]
        copy.wait_recv()
        return ring_in[a, k, i].astype(F32)

    def ring_first(a, k):
        for sgn, d in relayed(hy, sides[a]):
            ring_send(a, k, d * sgn, part[a, spans[k], yn(d * sgn)], (d - 2) * sgn)
        for d in direct(hy, sides[a]):
            if abs(d) == 1:
                ring_send(a, k, d, part[a, spans[k], yn(d)], d)

    def ring_second(a, k):
        for d in direct(hy, sides[a]):
            if abs(d) == 2:
                value = part[a, spans[k], yn(d)]
                for sgn, far in relayed(hy, sides[a]):
                    if sgn * d > 0:
                        value = value + ring_got(a, k, far * sgn)
                ring_send(a, k, d, value, d)

    def ring_end(a, k):
        value = part[a, spans[k], y]
        for d in reversed(direct(hy, sides[a])):
            value = value + ring_got(a, k, d)
        return value

    flushed = [0]

    def flush():
        for copy, only in pending[flushed[0] :]:
            if only is None:
                copy.wait_send()
            else:
                pl.when(only)(copy.wait_send)
        flushed[0] = len(pending)

    def multiply(k):
        gathered(k)
        for a in (0, 1):
            if k == turns[0]:
                (send_in, send_out)[a].wait_recv()
            product(a, k)
            ring_first(a, k)

    spread = {}

    def spread_first(buf, a, k):
        for d in direct(hy, sides[a]):
            block = buf.at[c, spans[k], y]
            spread[a, k, d] = send(block, block, to_y(d))

    def spread_second(buf, a, k):
        for d in direct(hy, sides[a]):
            spread[a, k, d].wait_recv()
            block = buf.at[c, spans[k], yn(-d)]
            for sgn, far in relayed(hy, sides[a]):
                if d == 2 * sgn:
                    spread[a, k, far * sgn] = send(block, block, to_y((far - 2) * sgn))

    def spread_end(a, k):
        for sgn, far in relayed(hy, sides[a]):
            spread[a, k, far * sgn].wait_recv()

    def pointwise(k):
        preact = ring_end(0, k) + bias_in[...][None, None, :]
        act_all[c, spans[k], y] = gelu_value(preact).astype(BF16)
        slope = gelu_slope(preact)
        gp_all[c, spans[k], y] = (ring_end(1, k) * slope).astype(BF16)
        spread_first(gp_all, 1, k)

    def row_terms(k, span):
        grads = gp_all[c, spans[k]].reshape(per * nz * rows, hid)
        for block in (0, 1):
            out = lax.dot_general(
                grads, w_in[block, span, :], (((1,), (1,)), ((), ())), preferred_element_type=F32
            ).reshape(per, nz, rows, span.size)
            g_full[spans[k], block, :, :, span] = out
            g_send[spans[k], block, :, :, span] = out.astype(BF16)

    tl, tr = {}, {}

    def home(kind, k, src, dst):
        for xs in range(k * per, (k + 1) * per):
            s = c * nxs + xs
            for block in (0, 1):
                sem = slot_sems.at[slot_id(kind, nx) + s]
                only = second_core if (xs, block) == (0, 0) else None
                send(src(xs, block), dst.at[s], to_x(s, block), sem, only)

    def at_home(kind, dst):
        for s in range(nx):
            sem = slot_sems.at[slot_id(kind, nx) + s]
            landed(dst.at[s], sem, second_core if s == 0 else None)

    def right_put(k, o, src, d):
        i = len([key for key in tr if key[0] == k])
        tr[k, o] = (send(src, rz_in.at[k, i], to_z(d)), i)

    def right_got(k, o):
        copy, i = tr[k, o]
        copy.wait_recv()
        return rz_in[k, i].astype(F32)

    def right_first(k):
        for sgn, d in relayed(hz, 1):
            o = d * sgn
            right_put(k, o, g_send.at[spans[k], :, slot[o], :, right], (d - 2) * sgn)
        for o in direct(hz, 1):
            if abs(o) == 1:
                right_put(k, o, g_send.at[spans[k], :, slot[o], :, right], o)

    def right_second(k):
        for i, o in enumerate(d for d in direct(hz, 1) if abs(d) == 2):
            value = g_full[spans[k], :, slot[o], :, right]
            for sgn, d in relayed(hz, 1):
                if sgn * o > 0:
                    value = value + right_got(k, d * sgn)
            rz_out[k, i] = value.astype(BF16)
            right_put(k, o, rz_out.at[k, i], o)

    def right_end(k):
        value = g_full[spans[k], :, 0, :, right]
        for o in reversed(direct(hz, 1)):
            value = value + right_got(k, o)
        rx_sum[spans[k]] = value
        home("right", k, lambda xs, block: rx_sum.at[xs, block], rx_in)

    def left_put(o, src, d):
        tl[o] = (send(src, lz_in.at[len(tl)], to_z(d)), len(tl))

    def left_got(o):
        copy, i = tl[o]
        copy.wait_recv()
        return lz_in[i]

    def left_first():
        at_home("left", lx_in)

        @pl.when(first_core)
        def _():
            lx_in[0] = g_send[0, 0, :, :, left]

        value = lx_in[0].astype(F32)
        for s in range(1, nx):
            value = value + lx_in[s].astype(F32)
        lz_sum[...] = value
        for sgn, d in relayed(hz, -1):
            left_put(d * sgn, lz_sum.at[slot[d * sgn]], (d - 2) * sgn)
        for o in direct(hz, -1):
            if abs(o) == 1:
                left_put(o, lz_sum.at[slot[o]], o)

    def left_second():
        for i, o in enumerate(d for d in direct(hz, -1) if abs(d) == 2):
            value = lz_sum[slot[o]]
            for sgn, d in relayed(hz, -1):
                if sgn * o > 0:
                    value = value + left_got(d * sgn)
            lz_out[i] = value
            left_put(o, lz_out.at[i], o)

    def left_end():
        value = lz_sum[0]
        for o in reversed(direct(hz, -1)):
            value = value + left_got(o)
        grad_tokens[:, left] = value.astype(BF16)

    half = nxs * nz * rows

    def weight_in_grad(i, n):
        step = feat // n
        span = pl.ds(i * step, step)
        out = lax.dot_general(
            tok_half[:, c, :, :, span].reshape(half, step),
            gp_all[c].reshape(half, hid),
            (((0,), (0,)), ((), ())),
            preferred_element_type=F32,
        ) + lax.dot_general(
            tok_other[:, :, :, span].reshape(half, step),
            gp_all[1 - c].reshape(half, hid),
            (((0,), (0,)), ((), ())),
            preferred_element_type=F32,
        )
        grad_weight_in[span, :] = out.astype(BF16)

    def weight_out_grad(i, n):
        step = hid // n
        span = pl.ds(i * step, step)
        out = lax.dot_general(
            act_all[c, :, :, :, span].reshape(half, step),
            og_half[:, c].reshape(half, feat),
            (((0,), (0,)), ((), ())),
            preferred_element_type=F32,
        ) + lax.dot_general(
            act_all[1 - c, :, :, :, span].reshape(half, step),
            og_other[...].reshape(half, feat),
            (((0,), (0,)), ((), ())),
            preferred_element_type=F32,
        )
        grad_weight_out[span, :] = out.astype(BF16)

    shared = []

    def row_start(k):
        spread_end(1, k)
        row_terms(k, right)
        right_first(k)
        row_terms(k, left)
        home("left", k, lambda xs, block: g_send.at[xs, block, :, :, left], lx_in)
        block = gp_all.at[c, spans[k]]
        shared.append(send(block, block, partner))

    def share_act(k):
        spread_end(0, k)
        block = act_all.at[c, spans[k]]
        shared.append(send(block, block, partner))

    one, rest_turns = turns[0], list(turns[1:])
    if near < nz:
        relay_x(1, batches[1])
    multiply(one)
    for k in rest_turns:
        right_relay(k)
    ring_second(0, one)
    ring_second(1, one)
    for k in rest_turns:
        multiply(k)
    pointwise(one)
    for a, other in enumerate((tok_other, og_other)):
        shared.append(send(sources[a][1].at[:, 1 - c], other, partner))
    for k in rest_turns:
        ring_second(0, k)
        ring_second(1, k)
    spread_second(gp_all, 1, one)
    for k in rest_turns:
        pointwise(k)
    row_start(one)
    for k in rest_turns:
        spread_second(gp_all, 1, k)
    for k in turns:
        spread_first(act_all, 0, k)
    for k in rest_turns:
        row_start(k)
    right_second(one)
    flush()
    for k in turns:
        spread_second(act_all, 0, k)
    for copy in shared:
        copy.wait_recv()
    shared.clear()
    weight_in_grad(0, 3)
    for k in rest_turns:
        right_second(k)
    left_first()
    for k in turns:
        share_act(k)
    weight_in_grad(1, 3)
    for k in turns:
        right_end(k)
    left_second()
    weight_in_grad(2, 3)
    grad_bias[...] = jnp.sum(gp_all[...].astype(F32).reshape(2 * half, hid), axis=0)
    flush()
    for copy in shared:
        copy.wait_recv()
    for i in range(3):
        weight_out_grad(i, 3)
    left_end()
    at_home("right", rx_in)

    @pl.when(first_core)
    def _():
        rx_in[0] = rx_sum[0, 0]

    value = rx_in[0]
    for s in range(1, nx):
        value = value + rx_in[s]
    grad_tokens[:, right] = value.astype(BF16)
    flush()


def body(nz, ny, tokens, weight_in, bias_in, weight_out, out_grad):
    rows, feat = tokens.shape
    hid = weight_in.shape[1]
    cut = feat // 3 * 2
    rest = feat - cut
    nx = X
    nxs = nx // 2
    chunks = min(CHUNKS, nxs)
    per = nxs // chunks
    pr = nz * rows // ny
    vmem, anywhere = pl.BlockSpec(memory_space=pltpu.VMEM), pl.BlockSpec(memory_space=pl.ANY)
    out = pl.pallas_call(
        functools.partial(kernel, nz, ny, chunks),
        out_shape=(
            pltpu.VMEM((rows, feat), BF16),
            pltpu.VMEM((feat, hid), BF16),
            pltpu.VMEM((hid, feat), BF16),
            pltpu.VMEM((hid,), F32),
        ),
        in_specs=[anywhere, anywhere, vmem, anywhere, anywhere],
        out_specs=(vmem, vmem, vmem, vmem),
        scratch_shapes=[
            pltpu.VMEM((2, nxs, 2, nz, rows, feat), BF16),
            pltpu.VMEM((nxs, nz, rows, feat), BF16),
            pltpu.VMEM((nxs, nz, rows, feat), BF16),
            pltpu.VMEM((2, nz, rows, cut), BF16),
            pltpu.VMEM((2, rows, rest), BF16),
            pltpu.VMEM((2, feat, hid), BF16),
            pltpu.VMEM((2, hid, feat), BF16),
            pltpu.VMEM((2, nxs, ny, pr, hid), F32),
            pltpu.VMEM((2, chunks, ny - 1, per, pr, hid), BF16),
            pltpu.VMEM((2, chunks, ny - 1, per, pr, hid), BF16),
            pltpu.VMEM((2, nxs, ny, pr, hid), BF16),
            pltpu.VMEM((2, nxs, ny, pr, hid), BF16),
            pltpu.VMEM((nxs, 2, nz, rows, feat), F32),
            pltpu.VMEM((nxs, 2, nz, rows, feat), BF16),
            pltpu.VMEM((nx, nz, rows, cut), BF16),
            pltpu.VMEM((nz, rows, cut), F32),
            pltpu.VMEM((2, rows, cut), F32),
            pltpu.VMEM((nz - 1, rows, cut), F32),
            pltpu.VMEM((chunks, 2, per, 2, rows, rest), BF16),
            pltpu.VMEM((chunks, nz - 1, per, 2, rows, rest), BF16),
            pltpu.VMEM((nxs, 2, rows, rest), F32),
            pltpu.VMEM((nx, rows, rest), F32),
            pltpu.SemaphoreType.DMA((N_SEMS,)),
            pltpu.SemaphoreType.DMA((N_SEMS,)),
            pltpu.SemaphoreType.DMA((64,)),
            pltpu.SemaphoreType.DMA((6,)),
        ],
        compiler_params=pltpu.CompilerParams(
            collective_id=0, has_side_effects=True, vmem_limit_bytes=LIMIT
        ),
    )(tokens, weight_in, bias_in, weight_out, out_grad)
    return pl.pallas_call(
        copy_out,
        out_shape=tuple(jax.ShapeDtypeStruct(v.shape, v.dtype) for v in out),
        in_specs=[vmem] * 4,
        out_specs=(anywhere,) * 4,
        scratch_shapes=[pltpu.SemaphoreType.DMA((4,))],
        compiler_params=pltpu.CompilerParams(vmem_limit_bytes=1024 * 1024),
    )(*(pltpu.with_memory_space_constraint(v, pltpu.VMEM) for v in out))


def solution(mesh):
    nz, ny = mesh.shape["row"] // X, mesh.shape["col"] // 2
    in_specs = (P("row", "col"), P("col", "row"), P("row"), P("row", "col"), P("row", "col"))
    out_specs = (P("row", "col"), P("col", "row"), P("row", "col"), P("row"))
    return jax.shard_map(
        functools.partial(body, nz, ny),
        mesh=mesh,
        in_specs=in_specs,
        out_specs=out_specs,
        check_vma=False,
    )
```

```python
import functools

import jax
import jax.numpy as jnp
from jax import lax
from jax.experimental import pallas as pl
from jax.experimental.pallas import tpu as pltpu
from jax.sharding import PartitionSpec as P

SQRT_HALF = 0.7071067811865476
INV_ROOT_TWO_PI = 0.3989422804014327
X = 4
N_SEMS = 192
CHUNKS = 2
LIMIT = 56 * 1024 * 1024
BF16, F32 = jnp.bfloat16, jnp.float32
MESH = pl.DeviceIdType.MESH


def gelu_value(preact):
    return preact * 0.5 * (1.0 + lax.erf(preact * SQRT_HALF))


def gelu_slope(preact):
    return 0.5 * (1.0 + lax.erf(preact * SQRT_HALF)) + preact * INV_ROOT_TWO_PI * jnp.exp(
        -0.5 * preact * preact
    )


def around(n):
    out = [0]
    for d in range(1, n // 2):
        out += [d, -d]
    return out + [n // 2]


def copy_out(*refs):
    copies = [pltpu.make_async_copy(refs[i], refs[4 + i], refs[8].at[i]) for i in (1, 2, 0, 3)]
    for copy in copies:
        copy.start()
    for copy in copies:
        copy.wait()


def kernel(
    nz,
    ny,
    chunks,
    tokens,
    weight_in,
    bias_in,
    weight_out,
    out_grad,
    grad_tokens,
    grad_weight_in,
    grad_weight_out,
    grad_bias,
    both,
    tok_other,
    og_other,
    stage,
    own_right,
    w_in,
    w_out,
    part,
    ring_out,
    ring_in,
    act_all,
    gp_all,
    g_full,
    g_send,
    lx_in,
    lz_sum,
    lz_out,
    lz_in,
    rz_out,
    rz_in,
    rx_sum,
    rx_in,
    send_sems,
    recv_sems,
    slot_sems,
    local_sems,
):
    nx = X
    nxs = nx // 2
    rows, feat = tokens.shape
    hid = w_in.shape[-1]
    cut = stage.shape[-1]
    rest = feat - cut
    pr = nz * rows // ny
    hz, hy = nz // 2, ny // 2
    per = nxs // chunks
    spans = [pl.ds(k * per, per) for k in range(chunks)]
    turns = range(chunks - 1, -1, -1)
    row, col = lax.axis_index("row"), lax.axis_index("col")
    z, x = lax.div(row, nx), lax.rem(row, nx)
    y, c = lax.div(col, 2), lax.rem(col, 2)
    first_core, second_core = c == 0, c == 1

    def yn(d):
        return lax.rem(y + (ny + d), ny)

    def to_z(d):
        return (lax.rem(z + (nz + d), nz) * nx + x, col)

    def to_x(j, core):
        return (z * nx + lax.rem(x + j, nx), y * 2 + core)

    def to_y(d):
        return (row, yn(d) * 2 + c)

    partner = (row, y * 2 + (1 - c))
    pending = []
    slot_ids = {}

    def slot_id(key, count):
        if key not in slot_ids:
            slot_ids[key] = sum(n for _, n in slot_ids.values()), count
        return slot_ids[key][0]

    def send(src, dst, device, recv_sem=None, only=None):
        i = len(pending)
        copy = pltpu.make_async_remote_copy(
            src_ref=src,
            dst_ref=dst,
            send_sem=send_sems.at[i],
            recv_sem=recv_sems.at[i] if recv_sem is None else recv_sem,
            device_id=device,
            device_id_type=MESH,
        )
        if only is None:
            copy.start()
        else:
            pl.when(only)(copy.start)
        pending.append((copy, only))
        return copy

    def landed(dst, sem, only=None):
        copy = pltpu.make_async_remote_copy(
            src_ref=dst,
            dst_ref=dst,
            send_sem=send_sems.at[0],
            recv_sem=sem,
            device_id=partner,
            device_id_type=MESH,
        )
        if only is None:
            copy.wait_recv()
        else:
            pl.when(only)(copy.wait_recv)

    def local(src, dst, i):
        copy = pltpu.make_async_copy(src, dst, local_sems.at[i])
        copy.start()
        return copy

    left, right = pl.ds(0, cut), pl.ds(cut, rest)
    low = lx_in.shape[-1]
    west, east = pl.ds(0, low), pl.ds(low, feat - low)
    slot = {d: i for i, d in enumerate(around(nz))}
    slot[-hz] = slot[hz]
    near = 2 * min(hz, 3) - 1
    batches = [pl.ds(0, near)] + [pl.ds(near, nz - near)] * (near < nz)

    def direct(h, side):
        out = []
        for d in (2, 1):
            if d < h:
                out += [d, -d]
            elif d == h:
                out.append(d * side)
        return out

    def relayed(h, side):
        return [(sgn, d) for sgn in (1, -1) for d in (3, 4) if d < h or (d == h and sgn == side)]

    tok_half, og_half = both.at[0], both.at[1]
    sources = ((tokens, tok_half), (out_grad, og_half))
    sides = (1, -1)
    own = []
    for a, (src, _) in enumerate(sources):
        own.append(local(src.at[:, left], stage.at[a, 0], 2 * a))
        own.append(local(src.at[:, right], own_right.at[a], 2 * a + 1))
    load_in = local(weight_in, w_in.at[c], 4)
    load_out = local(weight_out, w_out.at[c], 5)

    barrier = pltpu.get_barrier_semaphore()
    friends = [to_x(j, core) for j in range(1, nx) for core in (0, 1)] + [partner]
    for d in (1, -1, 2, -2):
        friends += [to_z(d)] * (abs(d) <= hz) + [to_y(d)] * (abs(d) <= hy)
    for device in friends:
        pl.semaphore_signal(barrier, inc=1, device_id=device, device_id_type=MESH)
    pl.semaphore_wait(barrier, len(friends))
    for copy in own:
        copy.wait()

    lz, rz = {}, {}
    hops = sorted(range(1, nx), key=lambda j: -((nx - j) % nxs))

    def far_relay(kind):
        return nx == 4 and kind != "r"

    def x_sem(kind, xs, block):
        return slot_sems.at[slot_id((kind, xs), 2) + block]

    def over_x(kind, src, dst):
        for j in hops + [0]:
            core, xs = divmod((nx - j) % nx, nxs)
            if far_relay(kind) and j == nx // 2:
                continue
            if j == 0:
                send(src, dst(0, 1), partner, x_sem(kind, 0, 1), second_core)
            else:
                send(src, dst(xs, c), to_x(j, core), x_sem(kind, xs, c))

    def from_x(kind, xs, dst):
        for block in (0, 1):
            only = second_core if (xs, block) == (0, 0) else None
            landed(dst(xs, block), x_sem(kind, xs, block), only)

    def left_at(zs):
        return lambda xs, block: both.at[:, xs, block, zs, :, left]

    def right_at(xs, block):
        return both.at[:, xs, block, 0, :, right]

    def relay_x(kind, zs):
        if not far_relay(kind):
            return
        for block in (0, 1):
            landed(left_at(zs)(1, block), x_sem(kind, 1, block))
        a = 1 - c
        send(
            both.at[a, 1, :, zs, :, left],
            both.at[a, 0, :, zs, :, left],
            to_x(c + (nx - 1) * (1 - c), 1),
            slot_sems.at[slot_id((kind, "far"), 2) + a],
        )

    def from_x_left(kind, zs, xs):
        if not far_relay(kind):
            from_x(kind, xs, left_at(zs))
        elif xs == 0:
            landed(left_at(zs)(0, 1), x_sem(kind, 0, 1), first_core)
            for a in (0, 1):
                sem = slot_sems.at[slot_id((kind, "far"), 2) + a]
                landed(both.at[a, 0, :, zs, :, left], sem, second_core)

    far_side = [(sgn, hz, a) for a, sgn in enumerate(sides)] if hz > 2 else []
    relays = [(1, 3, None), (-1, 3, None)] * (hz > 3) + far_side

    def right_block(k, s, a=None):
        return both.at[slice(None) if a is None else a, spans[k], :, s, :, right]

    def stage_block(s, a=None):
        return stage.at[slice(None) if a is None else a, s]

    over_x("r", own_right, right_at)
    for d in direct(hz, 1):
        lz[d] = send(stage_block(0), stage_block(slot[-d]), to_z(d))

    @pl.when(first_core)
    def _():
        for a, (_, buf) in enumerate(sources):
            buf[0, 0, 0, :, right] = own_right[a]

    def right_start(k):
        for xs in range(k * per, (k + 1) * per):
            from_x("r", xs, right_at)
        for d in direct(hz, 1):
            rz[k, d] = send(right_block(k, 0), right_block(k, slot[-d]), to_z(d))

    def right_relay(k):
        for sgn, d, a in relays:
            if d == 3:
                rz[k, 2 * sgn].wait_recv()
            rz[k, d * sgn, a] = send(
                right_block(k, slot[-2 * sgn], a), right_block(k, slot[-d * sgn], a), to_z((d - 2) * sgn)
            )

    def left_relay():
        for sgn, d, a in relays:
            if d == 3:
                lz[2 * sgn].wait_recv()
            lz[d * sgn, a] = send(
                stage_block(slot[-2 * sgn], a), stage_block(slot[-d * sgn], a), to_z((d - 2) * sgn)
            )
        for d in direct(hz, 1):
            if not (hz > 2 and abs(d) == 2):
                lz[d].wait_recv()
        over_x(0, stage.at[:, batches[0]], left_at(batches[0]))

    def left_rest():
        for sgn, d, a in relays:
            lz[d * sgn, a].wait_recv()
        if near < nz:
            over_x(1, stage.at[:, batches[1]], left_at(batches[1]))

    right_start(turns[0])
    load_in.wait()
    send_in = send(w_in.at[c], w_in.at[c], partner)
    left_relay()
    load_out.wait()
    send_out = send(w_out.at[c], w_out.at[c], partner)
    right_relay(turns[0])
    for k in turns[1:]:
        right_start(k)
    left_rest()
    relay_x(0, batches[0])

    @pl.when(first_core)
    def _():
        for a, (_, buf) in enumerate(sources):
            buf[0, 0, :, :, left] = stage[a]

    def gathered(k):
        for d in direct(hz, 1):
            if not (hz > 2 and abs(d) == 2):
                rz[k, d].wait_recv()
        for sgn, d, a in relays:
            rz[k, d * sgn, a].wait_recv()
        for xs in range(k * per, (k + 1) * per):
            for i, zs in enumerate(batches):
                from_x_left(i, zs, xs)

    def product(a, k):
        total = 0
        for block in (0, 1):
            lhs = sources[a][1][spans[k], block].reshape(per * nz * rows, feat)
            if a == 0:
                out = jnp.dot(lhs, w_in[block], preferred_element_type=F32)
            else:
                out = lax.dot_general(
                    lhs, w_out[block], (((1,), (1,)), ((), ())), preferred_element_type=F32
                )
            total = out if block == 0 else total + out
        part[a, spans[k]] = total.reshape(per, ny, pr, hid)

    ring = {}

    def ring_send(a, k, o, value, d):
        i = len([key for key in ring if key[:2] == (a, k)])
        ring_out[a, k, i] = value.astype(BF16)
        ring[a, k, o] = (send(ring_out.at[a, k, i], ring_in.at[a, k, i], to_y(d)), i)

    def ring_got(a, k, o):
        copy, i = ring[a, k, o]
        copy.wait_recv()
        return ring_in[a, k, i].astype(F32)

    def ring_first(a, k):
        for sgn, d in relayed(hy, sides[a]):
            ring_send(a, k, d * sgn, part[a, spans[k], yn(d * sgn)], (d - 2) * sgn)
        for d in direct(hy, sides[a]):
            if abs(d) == 1:
                ring_send(a, k, d, part[a, spans[k], yn(d)], d)

    def ring_second(a, k):
        for d in direct(hy, sides[a]):
            if abs(d) == 2:
                value = part[a, spans[k], yn(d)]
                for sgn, far in relayed(hy, sides[a]):
                    if sgn * d > 0:
                        value = value + ring_got(a, k, far * sgn)
                ring_send(a, k, d, value, d)

    def ring_end(a, k):
        value = part[a, spans[k], y]
        for d in reversed(direct(hy, sides[a])):
            value = value + ring_got(a, k, d)
        return value

    flushed = [0]

    def flush():
        for copy, only in pending[flushed[0] :]:
            if only is None:
                copy.wait_send()
            else:
                pl.when(only)(copy.wait_send)
        flushed[0] = len(pending)

    def multiply(k):
        gathered(k)
        for a in (0, 1):
            if k == turns[0]:
                (send_in, send_out)[a].wait_recv()
            product(a, k)
            ring_first(a, k)

    spread = {}

    def spread_first(buf, a, k):
        for d in direct(hy, sides[a]):
            block = buf.at[c, spans[k], y]
            spread[a, k, d] = send(block, block, to_y(d))

    def spread_second(buf, a, k):
        for d in direct(hy, sides[a]):
            spread[a, k, d].wait_recv()
            block = buf.at[c, spans[k], yn(-d)]
            for sgn, far in relayed(hy, sides[a]):
                if d == 2 * sgn:
                    spread[a, k, far * sgn] = send(block, block, to_y((far - 2) * sgn))

    def spread_end(a, k):
        for sgn, far in relayed(hy, sides[a]):
            spread[a, k, far * sgn].wait_recv()

    def pointwise(k):
        preact = ring_end(0, k) + bias_in[...][None, None, :]
        act_all[c, spans[k], y] = gelu_value(preact).astype(BF16)
        slope = gelu_slope(preact)
        gp_all[c, spans[k], y] = (ring_end(1, k) * slope).astype(BF16)
        spread_first(gp_all, 1, k)

    def row_terms(k, span):
        grads = gp_all[c, spans[k]].reshape(per * nz * rows, hid)
        for block in (0, 1):
            out = lax.dot_general(
                grads, w_in[block, span, :], (((1,), (1,)), ((), ())), preferred_element_type=F32
            ).reshape(per, nz, rows, span.size)
            g_full[spans[k], block, :, :, span] = out
            g_send[spans[k], block, :, :, span] = out.astype(BF16)

    tl, tr = {}, {}

    def home(kind, k, src, dst):
        for xs in range(k * per, (k + 1) * per):
            s = c * nxs + xs
            for block in (0, 1):
                sem = slot_sems.at[slot_id(kind, nx) + s]
                only = second_core if (xs, block) == (0, 0) else None
                send(src(xs, block), dst.at[s], to_x(s, block), sem, only)

    def at_home(kind, dst):
        for s in range(nx):
            sem = slot_sems.at[slot_id(kind, nx) + s]
            landed(dst.at[s], sem, second_core if s == 0 else None)

    def right_put(k, o, src, d):
        i = len([key for key in tr if key[0] == k])
        tr[k, o] = (send(src, rz_in.at[k, i], to_z(d)), i)

    def right_got(k, o):
        copy, i = tr[k, o]
        copy.wait_recv()
        return rz_in[k, i].astype(F32)

    def right_first(k):
        for sgn, d in relayed(hz, 1):
            o = d * sgn
            right_put(k, o, g_send.at[spans[k], :, slot[o], :, east], (d - 2) * sgn)
        for o in direct(hz, 1):
            if abs(o) == 1:
                right_put(k, o, g_send.at[spans[k], :, slot[o], :, east], o)

    def right_second(k):
        for i, o in enumerate(d for d in direct(hz, 1) if abs(d) == 2):
            value = g_full[spans[k], :, slot[o], :, east]
            for sgn, d in relayed(hz, 1):
                if sgn * o > 0:
                    value = value + right_got(k, d * sgn)
            rz_out[k, i] = value.astype(BF16)
            right_put(k, o, rz_out.at[k, i], o)

    def right_end(k):
        value = g_full[spans[k], :, 0, :, east]
        for o in reversed(direct(hz, 1)):
            value = value + right_got(k, o)
        rx_sum[spans[k]] = value
        home("right", k, lambda xs, block: rx_sum.at[xs, block], rx_in)

    def left_put(o, src, d):
        tl[o] = (send(src, lz_in.at[len(tl)], to_z(d)), len(tl))

    def left_got(o):
        copy, i = tl[o]
        copy.wait_recv()
        return lz_in[i]

    def left_first():
        at_home("left", lx_in)

        @pl.when(first_core)
        def _():
            lx_in[0] = g_send[0, 0, :, :, west]

        value = lx_in[0].astype(F32)
        for s in range(1, nx):
            value = value + lx_in[s].astype(F32)
        lz_sum[...] = value
        for sgn, d in relayed(hz, -1):
            left_put(d * sgn, lz_sum.at[slot[d * sgn]], (d - 2) * sgn)
        for o in direct(hz, -1):
            if abs(o) == 1:
                left_put(o, lz_sum.at[slot[o]], o)

    def left_second():
        for i, o in enumerate(d for d in direct(hz, -1) if abs(d) == 2):
            value = lz_sum[slot[o]]
            for sgn, d in relayed(hz, -1):
                if sgn * o > 0:
                    value = value + left_got(d * sgn)
            lz_out[i] = value
            left_put(o, lz_out.at[i], o)

    def left_end():
        value = lz_sum[0]
        for o in reversed(direct(hz, -1)):
            value = value + left_got(o)
        grad_tokens[:, west] = value.astype(BF16)

    half = nxs * nz * rows

    def weight_in_grad(i, n):
        step = feat // n
        span = pl.ds(i * step, step)
        out = lax.dot_general(
            tok_half[:, c, :, :, span].reshape(half, step),
            gp_all[c].reshape(half, hid),
            (((0,), (0,)), ((), ())),
            preferred_element_type=F32,
        ) + lax.dot_general(
            tok_other[:, :, :, span].reshape(half, step),
            gp_all[1 - c].reshape(half, hid),
            (((0,), (0,)), ((), ())),
            preferred_element_type=F32,
        )
        grad_weight_in[span, :] = out.astype(BF16)

    def weight_out_grad(i, n):
        step = hid // n
        span = pl.ds(i * step, step)
        out = lax.dot_general(
            act_all[c, :, :, :, span].reshape(half, step),
            og_half[:, c].reshape(half, feat),
            (((0,), (0,)), ((), ())),
            preferred_element_type=F32,
        ) + lax.dot_general(
            act_all[1 - c, :, :, :, span].reshape(half, step),
            og_other[...].reshape(half, feat),
            (((0,), (0,)), ((), ())),
            preferred_element_type=F32,
        )
        grad_weight_out[span, :] = out.astype(BF16)

    shared = []

    def row_start(k):
        spread_end(1, k)
        row_terms(k, east)
        right_first(k)
        row_terms(k, west)
        home("left", k, lambda xs, block: g_send.at[xs, block, :, :, west], lx_in)
        block = gp_all.at[c, spans[k]]
        shared.append(send(block, block, partner))

    def share_act(k):
        spread_end(0, k)
        block = act_all.at[c, spans[k]]
        shared.append(send(block, block, partner))

    one, rest_turns = turns[0], list(turns[1:])
    if near < nz:
        relay_x(1, batches[1])
    multiply(one)
    for k in rest_turns:
        right_relay(k)
    ring_second(0, one)
    ring_second(1, one)
    for k in rest_turns:
        multiply(k)
    pointwise(one)
    for a, other in enumerate((tok_other, og_other)):
        shared.append(send(sources[a][1].at[:, 1 - c], other, partner))
    for k in rest_turns:
        ring_second(0, k)
        ring_second(1, k)
    spread_second(gp_all, 1, one)
    for k in rest_turns:
        pointwise(k)
    row_start(one)
    for k in rest_turns:
        spread_second(gp_all, 1, k)
    for k in turns:
        spread_first(act_all, 0, k)
    flush()
    right_second(one)
    for k in rest_turns:
        row_start(k)
    for k in turns:
        spread_second(act_all, 0, k)
    for copy in shared:
        copy.wait_recv()
    shared.clear()
    weight_in_grad(0, 3)
    for k in rest_turns:
        right_second(k)
    left_first()
    weight_in_grad(1, 3)
    for k in turns:
        right_end(k)
    left_second()
    for k in turns:
        share_act(k)
    weight_in_grad(2, 3)
    grad_bias[...] = jnp.sum(gp_all[...].astype(F32).reshape(2 * half, hid), axis=0)
    flush()
    for copy in shared:
        copy.wait_recv()
    for i in range(3):
        weight_out_grad(i, 3)
    left_end()
    at_home("right", rx_in)

    @pl.when(first_core)
    def _():
        rx_in[0] = rx_sum[0, 0]

    value = rx_in[0]
    for s in range(1, nx):
        value = value + rx_in[s]
    grad_tokens[:, east] = value.astype(BF16)
    flush()


def body(nz, ny, tokens, weight_in, bias_in, weight_out, out_grad):
    rows, feat = tokens.shape
    hid = weight_in.shape[1]
    cut = feat // 3 * 2
    rest = feat - cut
    low = feat // 3
    high = feat - low
    nx = X
    nxs = nx // 2
    chunks = min(CHUNKS, nxs)
    per = nxs // chunks
    pr = nz * rows // ny
    vmem, anywhere = pl.BlockSpec(memory_space=pltpu.VMEM), pl.BlockSpec(memory_space=pl.ANY)
    out = pl.pallas_call(
        functools.partial(kernel, nz, ny, chunks),
        out_shape=(
            pltpu.VMEM((rows, feat), BF16),
            pltpu.VMEM((feat, hid), BF16),
            pltpu.VMEM((hid, feat), BF16),
            pltpu.VMEM((hid,), F32),
        ),
        in_specs=[anywhere, anywhere, vmem, anywhere, anywhere],
        out_specs=(vmem, vmem, vmem, vmem),
        scratch_shapes=[
            pltpu.VMEM((2, nxs, 2, nz, rows, feat), BF16),
            pltpu.VMEM((nxs, nz, rows, feat), BF16),
            pltpu.VMEM((nxs, nz, rows, feat), BF16),
            pltpu.VMEM((2, nz, rows, cut), BF16),
            pltpu.VMEM((2, rows, rest), BF16),
            pltpu.VMEM((2, feat, hid), BF16),
            pltpu.VMEM((2, hid, feat), BF16),
            pltpu.VMEM((2, nxs, ny, pr, hid), F32),
            pltpu.VMEM((2, chunks, ny - 1, per, pr, hid), BF16),
            pltpu.VMEM((2, chunks, ny - 1, per, pr, hid), BF16),
            pltpu.VMEM((2, nxs, ny, pr, hid), BF16),
            pltpu.VMEM((2, nxs, ny, pr, hid), BF16),
            pltpu.VMEM((nxs, 2, nz, rows, feat), F32),
            pltpu.VMEM((nxs, 2, nz, rows, feat), BF16),
            pltpu.VMEM((nx, nz, rows, low), BF16),
            pltpu.VMEM((nz, rows, low), F32),
            pltpu.VMEM((2, rows, low), F32),
            pltpu.VMEM((nz - 1, rows, low), F32),
            pltpu.VMEM((chunks, 2, per, 2, rows, high), BF16),
            pltpu.VMEM((chunks, nz - 1, per, 2, rows, high), BF16),
            pltpu.VMEM((nxs, 2, rows, high), F32),
            pltpu.VMEM((nx, rows, high), F32),
            pltpu.SemaphoreType.DMA((N_SEMS,)),
            pltpu.SemaphoreType.DMA((N_SEMS,)),
            pltpu.SemaphoreType.DMA((64,)),
            pltpu.SemaphoreType.DMA((6,)),
        ],
        compiler_params=pltpu.CompilerParams(
            collective_id=0, has_side_effects=True, vmem_limit_bytes=LIMIT
        ),
    )(tokens, weight_in, bias_in, weight_out, out_grad)
    return pl.pallas_call(
        copy_out,
        out_shape=tuple(jax.ShapeDtypeStruct(v.shape, v.dtype) for v in out),
        in_specs=[vmem] * 4,
        out_specs=(anywhere,) * 4,
        scratch_shapes=[pltpu.SemaphoreType.DMA((4,))],
        compiler_params=pltpu.CompilerParams(vmem_limit_bytes=1024 * 1024),
    )(*(pltpu.with_memory_space_constraint(v, pltpu.VMEM) for v in out))


def solution(mesh):
    nz, ny = mesh.shape["row"] // X, mesh.shape["col"] // 2
    in_specs = (P("row", "col"), P("col", "row"), P("row"), P("row", "col"), P("row", "col"))
    out_specs = (P("row", "col"), P("col", "row"), P("row", "col"), P("row"))
    return jax.shard_map(
        functools.partial(body, nz, ny),
        mesh=mesh,
        in_specs=in_specs,
        out_specs=out_specs,
        check_vma=False,
    )
```
